32 devices in a mesh: seq: 8 (over z, core), head: 4 (over y, x).
Axes of the slice: x: 2, y: 2, z: 4, core: 2. Of those that a mesh axis runs over, the one named last changes fastest.
Arguments:
- queries: bfloat16 [24576, 8, 128], P('seq', 'head'), may hold values from -6 to 6
- keys: bfloat16 [24576, 8, 128], P('seq', 'head'), may hold values from -6 to 6
- values: bfloat16 [24576, 8, 128], P('seq', 'head'), may hold values from -60 to 60
- cotangent: bfloat16 [24576, 8, 128], P('seq', 'head'), may hold values from -6 to 6
- doc_lengths: int32 [6], replicated, may hold values from 1 to 18432, 24576 in all
Outputs:
- output: bfloat16 [24576, 8, 128], P('seq', 'head')
- grad_queries: bfloat16 [24576, 8, 128], P('seq', 'head')
- grad_keys: bfloat16 [24576, 8, 128], P('seq', 'head')
- grad_values: bfloat16 [24576, 8, 128], P('seq', 'head')
The draws below stay inside these ranges and needn't reach their ends.
All inputs are finite; a program needn't handle non-finite values.
Results may differ from the reference program's by a relative error of at most 0.0058.
Values sent between devices are 32-bit elements; how exact they have to be, the bound alone decides.
No kernel may reach another device: no remote copies, remote signals or barrier semaphores. Data moves between devices by JAX's collectives and lax.ppermute only.
A program may use at most 128 MiB of HBM per device.

```python
import math
import jax
import jax.numpy as jnp
import numpy as np
from jax import lax

DH = 128
GROUP = 256
NDOCS = 6
TOK_DEV = 3072
TOKENS = 24576
HEADS = 8


def draw_values(key, part):
    noise_key, head_key, row_key = jax.random.split(key, 3)
    head_place = jnp.arange(HEADS, dtype=jnp.float32)
    head_scale = 10.0 ** ((head_place + jax.random.uniform(head_key, (HEADS,), dtype=jnp.float32)) / HEADS - 0.5)
    unit_noise = jnp.clip(jax.random.normal(noise_key, (TOKENS, HEADS, DH), dtype=jnp.float32), -6.0, 6.0)
    row_scale = jnp.exp(jax.random.uniform(row_key, (TOKENS,), dtype=jnp.float32, minval=math.log(0.3), maxval=math.log(3.0)))
    return (unit_noise * row_scale[:, None, None] * head_scale[None, :, None]).astype(jnp.bfloat16)


def block_scale(key, extent, pieces, low, largest):
    def one(position, shards_of):
        heights = jax.random.uniform(jax.random.fold_in(jax.random.fold_in(key, 6), position), (shards_of,), jnp.float32, low / len(pieces), largest / len(pieces))
        return jnp.repeat(jnp.exp(heights), extent[position] // shards_of).reshape((-1,) + (1,) * (len(extent) - position - 1))

    gain = one(*pieces[0])
    for cut in pieces[1:]:
        gain = gain * one(*cut)
    return gain


def length_profile(count, total, bound, skew):
    portions = [(1 << 20) // math.isqrt(rank ** skew) + 1 for rank in range(2, count + 1)]
    surplus, counts = total - bound - (count - 1), [1] * (count - 1)
    while surplus > 0:
        free = [i for i in range(count - 1) if counts[i] < bound]
        whole, remaining = sum([portions[i] for i in free]), surplus
        for i in free:
            extra = min(bound - counts[i], max(1, remaining * portions[i] // whole), surplus)
            counts[i] = counts[i] + extra
            surplus = surplus - extra
    return np.array([bound] + counts)


def ragged_sizes(own_key, number_of, total, bound, slope):
    if number_of == 2:
        one = jax.random.randint(own_key, (), max(1, total - bound), min(bound, total - 1) + 1)
        return jnp.stack([one, total - one])
    lengths = jnp.asarray(length_profile(number_of, total, bound, slope), jnp.int32)
    couples = (number_of - 1) // 2
    donor, sink = lengths[1:1 + 2 * couples:2], lengths[2:2 + 2 * couples:2]
    slack = jnp.minimum(donor - 1, bound - sink)
    shifted = jax.random.randint(jax.random.fold_in(own_key, 1), (couples,), 0, 1 << 20) % (slack + 1)
    lengths = lengths.at[1:1 + 2 * couples:2].set(donor - shifted).at[2:2 + 2 * couples:2].set(sink + shifted)
    return lengths[jax.random.permutation(jax.random.fold_in(own_key, 2), number_of)]


def normal_values(own_key, shape, spread, most, cuts=(), held_as=jnp.bfloat16):
    values = spread * jax.random.normal(own_key, shape, jnp.float32)
    if cuts:
        values = values * block_scale(own_key, shape, cuts, -0.22, 0.18)
    return jnp.clip(values, -most, most).astype(held_as)


def setup_inputs(seed: int = 0) -> dict:
    seeds = jax.random.split(jax.random.key(seed), 6)
    return {
        "queries": normal_values(seeds[0], (TOKENS, HEADS, DH), 1.0, 6.0, ((0, 8), (1, 4))),
        "keys": normal_values(seeds[1], (TOKENS, HEADS, DH), 1.0, 6.0, ((0, 8), (1, 4))),
        "values": draw_values(jax.random.fold_in(seeds[5], 71), 0),
        "cotangent": normal_values(seeds[3], (TOKENS, HEADS, DH), 1.0, 6.0, ((0, 8), (1, 4))),
        "doc_lengths": ragged_sizes(seeds[4], NDOCS, TOKENS, 3 * TOKENS // 4, 1).astype(jnp.int32),
    }


EPSILON = 1e-06

def segment_of(places, doc_ends):
    return lax.optimization_barrier(jnp.sum((doc_ends[None, :] <= places[:, None]).astype(jnp.int32), axis=1))

def rounded(array):
    return lax.optimization_barrier(array.astype(jnp.bfloat16)).astype(jnp.float32)

def reference(queries, keys, values, cotangent, doc_lengths):
    doc_ends = jnp.cumsum(doc_lengths).astype(jnp.int32)
    n_groups = TOKENS // GROUP
    per_shard = TOK_DEV // GROUP
    width_all = float(HEADS * DH)

    def blocks(array):
        return array.reshape(n_groups, GROUP, HEADS, DH)
    query_blocks = blocks(queries)
    key_blocks = blocks(keys)
    value_blocks = blocks(values)
    grad_blocks = blocks(cotangent)
    positions = jnp.arange(TOKENS, dtype=jnp.int32)
    segment = segment_of(positions, doc_ends).reshape(n_groups, GROUP)
    group_ids = jnp.arange(n_groups, dtype=jnp.int32)
    group_first = group_ids * GROUP
    before_group = segment_of(group_first - 1, doc_ends)
    after_group = segment_of(group_first + GROUP, doc_ends)
    shard_first = group_ids // per_shard * TOK_DEV
    before_shard = segment_of(shard_first - 1, doc_ends)
    after_shard = segment_of(shard_first + TOK_DEV, doc_ends)
    opens = group_ids % per_shard == 0
    closes = group_ids % per_shard == per_shard - 1
    causal = jnp.arange(GROUP)[:, None] >= jnp.arange(GROUP)[None, :]
    zero_state = jnp.zeros((HEADS, DH, DH), jnp.float32)

    def group_probs(query_f, key_f, segment_group):
        within = causal & (segment_group[:, None] == segment_group[None, :])
        scores = jnp.einsum('thd,shd->hts', query_f, key_f)
        return (within, rounded(jnp.where(within[None], scores, 0.0)))

    def forward_step(running, inputs):
        state_in, state_local, last_before = running
        query_group, key_group, value_group, grad_group, segment_group, before_c, before_s, opening = inputs
        joined = jnp.where(before_s == last_before, state_in, 0.0) + state_local
        state_in = jnp.where(opening, joined, state_in)
        state_local = jnp.where(opening, 0.0, state_local)
        query_f = query_group.astype(jnp.float32)
        key_f = key_group.astype(jnp.float32)
        value_f = value_group.astype(jnp.float32)
        within, probs = group_probs(query_f, key_f, segment_group)
        local_bf = rounded(state_local)
        remote_bf = rounded(state_in)
        gate_local = (segment_group == before_c).astype(jnp.float32)[:, None, None]
        gate_remote = (segment_group == before_s).astype(jnp.float32)[:, None, None]
        mixed = jnp.einsum('hts,shd->thd', probs, value_f)
        mixed = mixed + gate_local * jnp.einsum('thi,hij->thj', query_f, local_bf)
        mixed = mixed + gate_remote * jnp.einsum('thi,hij->thj', query_f, remote_bf)
        squares = lax.optimization_barrier(jnp.sum(mixed * mixed, axis=(1, 2)))
        root = jnp.sqrt(squares / width_all + EPSILON)
        normed = mixed / root[:, None, None]
        grad_f = grad_group.astype(jnp.float32)
        centre = lax.optimization_barrier(jnp.sum(grad_f * normed, axis=(1, 2))) / width_all
        grad_mixed = ((grad_f - normed * centre[:, None, None]) / root[:, None, None]).astype(jnp.bfloat16)
        grad_mf = lax.optimization_barrier(grad_mixed).astype(jnp.float32)
        grad_probs = rounded(jnp.where(within[None], jnp.einsum('thd,shd->hts', grad_mf, value_f), 0.0))
        grad_query = jnp.einsum('hts,shd->thd', grad_probs, key_f)
        grad_query = grad_query + gate_local * jnp.einsum('thj,hij->thi', grad_mf, local_bf)
        grad_query = grad_query + gate_remote * jnp.einsum('thj,hij->thi', grad_mf, remote_bf)
        ending = segment_group[-1]
        tail = (segment_group == ending).astype(jnp.float32)[:, None, None]
        added = jnp.einsum('thi,thj->hij', key_f * tail, value_f)
        state_local = jnp.where(ending == before_c, state_local, 0.0) + added
        return ((state_in, state_local, before_s), (normed.astype(jnp.bfloat16), grad_query.astype(jnp.bfloat16), grad_mixed))
    start_before = segment_of(jnp.array([-1], dtype=jnp.int32), doc_ends)[0]
    inputs = (query_blocks, key_blocks, value_blocks, grad_blocks, segment, before_group, before_shard, opens)
    _, (output, grad_queries, grad_mixed_all) = lax.scan(forward_step, (zero_state, zero_state, start_before), inputs)

    def backward_step(running, inputs):
        state_in, state_local, last_after = running
        query_group, key_group, value_group, grad_group, segment_group, after_c, after_s, closing = inputs
        joined = jnp.where(after_s == last_after, state_in, 0.0) + state_local
        state_in = jnp.where(closing, joined, state_in)
        state_local = jnp.where(closing, 0.0, state_local)
        query_f = query_group.astype(jnp.float32)
        key_f = key_group.astype(jnp.float32)
        value_f = value_group.astype(jnp.float32)
        grad_mf = grad_group.astype(jnp.float32)
        within, probs = group_probs(query_f, key_f, segment_group)
        grad_probs = rounded(jnp.where(within[None], jnp.einsum('thd,shd->hts', grad_mf, value_f), 0.0))
        local_bf = rounded(state_local)
        remote_bf = rounded(state_in)
        gate_local = (segment_group == after_c).astype(jnp.float32)[:, None, None]
        gate_remote = (segment_group == after_s).astype(jnp.float32)[:, None, None]
        grad_key = jnp.einsum('hts,thd->shd', grad_probs, query_f)
        grad_key = grad_key + gate_local * jnp.einsum('shj,hij->shi', value_f, local_bf)
        grad_key = grad_key + gate_remote * jnp.einsum('shj,hij->shi', value_f, remote_bf)
        grad_value = jnp.einsum('hts,thd->shd', probs, grad_mf)
        grad_value = grad_value + gate_local * jnp.einsum('shi,hij->shj', key_f, local_bf)
        grad_value = grad_value + gate_remote * jnp.einsum('shi,hij->shj', key_f, remote_bf)
        leading = segment_group[0]
        head_part = (segment_group == leading).astype(jnp.float32)[:, None, None]
        added = jnp.einsum('thi,thj->hij', query_f * head_part, grad_mf)
        state_local = jnp.where(leading == after_c, state_local, 0.0) + added
        return ((state_in, state_local, after_s), (grad_key.astype(jnp.bfloat16), grad_value.astype(jnp.bfloat16)))
    start_after = segment_of(jnp.array([TOKENS], dtype=jnp.int32), doc_ends)[0]
    inputs = (query_blocks, key_blocks, value_blocks, grad_mixed_all, segment, after_group, after_shard, closes)
    _, (grad_keys, grad_values) = lax.scan(backward_step, (zero_state, zero_state, start_after), inputs, reverse=True)
    shape = (TOKENS, HEADS, DH)
    return (output.reshape(shape), grad_queries.reshape(shape), grad_keys.reshape(shape), grad_values.reshape(shape))
```

```python
import functools

import jax
import jax.numpy as jnp
from jax import lax
from jax.experimental import pallas as pl
from jax.experimental.pallas import tpu as pltpu
from jax.sharding import PartitionSpec as P

GROUP = 256
EPSILON = 1e-06
F32 = jnp.float32
BF16 = jnp.bfloat16

NN = (((1,), (0,)), ((), ()))
NT = (((1,), (1,)), ((), ()))
TN = (((0,), (0,)), ((), ()))


def dot(a, b, dims=NN):
    return lax.dot_general(a, b, dims, preferred_element_type=F32)


def doc_ends_of(doc_ref):
    ends, total = [], jnp.int32(0)
    for j in range(doc_ref.shape[0]):
        total = total + doc_ref[j]
        ends.append(total)
    return ends


def start_of(ends, place):
    found = jnp.int32(0)
    for end in ends:
        found = jnp.where(end <= place, end, found)
    return found


def end_of(ends, place):
    found = jnp.int32(2**30)
    for end in reversed(ends):
        found = jnp.where(end > place, end, found)
    return found


def rows_iota(width):
    return lax.broadcasted_iota(jnp.int32, (GROUP, width), 0)


def group_mask(ends, first):
    place = rows_iota(128) + first
    begin = jnp.zeros((GROUP, 128), jnp.int32)
    for end in ends:
        begin = jnp.where(place >= end, end, begin)
    begin = begin - first
    begin = jnp.concatenate([begin] * (GROUP // 128), axis=1)
    column = lax.broadcasted_iota(jnp.int32, (GROUP, GROUP), 1)
    return (column >= begin) & (column <= rows_iota(GROUP))


def keep_rows(keep, x):
    return jnp.where(keep, x.astype(F32), 0.0).astype(BF16)


def split_heads(src_ref, tmp_ref, g, heads):
    rows = pl.ds(pl.multiple_of(g * (GROUP * heads), GROUP * heads), GROUP * heads)
    tmp_ref[rows, :] = src_ref[rows, :].astype(F32)
    return [
        tmp_ref[pl.ds(g * (GROUP * heads) + h, GROUP, stride=heads), :] for h in range(heads)
    ]


def group_rows(g):
    return pl.ds(pl.multiple_of(g * GROUP, GROUP), GROUP)


def state_kernel(doc_ref, k2_ref, v2_ref, kd_ref, vd_ref, mine_ref, send_ref, tmpk, tmpv, acc):
    tokens, width = kd_ref.shape
    heads = width // 128
    half = heads // 2
    shard = lax.axis_index("seq")
    core = shard % 2
    anchor = shard * tokens
    ends = doc_ends_of(doc_ref)
    tail = start_of(ends, anchor + tokens - 1) - anchor
    acc[...] = jnp.zeros_like(acc)
    for g in range(tokens // GROUP):
        keep = rows_iota(128) + g * GROUP >= tail
        ks = split_heads(k2_ref, tmpk, g, heads)
        vs = split_heads(v2_ref, tmpv, g, heads)
        for h in range(heads):
            lanes = slice(h * 128, (h + 1) * 128)
            v = vs[h].astype(BF16)
            kd_ref[group_rows(g), lanes] = ks[h].astype(BF16)
            vd_ref[group_rows(g), lanes] = v
            acc[h] += dot(jnp.where(keep, ks[h], 0.0).astype(BF16), v, TN)
    mine_ref[...] = acc[pl.ds(core * half, half)]
    send_ref[...] = acc[pl.ds((1 - core) * half, half)]


def local_kernel(
    doc_ref, kd_ref, vd_ref, q2_ref, c2_ref, qd_ref, qt_ref, cd_ref, p_ref, o_ref, sb_ref, tmpq, tmpc, state
):
    tokens, width = kd_ref.shape
    heads = width // 128
    anchor = lax.axis_index("seq") * tokens
    ends = doc_ends_of(doc_ref)
    state[...] = jnp.zeros_like(state)

    def body(g, carry):
        first = anchor + g * GROUP
        rows = group_rows(g)
        mask = group_mask(ends, first)
        place = rows_iota(128)
        opened = place < end_of(ends, first - 1) - first
        begin = start_of(ends, first + GROUP - 1)
        tail = place >= begin - first
        kept = (begin < first).astype(F32)
        qs = split_heads(q2_ref, tmpq, g, heads)
        cs = split_heads(c2_ref, tmpc, g, heads)
        for h in range(heads):
            lanes = slice(h * 128, (h + 1) * 128)
            q = qs[h].astype(BF16)
            k = kd_ref[rows, lanes]
            v = vd_ref[rows, lanes]
            qd_ref[rows, lanes] = q
            qt_ref[lanes, rows] = qs[h].T.astype(BF16)
            cd_ref[rows, lanes] = cs[h].astype(BF16)
            p = jnp.where(mask, dot(q, k, NT), 0.0).astype(BF16)
            p_ref[h, rows, :] = p
            sb = state[h].astype(BF16)
            sb_ref[g, h] = sb
            o_ref[rows, lanes] = dot(p, v) + dot(jnp.where(opened, qs[h], 0.0).astype(BF16), sb)
            state[h] = state[h] * kept + dot(keep_rows(tail, k), v, TN)
        return carry

    lax.fori_loop(0, tokens // GROUP, body, 0)


def place_halves(core, out_ref, own_ref, other_ref):
    half = own_ref.shape[0]
    out_ref[pl.ds(core * half, half)] = own_ref[...].astype(BF16)
    out_ref[pl.ds((1 - core) * half, half)] = other_ref[...].astype(BF16)


def stats_kernel(doc_ref, qd_ref, ol_ref, cd_ref, own_ref, other_ref, o_ref, sin_ref, st_ref):
    tokens, width = qd_ref.shape
    heads = width // 128
    shard = lax.axis_index("seq")
    anchor = shard * tokens
    ends = doc_ends_of(doc_ref)
    opened_to = end_of(ends, anchor - 1) - anchor
    place_halves(shard % 2, sin_ref, own_ref, other_ref)
    row = lax.broadcasted_iota(jnp.int32, (8, 128), 0)
    pick0 = (row == 0).astype(F32).astype(BF16)
    pick1 = (row == 1).astype(F32).astype(BF16)
    for g in range(tokens // GROUP):
        rows = group_rows(g)
        opened = rows_iota(128) + g * GROUP < opened_to
        squares = jnp.zeros((GROUP, 128), F32)
        inner = jnp.zeros((GROUP, 128), F32)
        for h in range(heads):
            lanes = slice(h * 128, (h + 1) * 128)
            o = ol_ref[rows, lanes] + dot(keep_rows(opened, qd_ref[rows, lanes]), sin_ref[h])
            o_ref[rows, lanes] = o
            squares += o * o
            inner += o * cd_ref[rows, lanes].astype(F32)
        both = dot(pick0, squares.astype(BF16), NT) + dot(pick1, inner.astype(BF16), NT)
        for r in range(st_ref.shape[0]):
            st_ref[r, :, rows] = both[:2]


def norm_kernel(
    width_all, doc_ref, st_ref, o_ref, cd_ref, qt_ref, dob_ref, inv_ref, mine_ref, send_ref, acc
):
    tokens, width = cd_ref.shape
    heads = width // 128
    half = heads // 2
    shard = lax.axis_index("seq")
    core = shard % 2
    anchor = shard * tokens
    ends = doc_ends_of(doc_ref)
    head_to = end_of(ends, anchor) - anchor
    acc[...] = jnp.zeros_like(acc)
    for g in range(tokens // GROUP):
        rows = group_rows(g)
        keep = rows_iota(128) + g * GROUP < head_to
        total = st_ref[0, :, rows]
        for r in range(1, st_ref.shape[0]):
            total = total + st_ref[r, :, rows]
        total = total * (1.0 / width_all)
        inv = lax.rsqrt(total[0:1] + EPSILON)
        slope = total[1:2] * inv * inv * inv
        columns = jnp.concatenate([inv, slope, jnp.zeros((6, GROUP), F32)], axis=0).T
        inv_col = jnp.broadcast_to(columns[:, 0:1], (GROUP, 128))
        slope_col = jnp.broadcast_to(columns[:, 1:2], (GROUP, 128))
        inv_ref[rows, :] = inv_col
        for h in range(heads):
            lanes = slice(h * 128, (h + 1) * 128)
            dob = inv_col * cd_ref[rows, lanes].astype(F32) - slope_col * o_ref[rows, lanes]
            dob_ref[rows, lanes] = dob.astype(BF16)
            acc[h] += dot(qt_ref[lanes, rows], jnp.where(keep, dob, 0.0).astype(BF16))
    mine_ref[...] = acc[pl.ds(core * half, half)]
    send_ref[...] = acc[pl.ds((1 - core) * half, half)]


def grad_kernel(
    doc_ref, o_ref, inv_ref, dob_ref, p_ref, qd_ref, qt_ref, kd_ref, vd_ref, sb_ref, sin_ref,
    dk_ref, dv_ref, out_ref, gq_ref, tmpo, tmpq, bufo, bufq, state, sems,
):
    tokens, width = kd_ref.shape
    heads = width // 128
    n_groups = tokens // GROUP
    anchor = lax.axis_index("seq") * tokens
    ends = doc_ends_of(doc_ref)
    opened_to = end_of(ends, anchor - 1)
    state[...] = jnp.zeros_like(state)

    def copies(g):
        pairs = pl.ds(pl.multiple_of(g * GROUP * heads, GROUP * heads), GROUP * heads)
        return (
            pltpu.make_async_copy(bufo.at[pairs], out_ref.at[pairs], sems.at[0, g]),
            pltpu.make_async_copy(bufq.at[pairs], gq_ref.at[pairs], sems.at[1, g]),
        )

    def body(i, carry):
        g = n_groups - 1 - i
        first = anchor + g * GROUP
        rows = group_rows(g)
        pairs = pl.ds(pl.multiple_of(g * GROUP * heads, GROUP * heads), GROUP * heads)
        mask = group_mask(ends, first)
        place = rows_iota(128)
        opened = place < end_of(ends, first - 1) - first
        opened_far = place < opened_to - first
        closing = place >= start_of(ends, first + GROUP) - first
        end = end_of(ends, first)
        head_part = place < end - first
        kept = (end > first + GROUP).astype(F32)
        for h in range(heads):
            lanes = slice(h * 128, (h + 1) * 128)
            q = qd_ref[rows, lanes]
            k = kd_ref[rows, lanes]
            v = vd_ref[rows, lanes]
            dob = dob_ref[rows, lanes]
            dp = jnp.where(mask, dot(dob, v, NT), 0.0).astype(BF16)
            gq = (
                dot(dp, k)
                + dot(keep_rows(opened, dob), sb_ref[g, h], NT)
                + dot(keep_rows(opened_far, dob), sin_ref[h], NT)
            )
            mine = pl.ds(g * (GROUP * heads) + h, GROUP, stride=heads)
            tmpq[mine, :] = gq
            tmpo[mine, :] = o_ref[rows, lanes] * inv_ref[rows, :]
            rb = state[h].astype(BF16)
            dk_ref[rows, lanes] = dot(dp, q, TN) + dot(keep_rows(closing, v), rb, NT)
            dv_ref[rows, lanes] = dot(p_ref[h, rows, :], dob, TN) + dot(keep_rows(closing, k), rb)
            state[h] = state[h] * kept + dot(qt_ref[lanes, rows], keep_rows(head_part, dob))
        bufq[pairs, :] = tmpq[pairs, :].astype(BF16)
        bufo[pairs, :] = tmpo[pairs, :].astype(BF16)
        for copy in copies(g):
            copy.start()
        return carry

    lax.fori_loop(0, n_groups, body, 0)

    def drain(g, carry):
        for copy in copies(g):
            copy.wait()
        return carry

    lax.fori_loop(0, n_groups, drain, 0)


def final_kernel(
    doc_ref, dk_ref, dv_ref, kd_ref, vd_ref, own_ref, other_ref, gk_ref, gv_ref, rin, tmpk, tmpv, bufk, bufv, sems
):
    tokens, width = kd_ref.shape
    heads = width // 128
    n_groups = tokens // GROUP
    shard = lax.axis_index("seq")
    anchor = shard * tokens
    ends = doc_ends_of(doc_ref)
    begin = start_of(ends, anchor + tokens) - anchor
    place_halves(shard % 2, rin, own_ref, other_ref)
    started = []
    for g in range(n_groups):
        rows = group_rows(g)
        pairs = pl.ds(g * GROUP * heads, GROUP * heads)
        closing = rows_iota(128) + g * GROUP >= begin
        for h in range(heads):
            lanes = slice(h * 128, (h + 1) * 128)
            mine = pl.ds(g * (GROUP * heads) + h, GROUP, stride=heads)
            tmpk[mine, :] = dk_ref[rows, lanes] + dot(keep_rows(closing, vd_ref[rows, lanes]), rin[h], NT)
            tmpv[mine, :] = dv_ref[rows, lanes] + dot(keep_rows(closing, kd_ref[rows, lanes]), rin[h])
        bufk[pairs, :] = tmpk[pairs, :].astype(BF16)
        bufv[pairs, :] = tmpv[pairs, :].astype(BF16)
        for n, (buf, out) in enumerate(((bufk, gk_ref), (bufv, gv_ref))):
            copy = pltpu.make_async_copy(buf.at[pairs], out.at[pairs], sems.at[n, g])
            copy.start()
            started.append(copy)
    for copy in started:
        copy.wait()


def call(kernel, name, outs, scratch, out_any=(), flops=0, n_in=0):
    vmem = pl.BlockSpec(memory_space=pltpu.VMEM)
    specs = [pl.BlockSpec(memory_space=pl.ANY) if i in out_any else vmem for i in range(len(outs))]
    return pl.pallas_call(
        kernel,
        name=name,
        out_shape=[jax.ShapeDtypeStruct(s, d) for s, d in outs],
        in_specs=[pl.BlockSpec(memory_space=pltpu.SMEM)] + [vmem] * n_in,
        out_specs=specs,
        scratch_shapes=scratch,
        cost_estimate=pl.CostEstimate(flops=flops, bytes_accessed=8 << 20, transcendentals=0),
        compiler_params=pltpu.CompilerParams(vmem_limit_bytes=30 << 20),
    )


def segment(ends, place):
    return jnp.sum((ends <= place).astype(jnp.int32))


def per_device(queries, keys, values, cotangent, doc_lengths):
    tokens, heads, head_width = queries.shape
    width = heads * head_width
    half = heads // 2
    n_groups = tokens // GROUP
    n_seq = lax.axis_size("seq")
    n_head = lax.axis_size("head")
    shard = lax.axis_index("seq")
    core = shard % 2
    chip = shard // 2
    n_chips = n_seq // 2
    ends = jnp.cumsum(doc_lengths)
    seg = functools.partial(segment, ends)
    chip_first = chip * (2 * tokens)
    middle = chip_first + tokens
    chip_end = middle + tokens

    def pairs(x):
        return x.reshape(tokens * heads, head_width)

    q2, k2, v2, c2 = pairs(queries), pairs(keys), pairs(values), pairs(cotangent)
    full = (tokens, width)
    piece = (half, head_width, head_width)
    state_shape = (heads, head_width, head_width)
    flat = (tokens * heads, head_width)
    swap_pairs = [(i, i ^ 1) for i in range(n_seq)]

    def swap(x):
        return lax.ppermute(x, "seq", swap_pairs)

    def exchange(mine, got, sign, after):
        near = jnp.where(core == (0 if sign > 0 else 1), mine, got)
        far = jnp.where(core == (0 if sign > 0 else 1), got, mine)
        if sign > 0:
            joined = seg(middle - 1) == seg(chip_end - 1)
            onward = seg(chip_first - 1) == seg(middle - 1)
        else:
            joined = seg(middle) == seg(chip_first)
            onward = seg(chip_end) == seg(middle)
        chip_state = far + joined.astype(F32) * near
        chip_state, after = lax.optimization_barrier((chip_state, after))
        total = jnp.zeros(piece, F32)
        for k in range(1, n_chips):
            links = [(i, i + 2 * k * sign) for i in range(n_seq) if 0 <= i + 2 * k * sign < n_seq]
            arrived = lax.ppermute(chip_state, "seq", links)
            if sign > 0:
                same = seg(chip_first - 2 * tokens * (k - 1) - 1) == seg(chip_first - 1)
            else:
                same = seg(chip_end + 2 * tokens * (k - 1)) == seg(chip_end)
            total = total + same.astype(F32) * arrived
        return near, onward.astype(F32), total, after

    def finish(near, onward, total, sign):
        farther = near + onward * total
        is_near = core == (0 if sign > 0 else 1)
        own = jnp.where(is_near, total, farther)
        send = jnp.where(is_near, farther, total)
        return own, swap(send)

    mm = 2 * tokens * heads * head_width * head_width
    kd, vd, mine, send = call(
        state_kernel,
        "shard_state",
        [(full, BF16), (full, BF16), (piece, F32), (piece, F32)],
        [pltpu.VMEM(flat, F32), pltpu.VMEM(flat, F32), pltpu.VMEM(state_shape, F32)],
        n_in=2,
        flops=mm,
    )(doc_lengths, k2, v2)
    near, onward, total, (kd_b, vd_b) = exchange(mine, swap(send), 1, (kd, vd))
    qd, qt, cd, probs, o_local, sb = call(
        local_kernel,
        "local_mix",
        [
            (full, BF16),
            ((width, tokens), BF16),
            (full, BF16),
            ((heads, tokens, GROUP), BF16),
            (full, F32),
            ((n_groups, heads, head_width, head_width), BF16),
        ],
        [pltpu.VMEM(flat, F32), pltpu.VMEM(flat, F32), pltpu.VMEM(state_shape, F32)],
        n_in=4,
        flops=6 * mm,
    )(doc_lengths, kd_b, vd_b, q2, c2)
    own, other = finish(near, onward, total, 1)
    o, sin, stats = call(
        stats_kernel,
        "mix_and_stats",
        [(full, F32), (state_shape, BF16), ((n_head, 2, tokens), F32)],
        [],
        n_in=5,
        flops=mm,
    )(doc_lengths, qd, o_local, cd, own, other)
    stats = lax.all_to_all(stats, "head", 0, 0)
    dob, inv, mine, send = call(
        functools.partial(norm_kernel, float(width * n_head)),
        "norm_back",
        [(full, BF16), ((tokens, head_width), F32), (piece, F32), (piece, F32)],
        [pltpu.VMEM(state_shape, F32)],
        n_in=4,
        flops=mm,
    )(doc_lengths, stats, o, cd, qt)
    near, onward, total, (dob_b, inv_b) = exchange(mine, swap(send), -1, (dob, inv))
    dk, dv, output, grad_q = call(
        grad_kernel,
        "local_grads",
        [(full, F32), (full, F32), (flat, BF16), (flat, BF16)],
        [
            pltpu.VMEM(flat, F32),
            pltpu.VMEM(flat, F32),
            pltpu.VMEM(flat, BF16),
            pltpu.VMEM(flat, BF16),
            pltpu.VMEM(state_shape, F32),
            pltpu.SemaphoreType.DMA((2, n_groups)),
        ],
        n_in=10,
        out_any=(2, 3),
        flops=12 * mm,
    )(doc_lengths, o, inv_b, dob_b, probs, qd, qt, kd, vd, sb, sin)
    own, other = finish(near, onward, total, -1)
    grad_k, grad_v = call(
        final_kernel,
        "final_grads",
        [(flat, BF16), (flat, BF16)],
        [
            pltpu.VMEM(state_shape, BF16),
            pltpu.VMEM(flat, F32),
            pltpu.VMEM(flat, F32),
            pltpu.VMEM(flat, BF16),
            pltpu.VMEM(flat, BF16),
            pltpu.SemaphoreType.DMA((2, n_groups)),
        ],
        n_in=6,
        out_any=(0, 1),
        flops=2 * mm,
    )(doc_lengths, dk, dv, kd, vd, own, other)
    return tuple(x.reshape(queries.shape) for x in (output, grad_q, grad_k, grad_v))


def solution(mesh):
    spec = P("seq", "head", None)
    return jax.shard_map(
        per_device,
        mesh=mesh,
        in_specs=(spec, spec, spec, spec, P()),
        out_specs=(spec, spec, spec, spec),
        check_vma=False,
    )
```

```python
import functools

import jax
import jax.numpy as jnp
from jax import lax
from jax.experimental import pallas as pl
from jax.experimental.pallas import tpu as pltpu
from jax.sharding import PartitionSpec as P

GROUP = 256
EPSILON = 1e-06
UNROLL_MIX = 3
UNROLL_GRAD = 3
F32 = jnp.float32
BF16 = jnp.bfloat16

NN = (((1,), (0,)), ((), ()))
NT = (((1,), (1,)), ((), ()))
TN = (((0,), (0,)), ((), ()))


def dot(a, b, dims=NN):
    return lax.dot_general(a, b, dims, preferred_element_type=F32)


def doc_ends_of(doc_ref):
    ends, total = [], jnp.int32(0)
    for j in range(doc_ref.shape[0]):
        total = total + doc_ref[j]
        ends.append(total)
    return ends


def start_of(ends, place):
    found = jnp.int32(0)
    for end in ends:
        found = jnp.where(end <= place, end, found)
    return found


def end_of(ends, place):
    found = jnp.int32(2**30)
    for end in reversed(ends):
        found = jnp.where(end > place, end, found)
    return found


def rows_iota(width):
    return lax.broadcasted_iota(jnp.int32, (GROUP, width), 0)


def group_mask(ends, first):
    place = rows_iota(128) + first
    begin = jnp.zeros((GROUP, 128), jnp.int32)
    for end in ends:
        begin = jnp.where(place >= end, end, begin)
    begin = begin - first
    begin = jnp.concatenate([begin] * (GROUP // 128), axis=1)
    column = lax.broadcasted_iota(jnp.int32, (GROUP, GROUP), 1)
    return (column >= begin) & (column <= rows_iota(GROUP))


def keep_rows(keep, x):
    return jnp.where(keep, x.astype(F32), 0.0).astype(BF16)


def pair_rows(g, heads):
    return pl.ds(pl.multiple_of(g * (GROUP * heads), GROUP * heads), GROUP * heads)


def fetch(src_ref, buf_ref, sem_ref, g, heads):
    rows = pair_rows(g, heads)
    return pltpu.make_async_copy(src_ref.at[rows], buf_ref.at[rows], sem_ref.at[g])


def split_heads(buf_ref, tmp_ref, g, heads):
    slot = g % tmp_ref.shape[0]
    tmp_ref[slot] = buf_ref[pair_rows(g, heads), :].astype(F32)
    return [tmp_ref[slot, pl.ds(h, GROUP, stride=heads), :] for h in range(heads)]


def for_groups(n_groups, body, unroll):
    if unroll >= n_groups:
        for g in range(n_groups):
            body(g)
    else:

        def step(i, carry):
            for j in range(unroll):
                body(i * unroll + j)
            return carry

        lax.fori_loop(0, n_groups // unroll, step, 0)


def group_rows(g):
    return pl.ds(pl.multiple_of(g * GROUP, GROUP), GROUP)


def weights_of(out_ref, ends, shard, tokens, n_seq, sign):
    core = shard % 2
    chip_first = (shard - core) * tokens
    middle = chip_first + tokens
    chip_end = middle + tokens
    if sign > 0:
        join = start_of(ends, chip_end - 1) < middle
        onward = start_of(ends, middle - 1) < chip_first
        same = [
            start_of(ends, chip_first - 1) < chip_first - 2 * tokens * k for k in range(n_seq // 2 - 1)
        ]
        is_near = core == 0
    else:
        join = end_of(ends, chip_first) > middle
        onward = end_of(ends, middle) > chip_end
        same = [end_of(ends, chip_end) > chip_end + 2 * tokens * k for k in range(n_seq // 2 - 1)]
        is_near = core == 1
    join, onward, is_near = (x.astype(F32) for x in (join, onward, is_near))
    far = 1.0 - is_near
    table = [
        is_near * join + far,
        is_near + far * join,
        is_near + far * onward,
        far,
        is_near * onward + far,
        is_near,
    ] + [x.astype(F32) for x in same]
    for i, x in enumerate(table):
        out_ref[pl.ds(i, 1), :] = jnp.full((1, 128), x, F32)


def state_kernel(
    n_seq, doc_ref, k2_ref, v2_ref, kd_ref, vd_ref, mine_ref, send_ref, fore_ref, back_ref, tmpk, tmpv, acc
):
    tokens, width = kd_ref.shape
    heads = width // 128
    half = heads // 2
    shard = lax.axis_index("seq")
    core = shard % 2
    anchor = shard * tokens
    ends = doc_ends_of(doc_ref)
    tail = start_of(ends, anchor + tokens - 1) - anchor
    acc[...] = jnp.zeros_like(acc)
    for g in range(tokens // GROUP):
        keep = rows_iota(128) + g * GROUP >= tail
        ks = split_heads(k2_ref, tmpk, g, heads)
        vs = split_heads(v2_ref, tmpv, g, heads)
        for h in range(heads):
            lanes = slice(h * 128, (h + 1) * 128)
            v = vs[h].astype(BF16)
            kd_ref[group_rows(g), lanes] = ks[h].astype(BF16)
            vd_ref[group_rows(g), lanes] = v
            acc[h] += dot(jnp.where(keep, ks[h], 0.0).astype(BF16), v, TN)
    mine_ref[...] = acc[pl.ds(core * half, half)]
    send_ref[...] = acc[pl.ds((1 - core) * half, half)]
    weights_of(fore_ref, ends, shard, tokens, n_seq, 1)
    weights_of(back_ref, ends, shard, tokens, n_seq, -1)


def local_kernel(
    doc_ref, kd_ref, vd_ref, q2_ref, c2_ref, qd_ref, qt_ref, cd_ref, p_ref, o_ref, sb_ref,
    tmpq, tmpc, state,
):
    tokens, width = kd_ref.shape
    heads = width // 128
    anchor = lax.axis_index("seq") * tokens
    ends = doc_ends_of(doc_ref)
    state[...] = jnp.zeros_like(state)

    def body(g):
        first = anchor + g * GROUP
        rows = group_rows(g)
        mask = group_mask(ends, first)
        place = rows_iota(128)
        opened = place < end_of(ends, first - 1) - first
        begin = start_of(ends, first + GROUP - 1)
        tail = place >= begin - first
        kept = (begin < first).astype(F32)
        qs = split_heads(q2_ref, tmpq, g, heads)
        cs = split_heads(c2_ref, tmpc, g, heads)
        for h in range(heads):
            lanes = slice(h * 128, (h + 1) * 128)
            q = qs[h].astype(BF16)
            k = kd_ref[rows, lanes]
            v = vd_ref[rows, lanes]
            qd_ref[rows, lanes] = q
            qt_ref[lanes, rows] = qs[h].T.astype(BF16)
            cd_ref[rows, lanes] = cs[h].astype(BF16)
            p = jnp.where(mask, dot(q, k, NT), 0.0).astype(BF16)
            p_ref[h, rows, :] = p
            sb = state[h].astype(BF16)
            sb_ref[g, h] = sb
            o_ref[rows, lanes] = dot(p, v) + dot(jnp.where(opened, qs[h], 0.0).astype(BF16), sb)
            state[h] = state[h] * kept + dot(keep_rows(tail, k), v, TN)

    for_groups(tokens // GROUP, body, UNROLL_MIX)


def place_halves(core, out_ref, own_ref, other_ref):
    half = own_ref.shape[0]
    out_ref[pl.ds(core * half, half)] = own_ref[...].astype(BF16)
    out_ref[pl.ds((1 - core) * half, half)] = other_ref[...].astype(BF16)


def stats_kernel(doc_ref, qd_ref, ol_ref, cd_ref, own_ref, other_ref, o_ref, sin_ref, st_ref):
    tokens, width = qd_ref.shape
    heads = width // 128
    shard = lax.axis_index("seq")
    anchor = shard * tokens
    ends = doc_ends_of(doc_ref)
    opened_to = end_of(ends, anchor - 1) - anchor
    place_halves(shard % 2, sin_ref, own_ref, other_ref)
    row = lax.broadcasted_iota(jnp.int32, (8, 128), 0)
    pick0 = (row == 0).astype(F32).astype(BF16)
    pick1 = (row == 1).astype(F32).astype(BF16)
    for g in range(tokens // GROUP):
        rows = group_rows(g)
        opened = rows_iota(128) + g * GROUP < opened_to
        squares = jnp.zeros((GROUP, 128), F32)
        inner = jnp.zeros((GROUP, 128), F32)
        for h in range(heads):
            lanes = slice(h * 128, (h + 1) * 128)
            o = ol_ref[rows, lanes] + dot(keep_rows(opened, qd_ref[rows, lanes]), sin_ref[h])
            o_ref[rows, lanes] = o
            squares += o * o
            inner += o * cd_ref[rows, lanes].astype(F32)
        both = dot(pick0, squares.astype(BF16), NT) + dot(pick1, inner.astype(BF16), NT)
        for r in range(st_ref.shape[0]):
            st_ref[r, :, rows] = both[:2]


def norm_kernel(
    width_all, doc_ref, st_ref, o_ref, cd_ref, qt_ref, dob_ref, inv_ref, mine_ref, send_ref, acc
):
    tokens, width = cd_ref.shape
    heads = width // 128
    half = heads // 2
    shard = lax.axis_index("seq")
    core = shard % 2
    anchor = shard * tokens
    ends = doc_ends_of(doc_ref)
    head_to = end_of(ends, anchor) - anchor
    acc[...] = jnp.zeros_like(acc)
    for g in range(tokens // GROUP):
        rows = group_rows(g)
        keep = rows_iota(128) + g * GROUP < head_to
        total = st_ref[0, :, rows]
        for r in range(1, st_ref.shape[0]):
            total = total + st_ref[r, :, rows]
        total = total * (1.0 / width_all)
        inv = lax.rsqrt(total[0:1] + EPSILON)
        slope = total[1:2] * inv * inv * inv
        columns = jnp.concatenate([inv, slope, jnp.zeros((6, GROUP), F32)], axis=0).T
        inv_col = jnp.broadcast_to(columns[:, 0:1], (GROUP, 128))
        slope_col = jnp.broadcast_to(columns[:, 1:2], (GROUP, 128))
        inv_ref[rows, :] = inv_col
        for h in range(heads):
            lanes = slice(h * 128, (h + 1) * 128)
            dob = inv_col * cd_ref[rows, lanes].astype(F32) - slope_col * o_ref[rows, lanes]
            dob_ref[rows, lanes] = dob.astype(BF16)
            acc[h] += dot(qt_ref[lanes, rows], jnp.where(keep, dob, 0.0).astype(BF16))
    mine_ref[...] = acc[pl.ds(core * half, half)]
    send_ref[...] = acc[pl.ds((1 - core) * half, half)]


def grad_kernel(
    doc_ref, o_ref, inv_ref, dob_ref, p_ref, qd_ref, qt_ref, kd_ref, vd_ref, sb_ref, sin_ref,
    dk_ref, dv_ref, out_ref, gq_ref, tmpo, tmpq, bufo, bufq, state, sems,
):
    tokens, width = kd_ref.shape
    heads = width // 128
    n_groups = tokens // GROUP
    anchor = lax.axis_index("seq") * tokens
    ends = doc_ends_of(doc_ref)
    opened_to = end_of(ends, anchor - 1)
    state[...] = jnp.zeros_like(state)

    def copies(g):
        pairs = pl.ds(pl.multiple_of(g * GROUP * heads, GROUP * heads), GROUP * heads)
        return (
            pltpu.make_async_copy(bufo.at[pairs], out_ref.at[pairs], sems.at[0, g]),
            pltpu.make_async_copy(bufq.at[pairs], gq_ref.at[pairs], sems.at[1, g]),
        )

    def body(i):
        g = n_groups - 1 - i
        slot = g % tmpq.shape[0]
        first = anchor + g * GROUP
        rows = group_rows(g)
        pairs = pl.ds(pl.multiple_of(g * GROUP * heads, GROUP * heads), GROUP * heads)
        mask = group_mask(ends, first)
        place = rows_iota(128)
        opened = place < end_of(ends, first - 1) - first
        opened_far = place < opened_to - first
        closing = place >= start_of(ends, first + GROUP) - first
        end = end_of(ends, first)
        head_part = place < end - first
        kept = (end > first + GROUP).astype(F32)
        for h in range(heads):
            lanes = slice(h * 128, (h + 1) * 128)
            q = qd_ref[rows, lanes]
            k = kd_ref[rows, lanes]
            v = vd_ref[rows, lanes]
            dob = dob_ref[rows, lanes]
            dp = jnp.where(mask, dot(dob, v, NT), 0.0).astype(BF16)
            gq = (
                dot(dp, k)
                + dot(keep_rows(opened, dob), sb_ref[g, h], NT)
                + dot(keep_rows(opened_far, dob), sin_ref[h], NT)
            )
            mine = pl.ds(h, GROUP, stride=heads)
            tmpq[slot, mine, :] = gq
            tmpo[slot, mine, :] = o_ref[rows, lanes] * inv_ref[rows, :]
            rb = state[h].astype(BF16)
            dk_ref[rows, lanes] = dot(dp, q, TN) + dot(keep_rows(closing, v), rb, NT)
            dv_ref[rows, lanes] = dot(p_ref[h, rows, :], dob, TN) + dot(keep_rows(closing, k), rb)
            state[h] = state[h] * kept + dot(qt_ref[lanes, rows], keep_rows(head_part, dob))
        bufq[pairs, :] = tmpq[slot].astype(BF16)
        bufo[pairs, :] = tmpo[slot].astype(BF16)
        for copy in copies(g):
            copy.start()

    for_groups(n_groups, body, UNROLL_GRAD)

    def drain(g, carry):
        for copy in copies(g):
            copy.wait()
        return carry

    lax.fori_loop(0, n_groups, drain, 0)


def final_kernel(
    doc_ref, dk_ref, dv_ref, kd_ref, vd_ref, own_ref, other_ref, gk_ref, gv_ref, rin, tmpk, tmpv, bufk, bufv, sems
):
    tokens, width = kd_ref.shape
    heads = width // 128
    n_groups = tokens // GROUP
    shard = lax.axis_index("seq")
    anchor = shard * tokens
    ends = doc_ends_of(doc_ref)
    begin = start_of(ends, anchor + tokens) - anchor
    place_halves(shard % 2, rin, own_ref, other_ref)
    started = []
    for g in range(n_groups):
        rows = group_rows(g)
        pairs = pl.ds(g * GROUP * heads, GROUP * heads)
        closing = rows_iota(128) + g * GROUP >= begin
        for h in range(heads):
            lanes = slice(h * 128, (h + 1) * 128)
            slot = g % tmpk.shape[0]
            mine = pl.ds(h, GROUP, stride=heads)
            tmpk[slot, mine, :] = dk_ref[rows, lanes] + dot(keep_rows(closing, vd_ref[rows, lanes]), rin[h], NT)
            tmpv[slot, mine, :] = dv_ref[rows, lanes] + dot(keep_rows(closing, kd_ref[rows, lanes]), rin[h])
        bufk[pairs, :] = tmpk[slot].astype(BF16)
        bufv[pairs, :] = tmpv[slot].astype(BF16)
        for n, (buf, out) in enumerate(((bufk, gk_ref), (bufv, gv_ref))):
            copy = pltpu.make_async_copy(buf.at[pairs], out.at[pairs], sems.at[n, g])
            copy.start()
            started.append(copy)
    for copy in started:
        copy.wait()


def call(kernel, name, outs, scratch, in_hbm=(), out_hbm=(), flops=0, n_in=0, limit=16):
    vmem = pl.BlockSpec(memory_space=pltpu.VMEM)
    hbm = pl.BlockSpec(memory_space=pltpu.HBM)
    return pl.pallas_call(
        kernel,
        name=name,
        out_shape=[jax.ShapeDtypeStruct(s, d) for s, d in outs],
        in_specs=[pl.BlockSpec(memory_space=pltpu.SMEM)]
        + [hbm if i in in_hbm else vmem for i in range(n_in)],
        out_specs=[hbm if i in out_hbm else vmem for i in range(len(outs))],
        scratch_shapes=scratch,
        cost_estimate=pl.CostEstimate(flops=flops, bytes_accessed=8 << 20, transcendentals=0),
        compiler_params=pltpu.CompilerParams(vmem_limit_bytes=limit << 20),
    )


def per_device(queries, keys, values, cotangent, doc_lengths):
    tokens, heads, head_width = queries.shape
    width = heads * head_width
    half = heads // 2
    n_groups = tokens // GROUP
    n_seq = lax.axis_size("seq")
    n_head = lax.axis_size("head")
    n_chips = n_seq // 2

    def pairs(x):
        return x.reshape(tokens * heads, head_width)

    q2, k2, v2, c2 = pairs(queries), pairs(keys), pairs(values), pairs(cotangent)
    full = (tokens, width)
    piece = (half, head_width, head_width)
    state_shape = (heads, head_width, head_width)
    flat = (tokens * heads, head_width)
    buf = pltpu.VMEM(flat, BF16)
    tmp = pltpu.VMEM((2, GROUP * heads, head_width), F32)
    sems = pltpu.SemaphoreType.DMA((2, n_groups))
    swap_pairs = [(i, i ^ 1) for i in range(n_seq)]

    def swap(x):
        return lax.ppermute(x, "seq", swap_pairs)

    def exchange(mine, send, weights, sign, after):
        got = swap(send)
        chip_state, after = lax.optimization_barrier((weights[0] * mine + weights[1] * got, after))
        total = jnp.zeros(piece, F32)
        for k in range(1, n_chips):
            links = [(i, i + 2 * k * sign) for i in range(n_seq) if 0 <= i + 2 * k * sign < n_seq]
            total = total + weights[5 + k] * lax.ppermute(chip_state, "seq", links)
        return got, total, after

    def finish(mine, got, total, weights):
        return weights[2] * total + weights[3] * got, swap(weights[4] * total + weights[5] * mine)

    mm = 2 * tokens * heads * head_width * head_width
    table = ((5 + n_chips, 128), F32)
    kd, vd, mine, send, fore, back = call(
        functools.partial(state_kernel, n_seq),
        "shard_state",
        [(full, BF16), (full, BF16), (piece, F32), (piece, F32), table, table],
        [tmp, tmp, pltpu.VMEM(state_shape, F32)],
        n_in=2,
        flops=mm,
    )(doc_lengths, k2, v2)
    got, total, (kd_b, vd_b) = exchange(mine, send, fore, 1, (kd, vd))
    qd, qt, cd, probs, o_local, sb = call(
        local_kernel,
        "local_mix",
        [
            (full, BF16),
            ((width, tokens), BF16),
            (full, BF16),
            ((heads, tokens, GROUP), BF16),
            (full, F32),
            ((n_groups, heads, head_width, head_width), BF16),
        ],
        [tmp, tmp, pltpu.VMEM(state_shape, F32)],
        n_in=4,
        flops=6 * mm,
    )(doc_lengths, kd_b, vd_b, q2, c2)
    own, other = finish(mine, got, total, fore)
    o, sin, stats = call(
        stats_kernel,
        "mix_and_stats",
        [(full, F32), (state_shape, BF16), ((n_head, 2, tokens), F32)],
        [],
        n_in=5,
        flops=mm,
    )(doc_lengths, qd, o_local, cd, own, other)
    stats = lax.all_to_all(stats, "head", 0, 0)
    dob, inv, mine, send = call(
        functools.partial(norm_kernel, float(width * n_head)),
        "norm_back",
        [(full, BF16), ((tokens, head_width), F32), (piece, F32), (piece, F32)],
        [pltpu.VMEM(state_shape, F32)],
        n_in=4,
        flops=mm,
    )(doc_lengths, stats, o, cd, qt)
    got, total, (dob_b, inv_b) = exchange(mine, send, back, -1, (dob, inv))
    dk, dv, output, grad_q = call(
        grad_kernel,
        "local_grads",
        [(full, F32), (full, F32), (flat, BF16), (flat, BF16)],
        [tmp, tmp, buf, buf, pltpu.VMEM(state_shape, F32), sems],
        n_in=10,
        out_hbm=(2, 3),
        flops=12 * mm,
    )(doc_lengths, o, inv_b, dob_b, probs, qd, qt, kd, vd, sb, sin)
    own, other = finish(mine, got, total, back)
    grad_k, grad_v = call(
        final_kernel,
        "final_grads",
        [(flat, BF16), (flat, BF16)],
        [pltpu.VMEM(state_shape, BF16), tmp, tmp, buf, buf, sems],
        n_in=6,
        out_hbm=(0, 1),
        flops=2 * mm,
    )(doc_lengths, dk, dv, kd, vd, own, other)
    return tuple(x.reshape(queries.shape) for x in (output, grad_q, grad_k, grad_v))


def solution(mesh):
    spec = P("seq", "head", None)
    return jax.shard_map(
        per_device,
        mesh=mesh,
        in_specs=(spec, spec, spec, spec, P()),
        out_specs=(spec, spec, spec, spec),
        check_vma=False,
    )
```

```python
import functools

import jax
import jax.numpy as jnp
from jax import lax
from jax.experimental import pallas as pl
from jax.experimental.pallas import tpu as pltpu
from jax.sharding import PartitionSpec as P

GROUP = 256
EPSILON = 1e-06
F32 = jnp.float32
BF16 = jnp.bfloat16

NN = (((1,), (0,)), ((), ()))
NT = (((1,), (1,)), ((), ()))
TN = (((0,), (0,)), ((), ()))


def dot(a, b, dims=NN):
    return lax.dot_general(a, b, dims, preferred_element_type=F32)


def doc_ends_of(doc_ref):
    ends, total = [], jnp.int32(0)
    for j in range(doc_ref.shape[0]):
        total = total + doc_ref[j]
        ends.append(total)
    return ends


def start_of(ends, place):
    found = jnp.int32(0)
    for end in ends:
        found = jnp.where(end <= place, end, found)
    return found


def end_of(ends, place):
    found = jnp.int32(2**30)
    for end in reversed(ends):
        found = jnp.where(end > place, end, found)
    return found


def rows_iota(width):
    return lax.broadcasted_iota(jnp.int32, (GROUP, width), 0)


def lanes_iota(rows):
    return lax.broadcasted_iota(jnp.int32, (rows, GROUP), 1)


def group_mask(ends, first):
    place = lanes_iota(8) + first
    begin = jnp.zeros((8, GROUP), jnp.int32)
    for end in ends:
        begin = jnp.where(place >= end, end, begin)
    begin = begin - first
    begin = jnp.concatenate([begin] * (GROUP // 8), axis=0)
    row = rows_iota(GROUP)
    return (row >= begin) & (row <= lanes_iota(GROUP))


def keep_where(keep, x):
    return jnp.where(keep, x.astype(F32), 0.0).astype(BF16)


def at(h):
    return slice(h * 128, (h + 1) * 128)


def turn(x):
    return x.astype(BF16).T


def pair_rows(g, heads):
    return pl.ds(pl.multiple_of(g * (GROUP * heads), GROUP * heads), GROUP * heads)


def split_heads(buf_ref, tmp_ref, g, heads):
    slot = g % tmp_ref.shape[0]
    tmp_ref[slot] = buf_ref[pair_rows(g, heads), :].astype(F32)
    return [tmp_ref[slot, pl.ds(h, GROUP, stride=heads), :] for h in range(heads)]


def group_rows(g):
    return pl.ds(pl.multiple_of(g * GROUP, GROUP), GROUP)


def weights_of(out_ref, ends, shard, tokens, n_seq, sign):
    core = shard % 2
    chip_first = (shard - core) * tokens
    middle = chip_first + tokens
    chip_end = middle + tokens
    if sign > 0:
        join = start_of(ends, chip_end - 1) < middle
        onward = start_of(ends, middle - 1) < chip_first
        same = [
            start_of(ends, chip_first - 1) < chip_first - 2 * tokens * k for k in range(n_seq // 2 - 1)
        ]
        is_near = core == 0
    else:
        join = end_of(ends, chip_first) > middle
        onward = end_of(ends, middle) > chip_end
        same = [end_of(ends, chip_end) > chip_end + 2 * tokens * k for k in range(n_seq // 2 - 1)]
        is_near = core == 1
    join, onward, is_near = (x.astype(F32) for x in (join, onward, is_near))
    far = 1.0 - is_near
    table = [
        is_near * join + far,
        is_near + far * join,
        is_near + far * onward,
        far,
        is_near * onward + far,
        is_near,
    ] + [x.astype(F32) for x in same]
    for i, x in enumerate(table):
        out_ref[pl.ds(i, 1), :] = jnp.full((1, 128), x, F32)


def state_kernel(
    n_seq, doc_hbm, k2_ref, v2_ref, kd_ref, vd_ref, vt_ref, mine_ref, send_ref, fore_ref, back_ref,
    doc_ref, bufk, bufv, tmpk, tmpv, acc, sems, doc_sem,
):
    tokens, width = kd_ref.shape
    heads = width // 128
    half = heads // 2
    n_groups = tokens // GROUP

    def fetches(g):
        rows = pair_rows(g, heads)
        return (
            pltpu.make_async_copy(k2_ref.at[rows], bufk.at[rows], sems.at[0, g]),
            pltpu.make_async_copy(v2_ref.at[rows], bufv.at[rows], sems.at[1, g]),
        )

    doc_copy = pltpu.make_async_copy(doc_hbm, doc_ref, doc_sem)
    doc_copy.start()
    for g in range(n_groups):
        for copy in fetches(g):
            copy.start()
    doc_copy.wait()
    shard = lax.axis_index("seq")
    core = shard % 2
    anchor = shard * tokens
    ends = doc_ends_of(doc_ref)
    weights_of(fore_ref, ends, shard, tokens, n_seq, 1)
    weights_of(back_ref, ends, shard, tokens, n_seq, -1)
    tail = start_of(ends, anchor + tokens - 1) - anchor

    def prepare(g):
        for copy in fetches(g):
            copy.wait()
        rows = group_rows(g)
        keep = rows_iota(128) + g * GROUP >= tail
        ks = split_heads(bufk, tmpk, g, heads)
        vs = split_heads(bufv, tmpv, g, heads)
        ready = []
        for h in range(heads):
            vt = turn(vs[h])
            kd_ref[rows, at(h)] = ks[h].astype(BF16)
            vd_ref[rows, at(h)] = vs[h].astype(BF16)
            vt_ref[at(h), rows] = vt
            ready.append((vt, jnp.where(keep, ks[h], 0.0).astype(BF16)))
        return ready

    total = [jnp.zeros((128, 128), F32) for _ in range(heads)]
    ahead = prepare(0)
    for g in range(n_groups):
        ready = ahead
        if g + 1 < n_groups:
            ahead = prepare(g + 1)
        total = [t + dot(vt, k) for t, (vt, k) in zip(total, ready)]
    for h in range(heads):
        acc[h] = total[h]
    mine_ref[...] = acc[pl.ds(core * half, half)]
    send_ref[...] = acc[pl.ds((1 - core) * half, half)]


def local_kernel(
    doc_ref, kd_ref, vt_ref, q2_ref, c2_ref, qd_ref, qt_ref, kt_ref, ct_ref, pt_ref, ol_ref, sl_ref,
    tmpq, tmpc,
):
    tokens, width = kd_ref.shape
    heads = width // 128
    n_groups = tokens // GROUP
    anchor = lax.axis_index("seq") * tokens
    ends = doc_ends_of(doc_ref)

    def prepare(g):
        rows = group_rows(g)
        qs = split_heads(q2_ref, tmpq, g, heads)
        cs = split_heads(c2_ref, tmpc, g, heads)
        qts = []
        for h in range(heads):
            qt = turn(qs[h])
            qd_ref[rows, at(h)] = qs[h].astype(BF16)
            qt_ref[at(h), rows] = qt
            kt_ref[at(h), rows] = turn(kd_ref[rows, at(h)])
            ct_ref[at(h), rows] = turn(cs[h])
            qts.append(qt)
        return qts

    def scores(g, qts):
        rows = group_rows(g)
        mask = group_mask(ends, anchor + g * GROUP)
        pts = []
        for h in range(heads):
            pt = jnp.where(mask, dot(kd_ref[rows, at(h)], qts[h]), 0.0).astype(BF16)
            pt_ref[h, rows, :] = pt
            pts.append(pt)
        return pts

    state = [jnp.zeros((128, 128), F32) for _ in range(heads)]
    next_pts = scores(0, prepare(0))
    next_qts = prepare(1) if n_groups > 1 else None
    for g in range(n_groups):
        pts = next_pts
        if g + 1 < n_groups:
            next_pts = scores(g + 1, next_qts)
        if g + 2 < n_groups:
            next_qts = prepare(g + 2)
        first = anchor + g * GROUP
        rows = group_rows(g)
        begin = start_of(ends, first + GROUP - 1)
        tail = rows_iota(128) >= begin - first
        kept = (begin < first).astype(F32)
        for h in range(heads):
            vt = vt_ref[at(h), rows]
            sl_ref[g, h] = state[h]
            state[h] = state[h] * kept + dot(vt, keep_where(tail, kd_ref[rows, at(h)]))
            ol_ref[at(h), rows] = dot(vt, pts[h])


def place_halves(core, out_ref, own_ref, other_ref):
    half = own_ref.shape[0]
    out_ref[pl.ds(core * half, half)] = own_ref[...]
    out_ref[pl.ds((1 - core) * half, half)] = other_ref[...]


def stats_kernel(doc_ref, qt_ref, ol_ref, ct_ref, sl_ref, own_ref, other_ref, o_ref, sb_ref, st_ref, sin):
    width, tokens = qt_ref.shape
    heads = width // 128
    n_groups = tokens // GROUP
    shard = lax.axis_index("seq")
    anchor = shard * tokens
    ends = doc_ends_of(doc_ref)
    place_halves(shard % 2, sin, own_ref, other_ref)

    def opened_terms(g):
        rows = group_rows(g)
        first = anchor + g * GROUP
        opened = lanes_iota(128) < end_of(ends, first - 1) - first
        same = (start_of(ends, first - 1) < anchor).astype(F32)
        terms = []
        for h in range(heads):
            sb = (sl_ref[g, h] + same * sin[h]).astype(BF16)
            sb_ref[g, h] = sb
            terms.append(jnp.where(opened, dot(sb, qt_ref[at(h), rows]), 0.0))
        return terms

    ahead = opened_terms(0)
    for g in range(n_groups):
        terms = ahead
        if g + 1 < n_groups:
            ahead = opened_terms(g + 1)
        rows = group_rows(g)
        squares = jnp.zeros((1, GROUP), F32)
        inner = jnp.zeros((1, GROUP), F32)
        for h in range(heads):
            o = ol_ref[at(h), rows] + terms[h]
            o_ref[at(h), rows] = o
            squares += jnp.sum(o * o, axis=0, keepdims=True)
            inner += jnp.sum(o * ct_ref[at(h), rows].astype(F32), axis=0, keepdims=True)
        both = jnp.concatenate([squares, inner], axis=0)
        for r in range(st_ref.shape[0]):
            st_ref[r, :, rows] = both


def norm_kernel(
    width_all, doc_ref, st_ref, o_ref, ct_ref, qd_ref, dobt_ref, inv_ref, mine_ref, send_ref, acc
):
    tokens, width = qd_ref.shape
    heads = width // 128
    half = heads // 2
    n_groups = tokens // GROUP
    shard = lax.axis_index("seq")
    core = shard % 2
    anchor = shard * tokens
    ends = doc_ends_of(doc_ref)
    head_to = end_of(ends, anchor) - anchor

    def prepare(g):
        rows = group_rows(g)
        keep = lanes_iota(128) + g * GROUP < head_to
        total = st_ref[0, :, rows]
        for r in range(1, st_ref.shape[0]):
            total = total + st_ref[r, :, rows]
        total = total * (1.0 / width_all)
        inv = lax.rsqrt(total[0:1] + EPSILON)
        slope = total[1:2] * inv * inv * inv
        inv_ref[:, rows] = jnp.broadcast_to(inv, (8, GROUP))
        ready = []
        for h in range(heads):
            dob = inv * ct_ref[at(h), rows].astype(F32) - slope * o_ref[at(h), rows]
            dobt_ref[at(h), rows] = dob.astype(BF16)
            ready.append(jnp.where(keep, dob, 0.0).astype(BF16))
        return ready

    total = [jnp.zeros((128, 128), F32) for _ in range(heads)]
    ahead = prepare(0)
    for g in range(n_groups):
        ready = ahead
        if g + 1 < n_groups:
            ahead = prepare(g + 1)
        total = [total[h] + dot(ready[h], qd_ref[group_rows(g), at(h)]) for h in range(heads)]
    for h in range(heads):
        acc[h] = total[h]
    mine_ref[...] = acc[pl.ds(core * half, half)]
    send_ref[...] = acc[pl.ds((1 - core) * half, half)]


def grad_kernel(
    doc_ref, o_ref, inv_ref, dobt_ref, pt_ref, qd_ref, kt_ref, vd_ref, sb_ref,
    dk_ref, dv_ref, rl_ref, out_ref, gq_ref, tmpo, tmpq, bufo, bufq, sems,
):
    tokens, width = qd_ref.shape
    heads = width // 128
    n_groups = tokens // GROUP
    anchor = lax.axis_index("seq") * tokens
    ends = doc_ends_of(doc_ref)

    def scores(g):
        rows = group_rows(g)
        mask = group_mask(ends, anchor + g * GROUP)
        return [
            jnp.where(mask, dot(vd_ref[rows, at(h)], dobt_ref[at(h), rows]), 0.0).astype(BF16)
            for h in range(heads)
        ]

    state = [jnp.zeros((128, 128), F32) for _ in range(heads)]
    started = []
    ahead = scores(n_groups - 1)
    for g in reversed(range(n_groups)):
        dpts = ahead
        slot = g % tmpq.shape[0]
        first = anchor + g * GROUP
        rows = group_rows(g)
        pairs = pair_rows(g, heads)
        opened = lanes_iota(128) < end_of(ends, first - 1) - first
        end = end_of(ends, first)
        head_part = lanes_iota(128) < end - first
        kept = (end > first + GROUP).astype(F32)
        for h in range(heads):
            mine = pl.ds(h, GROUP, stride=heads)
            dv_ref[rows, at(h)] = dot(pt_ref[h, rows, :], turn(dobt_ref[at(h), rows]))
            tmpo[slot, mine, :] = turn(o_ref[at(h), rows] * inv_ref[0:1, rows]).astype(F32)
        bufo[pairs, :] = tmpo[slot].astype(BF16)
        if g > 0:
            ahead = scores(g - 1)
        near, grown = [], []
        for h in range(heads):
            dobt = dobt_ref[at(h), rows]
            near.append(jnp.where(opened, dot(turn(sb_ref[g, h]), dobt), 0.0))
            grown.append(dot(keep_where(head_part, dobt), qd_ref[rows, at(h)]))
        for h in range(heads):
            mine = pl.ds(h, GROUP, stride=heads)
            dk_ref[rows, at(h)] = dot(dpts[h], qd_ref[rows, at(h)])
            gq = dot(kt_ref[at(h), rows], dpts[h]) + near[h]
            tmpq[slot, mine, :] = turn(gq).astype(F32)
            rl_ref[g, h] = state[h]
            state[h] = state[h] * kept + grown[h]
        bufq[pairs, :] = tmpq[slot].astype(BF16)
        for n, (buf, out) in enumerate(((bufo, out_ref), (bufq, gq_ref))):
            copy = pltpu.make_async_copy(buf.at[pairs], out.at[pairs], sems.at[n, g])
            copy.start()
            started.append(copy)
    for copy in started:
        copy.wait()


def final_kernel(
    doc_ref, dk_ref, dv_ref, kd_ref, vd_ref, rl_ref, own_ref, other_ref, gk_ref, gv_ref,
    rin, tmpk, tmpv, bufk, bufv, sems,
):
    tokens, width = kd_ref.shape
    heads = width // 128
    n_groups = tokens // GROUP
    shard = lax.axis_index("seq")
    anchor = shard * tokens
    ends = doc_ends_of(doc_ref)
    place_halves(shard % 2, rin, own_ref, other_ref)

    def closing_terms(g):
        rows = group_rows(g)
        after = anchor + (g + 1) * GROUP
        closing = rows_iota(128) + (after - GROUP) >= start_of(ends, after)
        same = (end_of(ends, after) > anchor + tokens).astype(F32)
        terms = []
        for h in range(heads):
            rb = (rl_ref[g, h] + same * rin[h]).astype(BF16)
            terms.append(
                (
                    jnp.where(closing, dot(vd_ref[rows, at(h)], rb), 0.0),
                    jnp.where(closing, dot(kd_ref[rows, at(h)], rb, NT), 0.0),
                )
            )
        return terms

    started = []
    ahead = closing_terms(0)
    for g in range(n_groups):
        terms = ahead
        if g + 1 < n_groups:
            ahead = closing_terms(g + 1)
        rows = group_rows(g)
        pairs = pair_rows(g, heads)
        slot = g % tmpk.shape[0]
        for h in range(heads):
            mine = pl.ds(h, GROUP, stride=heads)
            tmpk[slot, mine, :] = dk_ref[rows, at(h)] + terms[h][0]
            tmpv[slot, mine, :] = dv_ref[rows, at(h)] + terms[h][1]
        bufk[pairs, :] = tmpk[slot].astype(BF16)
        bufv[pairs, :] = tmpv[slot].astype(BF16)
        for n, (buf, out) in enumerate(((bufk, gk_ref), (bufv, gv_ref))):
            copy = pltpu.make_async_copy(buf.at[pairs], out.at[pairs], sems.at[n, g])
            copy.start()
            started.append(copy)
    for copy in started:
        copy.wait()


def call(kernel, name, outs, scratch, in_hbm=(), out_hbm=(), flops=0, n_in=0, doc_hbm=False):
    vmem = pl.BlockSpec(memory_space=pltpu.VMEM)
    hbm = pl.BlockSpec(memory_space=pltpu.HBM)
    return pl.pallas_call(
        kernel,
        name=name,
        out_shape=[jax.ShapeDtypeStruct(s, d) for s, d in outs],
        in_specs=[hbm if doc_hbm else pl.BlockSpec(memory_space=pltpu.SMEM)]
        + [hbm if i in in_hbm else vmem for i in range(n_in)],
        out_specs=[hbm if i in out_hbm else vmem for i in range(len(outs))],
        scratch_shapes=scratch,
        cost_estimate=pl.CostEstimate(flops=flops, bytes_accessed=8 << 20, transcendentals=0),
        compiler_params=pltpu.CompilerParams(vmem_limit_bytes=16 << 20),
    )


def per_device(queries, keys, values, cotangent, doc_lengths):
    tokens, heads, head_width = queries.shape
    width = heads * head_width
    half = heads // 2
    n_groups = tokens // GROUP
    n_seq = lax.axis_size("seq")
    n_head = lax.axis_size("head")
    n_chips = n_seq // 2

    def pairs(x):
        return x.reshape(tokens * heads, head_width)

    q2, k2, v2, c2 = pairs(queries), pairs(keys), pairs(values), pairs(cotangent)
    full = (tokens, width)
    piece = (half, head_width, head_width)
    state_shape = (heads, head_width, head_width)
    flat = (tokens * heads, head_width)
    buf = pltpu.VMEM(flat, BF16)
    tmp = pltpu.VMEM((2, GROUP * heads, head_width), F32)
    sems = pltpu.SemaphoreType.DMA((2, n_groups))
    swap_pairs = [(i, i ^ 1) for i in range(n_seq)]

    def swap(x):
        return lax.ppermute(x, "seq", swap_pairs)

    def exchange(mine, send, weights, sign, after):
        got = swap(send)
        chip_state, after = lax.optimization_barrier((weights[0] * mine + weights[1] * got, after))
        total = jnp.zeros(piece, F32)
        for k in range(1, n_chips):
            links = [(i, i + 2 * k * sign) for i in range(n_seq) if 0 <= i + 2 * k * sign < n_seq]
            total = total + weights[5 + k] * lax.ppermute(chip_state, "seq", links)
        return got, total, after

    def finish(mine, got, total, weights):
        return weights[2] * total + weights[3] * got, swap(weights[4] * total + weights[5] * mine)

    mm = 2 * tokens * heads * head_width * head_width
    table = ((5 + n_chips, 128), F32)
    state = pltpu.VMEM(state_shape, F32)
    table = ((5 + n_chips, 128), F32)
    turned = (width, tokens)
    group_states = (n_groups, heads, head_width, head_width)
    kd, vd, vt, mine, send, fore, back = call(
        functools.partial(state_kernel, n_seq),
        "shard_state",
        [(full, BF16), (full, BF16), (turned, BF16), (piece, F32), (piece, F32), table, table],
        [
            pltpu.SMEM(doc_lengths.shape, jnp.int32),
            buf,
            buf,
            tmp,
            tmp,
            state,
            sems,
            pltpu.SemaphoreType.DMA,
        ],
        n_in=2,
        in_hbm=(0, 1),
        doc_hbm=True,
        flops=mm,
    )(*(pltpu.with_memory_space_constraint(x, pltpu.HBM) for x in (doc_lengths, k2, v2)))
    got, total, (kd_b, vt_b) = exchange(mine, send, fore, 1, (kd, vt))
    qd, qt, kt, ct, pt, o_local, sl = call(
        local_kernel,
        "local_mix",
        [
            (full, BF16),
            (turned, BF16),
            (turned, BF16),
            (turned, BF16),
            ((heads, tokens, GROUP), BF16),
            (turned, F32),
            (group_states, F32),
        ],
        [tmp, tmp],
        n_in=4,
        flops=6 * mm,
    )(doc_lengths, kd_b, vt_b, q2, c2)
    own, other = finish(mine, got, total, fore)
    o, sb, stats = call(
        stats_kernel,
        "mix_and_stats",
        [(turned, F32), (group_states, BF16), ((n_head, 2, tokens), F32)],
        [state],
        n_in=6,
        flops=mm,
    )(doc_lengths, qt, o_local, ct, sl, own, other)
    stats = lax.all_to_all(stats, "head", 0, 0)
    dobt, inv, mine, send = call(
        functools.partial(norm_kernel, float(width * n_head)),
        "norm_back",
        [(turned, BF16), ((8, tokens), F32), (piece, F32), (piece, F32)],
        [state],
        n_in=4,
        flops=mm,
    )(doc_lengths, stats, o, ct, qd)
    got, total, (dobt_b, inv_b) = exchange(mine, send, back, -1, (dobt, inv))
    dk, dv, rl, output, grad_q = call(
        grad_kernel,
        "local_grads",
        [(full, F32), (full, F32), (group_states, F32), (flat, BF16), (flat, BF16)],
        [tmp, tmp, buf, buf, sems],
        n_in=8,
        out_hbm=(3, 4),
        flops=12 * mm,
    )(doc_lengths, o, inv_b, dobt_b, pt, qd, kt, vd, sb)
    own, other = finish(mine, got, total, back)
    grad_k, grad_v = call(
        final_kernel,
        "final_grads",
        [(flat, BF16), (flat, BF16)],
        [state, tmp, tmp, buf, buf, sems],
        n_in=7,
        out_hbm=(0, 1),
        flops=2 * mm,
    )(doc_lengths, dk, dv, kd, vd, rl, own, other)
    return tuple(x.reshape(queries.shape) for x in (output, grad_q, grad_k, grad_v))


def solution(mesh):
    spec = P("seq", "head", None)
    return jax.shard_map(
        per_device,
        mesh=mesh,
        in_specs=(spec, spec, spec, spec, P()),
        out_specs=(spec, spec, spec, spec),
        check_vma=False,
    )
```

```python
import functools

import jax
import jax.numpy as jnp
from jax import lax
from jax.experimental import pallas as pl
from jax.experimental.pallas import tpu as pltpu
from jax.sharding import PartitionSpec as P

GROUP = 256
EPSILON = 1e-06
F32 = jnp.float32
BF16 = jnp.bfloat16

NN = (((1,), (0,)), ((), ()))
NT = (((1,), (1,)), ((), ()))
TN = (((0,), (0,)), ((), ()))


def dot(a, b, dims=NN):
    return lax.dot_general(a, b, dims, preferred_element_type=F32)


def doc_ends_of(doc_ref):
    ends, total = [], jnp.int32(0)
    for j in range(doc_ref.shape[0]):
        total = total + doc_ref[j]
        ends.append(total)
    return ends


def start_of(ends, place):
    found = jnp.int32(0)
    for end in ends:
        found = jnp.where(end <= place, end, found)
    return found


def end_of(ends, place):
    found = jnp.int32(2**30)
    for end in reversed(ends):
        found = jnp.where(end > place, end, found)
    return found


def rows_iota(width):
    return lax.broadcasted_iota(jnp.int32, (GROUP, width), 0)


def lanes_iota(rows):
    return lax.broadcasted_iota(jnp.int32, (rows, GROUP), 1)


def group_mask(ends, first):
    place = lanes_iota(8) + first
    begin = jnp.zeros((8, GROUP), jnp.int32)
    for end in ends:
        begin = jnp.where(place >= end, end, begin)
    begin = begin - first
    begin = jnp.concatenate([begin] * (GROUP // 8), axis=0)
    row = rows_iota(GROUP)
    return (row >= begin) & (row <= lanes_iota(GROUP))


def keep_where(keep, x):
    return jnp.where(keep, x.astype(F32), 0.0).astype(BF16)


def at(h):
    return slice(h * 128, (h + 1) * 128)


def turn(x):
    return x.astype(BF16).T


def pair_rows(g, heads):
    return pl.ds(pl.multiple_of(g * (GROUP * heads), GROUP * heads), GROUP * heads)


def split_heads(buf_ref, tmp_ref, g, heads):
    slot = g % tmp_ref.shape[0]
    tmp_ref[slot] = buf_ref[pair_rows(g, heads), :].astype(F32)
    return [tmp_ref[slot, pl.ds(h, GROUP, stride=heads), :] for h in range(heads)]


def group_rows(g):
    return pl.ds(pl.multiple_of(g * GROUP, GROUP), GROUP)


def source_of(index, step, size):
    if size & (size - 1):
        return (index + size - step) % size
    return index ^ step


def links_of(step, size):
    return [(source_of(i, step, size), i) for i in range(size)]


def weights_of(out_ref, ends, shard, tokens, n_seq, sign):
    core = shard % 2
    chip = shard // 2
    n_chips = n_seq // 2
    others = [source_of(chip, k, n_chips) for k in range(1, n_chips)]
    chip_first = (shard - core) * tokens
    middle = chip_first + tokens
    chip_end = middle + tokens
    if sign > 0:
        join = start_of(ends, chip_end - 1) < middle
        onward = start_of(ends, middle - 1) < chip_first
        begin = start_of(ends, chip_first - 1)
        same = [(other < chip) & (begin < (other + 1) * (2 * tokens)) for other in others]
        is_near = core == 0
    else:
        join = end_of(ends, chip_first) > middle
        onward = end_of(ends, middle) > chip_end
        end = end_of(ends, chip_end)
        same = [(other > chip) & (end > other * (2 * tokens)) for other in others]
        is_near = core == 1
    join, onward, is_near = (x.astype(F32) for x in (join, onward, is_near))
    far = 1.0 - is_near
    table = [
        is_near * join + far,
        is_near + far * join,
        is_near + far * onward,
        far,
        is_near * onward + far,
        is_near,
    ] + [x.astype(F32) for x in same]
    for i, x in enumerate(table):
        out_ref[pl.ds(i, 1), :] = jnp.full((1, 128), x, F32)


def state_kernel(
    n_seq, doc_hbm, k2_ref, v2_ref, kd_ref, vd_ref, vt_ref, mine_ref, send_ref, fore_ref, back_ref,
    doc_ref, bufk, bufv, tmpk, tmpv, acc, sems, doc_sem,
):
    tokens, width = kd_ref.shape
    heads = width // 128
    half = heads // 2
    n_groups = tokens // GROUP

    def fetches(g):
        rows = pair_rows(g, heads)
        return (
            pltpu.make_async_copy(k2_ref.at[rows], bufk.at[rows], sems.at[0, g]),
            pltpu.make_async_copy(v2_ref.at[rows], bufv.at[rows], sems.at[1, g]),
        )

    doc_copy = pltpu.make_async_copy(doc_hbm, doc_ref, doc_sem)
    doc_copy.start()
    for g in range(n_groups):
        for copy in fetches(g):
            copy.start()
    doc_copy.wait()
    shard = lax.axis_index("seq")
    core = shard % 2
    anchor = shard * tokens
    ends = doc_ends_of(doc_ref)
    weights_of(fore_ref, ends, shard, tokens, n_seq, 1)
    weights_of(back_ref, ends, shard, tokens, n_seq, -1)
    tail = start_of(ends, anchor + tokens - 1) - anchor

    def prepare(g):
        for copy in fetches(g):
            copy.wait()
        rows = group_rows(g)
        keep = rows_iota(128) + g * GROUP >= tail
        ks = split_heads(bufk, tmpk, g, heads)
        vs = split_heads(bufv, tmpv, g, heads)
        ready = []
        for h in range(heads):
            vt = turn(vs[h])
            kd_ref[rows, at(h)] = ks[h].astype(BF16)
            vd_ref[rows, at(h)] = vs[h].astype(BF16)
            vt_ref[at(h), rows] = vt
            ready.append((vt, jnp.where(keep, ks[h], 0.0).astype(BF16)))
        return ready

    total = [jnp.zeros((128, 128), F32) for _ in range(heads)]
    ahead = prepare(0)
    for g in range(n_groups):
        ready = ahead
        if g + 1 < n_groups:
            ahead = prepare(g + 1)
        total = [t + dot(vt, k) for t, (vt, k) in zip(total, ready)]
    for h in range(heads):
        acc[h] = total[h]
    mine_ref[...] = acc[pl.ds(core * half, half)]
    send_ref[...] = acc[pl.ds((1 - core) * half, half)]


def local_kernel(
    doc_ref, kd_ref, vt_ref, q2_ref, c2_ref, qd_ref, qt_ref, kt_ref, ct_ref, pt_ref, ol_ref, sl_ref,
    tmpq, tmpc,
):
    tokens, width = kd_ref.shape
    heads = width // 128
    n_groups = tokens // GROUP
    anchor = lax.axis_index("seq") * tokens
    ends = doc_ends_of(doc_ref)

    def prepare(g):
        rows = group_rows(g)
        qs = split_heads(q2_ref, tmpq, g, heads)
        cs = split_heads(c2_ref, tmpc, g, heads)
        qts = []
        for h in range(heads):
            qt = turn(qs[h])
            qd_ref[rows, at(h)] = qs[h].astype(BF16)
            qt_ref[at(h), rows] = qt
            kt_ref[at(h), rows] = turn(kd_ref[rows, at(h)])
            ct_ref[at(h), rows] = turn(cs[h])
            qts.append(qt)
        return qts

    def scores(g, qts):
        rows = group_rows(g)
        mask = group_mask(ends, anchor + g * GROUP)
        pts = []
        for h in range(heads):
            pt = jnp.where(mask, dot(kd_ref[rows, at(h)], qts[h]), 0.0).astype(BF16)
            pt_ref[h, rows, :] = pt
            pts.append(pt)
        return pts

    state = [jnp.zeros((128, 128), F32) for _ in range(heads)]
    next_pts = scores(0, prepare(0))
    next_qts = prepare(1) if n_groups > 1 else None
    for g in range(n_groups):
        pts = next_pts
        if g + 1 < n_groups:
            next_pts = scores(g + 1, next_qts)
        if g + 2 < n_groups:
            next_qts = prepare(g + 2)
        first = anchor + g * GROUP
        rows = group_rows(g)
        begin = start_of(ends, first + GROUP - 1)
        tail = rows_iota(128) >= begin - first
        kept = (begin < first).astype(F32)
        for h in range(heads):
            vt = vt_ref[at(h), rows]
            sl_ref[g, h] = state[h]
            state[h] = state[h] * kept + dot(vt, keep_where(tail, kd_ref[rows, at(h)]))
            ol_ref[at(h), rows] = dot(vt, pts[h])


def place_halves(core, out_ref, own_ref, other_ref):
    half = own_ref.shape[0]
    out_ref[pl.ds(core * half, half)] = own_ref[...]
    out_ref[pl.ds((1 - core) * half, half)] = other_ref[...]


def stats_kernel(doc_ref, qt_ref, ol_ref, ct_ref, sl_ref, own_ref, other_ref, o_ref, sb_ref, st_ref, sin):
    width, tokens = qt_ref.shape
    heads = width // 128
    n_groups = tokens // GROUP
    shard = lax.axis_index("seq")
    anchor = shard * tokens
    ends = doc_ends_of(doc_ref)
    place_halves(shard % 2, sin, own_ref, other_ref)

    def opened_terms(g):
        rows = group_rows(g)
        first = anchor + g * GROUP
        opened = lanes_iota(128) < end_of(ends, first - 1) - first
        same = (start_of(ends, first - 1) < anchor).astype(F32)
        terms = []
        for h in range(heads):
            sb = (sl_ref[g, h] + same * sin[h]).astype(BF16)
            sb_ref[g, h] = sb
            terms.append(jnp.where(opened, dot(sb, qt_ref[at(h), rows]), 0.0))
        return terms

    ahead = opened_terms(0)
    for g in range(n_groups):
        terms = ahead
        if g + 1 < n_groups:
            ahead = opened_terms(g + 1)
        rows = group_rows(g)
        squares = jnp.zeros((1, GROUP), F32)
        inner = jnp.zeros((1, GROUP), F32)
        for h in range(heads):
            o = ol_ref[at(h), rows] + terms[h]
            o_ref[at(h), rows] = o
            squares += jnp.sum(o * o, axis=0, keepdims=True)
            inner += jnp.sum(o * ct_ref[at(h), rows].astype(F32), axis=0, keepdims=True)
        both = jnp.concatenate([squares, inner], axis=0)
        st_ref[:, rows] = both


def norm_kernel(
    width_all, doc_ref, st_ref, o_ref, ct_ref, qd_ref, dobt_ref, inv_ref, mine_ref, send_ref, acc
):
    tokens, width = qd_ref.shape
    heads = width // 128
    half = heads // 2
    n_groups = tokens // GROUP
    shard = lax.axis_index("seq")
    core = shard % 2
    anchor = shard * tokens
    ends = doc_ends_of(doc_ref)
    head_to = end_of(ends, anchor) - anchor

    def prepare(g):
        rows = group_rows(g)
        keep = lanes_iota(128) + g * GROUP < head_to
        total = st_ref[:, rows] * (1.0 / width_all)
        inv = lax.rsqrt(total[0:1] + EPSILON)
        slope = total[1:2] * inv * inv * inv
        inv_ref[:, rows] = jnp.broadcast_to(inv, (8, GROUP))
        ready = []
        for h in range(heads):
            dob = inv * ct_ref[at(h), rows].astype(F32) - slope * o_ref[at(h), rows]
            dobt_ref[at(h), rows] = dob.astype(BF16)
            ready.append(jnp.where(keep, dob, 0.0).astype(BF16))
        return ready

    total = [jnp.zeros((128, 128), F32) for _ in range(heads)]
    ahead = prepare(0)
    for g in range(n_groups):
        ready = ahead
        if g + 1 < n_groups:
            ahead = prepare(g + 1)
        total = [total[h] + dot(ready[h], qd_ref[group_rows(g), at(h)]) for h in range(heads)]
    for h in range(heads):
        acc[h] = total[h]
    mine_ref[...] = acc[pl.ds(core * half, half)]
    send_ref[...] = acc[pl.ds((1 - core) * half, half)]


def grad_kernel(
    doc_ref, o_ref, inv_ref, dobt_ref, pt_ref, qd_ref, kt_ref, vd_ref, sb_ref,
    dk_ref, dv_ref, rl_ref, out_ref, gq_ref, tmpo, tmpq, bufo, bufq, sems,
):
    tokens, width = qd_ref.shape
    heads = width // 128
    n_groups = tokens // GROUP
    anchor = lax.axis_index("seq") * tokens
    ends = doc_ends_of(doc_ref)

    def scores(g):
        rows = group_rows(g)
        mask = group_mask(ends, anchor + g * GROUP)
        return [
            jnp.where(mask, dot(vd_ref[rows, at(h)], dobt_ref[at(h), rows]), 0.0).astype(BF16)
            for h in range(heads)
        ]

    state = [jnp.zeros((128, 128), F32) for _ in range(heads)]
    started = []
    ahead = scores(n_groups - 1)
    for g in reversed(range(n_groups)):
        dpts = ahead
        slot = g % tmpq.shape[0]
        first = anchor + g * GROUP
        rows = group_rows(g)
        pairs = pair_rows(g, heads)
        opened = lanes_iota(128) < end_of(ends, first - 1) - first
        end = end_of(ends, first)
        head_part = lanes_iota(128) < end - first
        kept = (end > first + GROUP).astype(F32)
        for h in range(heads):
            mine = pl.ds(h, GROUP, stride=heads)
            dv_ref[rows, at(h)] = dot(pt_ref[h, rows, :], turn(dobt_ref[at(h), rows]))
            tmpo[slot, mine, :] = turn(o_ref[at(h), rows] * inv_ref[0:1, rows]).astype(F32)
        bufo[pairs, :] = tmpo[slot].astype(BF16)
        if g > 0:
            ahead = scores(g - 1)
        near, grown = [], []
        for h in range(heads):
            dobt = dobt_ref[at(h), rows]
            near.append(jnp.where(opened, dot(turn(sb_ref[g, h]), dobt), 0.0))
            grown.append(dot(keep_where(head_part, dobt), qd_ref[rows, at(h)]))
        for h in range(heads):
            mine = pl.ds(h, GROUP, stride=heads)
            dk_ref[rows, at(h)] = dot(dpts[h], qd_ref[rows, at(h)])
            gq = dot(kt_ref[at(h), rows], dpts[h]) + near[h]
            tmpq[slot, mine, :] = turn(gq).astype(F32)
            rl_ref[g, h] = state[h]
            state[h] = state[h] * kept + grown[h]
        bufq[pairs, :] = tmpq[slot].astype(BF16)
        for n, (buf, out) in enumerate(((bufo, out_ref), (bufq, gq_ref))):
            copy = pltpu.make_async_copy(buf.at[pairs], out.at[pairs], sems.at[n, g])
            copy.start()
            started.append(copy)
    for copy in started:
        copy.wait()


def final_kernel(
    doc_ref, dk_ref, dv_ref, kd_ref, vd_ref, rl_ref, own_ref, other_ref, gk_ref, gv_ref,
    rin, tmpk, tmpv, bufk, bufv, sems,
):
    tokens, width = kd_ref.shape
    heads = width // 128
    n_groups = tokens // GROUP
    shard = lax.axis_index("seq")
    anchor = shard * tokens
    ends = doc_ends_of(doc_ref)
    place_halves(shard % 2, rin, own_ref, other_ref)

    def closing_terms(g):
        rows = group_rows(g)
        after = anchor + (g + 1) * GROUP
        closing = rows_iota(128) + (after - GROUP) >= start_of(ends, after)
        same = (end_of(ends, after) > anchor + tokens).astype(F32)
        terms = []
        for h in range(heads):
            rb = (rl_ref[g, h] + same * rin[h]).astype(BF16)
            terms.append(
                (
                    jnp.where(closing, dot(vd_ref[rows, at(h)], rb), 0.0),
                    jnp.where(closing, dot(kd_ref[rows, at(h)], rb, NT), 0.0),
                )
            )
        return terms

    started = []
    ahead = closing_terms(0)
    for g in range(n_groups):
        terms = ahead
        if g + 1 < n_groups:
            ahead = closing_terms(g + 1)
        rows = group_rows(g)
        pairs = pair_rows(g, heads)
        slot = g % tmpk.shape[0]
        for h in range(heads):
            mine = pl.ds(h, GROUP, stride=heads)
            tmpk[slot, mine, :] = dk_ref[rows, at(h)] + terms[h][0]
            tmpv[slot, mine, :] = dv_ref[rows, at(h)] + terms[h][1]
        bufk[pairs, :] = tmpk[slot].astype(BF16)
        bufv[pairs, :] = tmpv[slot].astype(BF16)
        for n, (buf, out) in enumerate(((bufk, gk_ref), (bufv, gv_ref))):
            copy = pltpu.make_async_copy(buf.at[pairs], out.at[pairs], sems.at[n, g])
            copy.start()
            started.append(copy)
    for copy in started:
        copy.wait()


def call(kernel, name, outs, scratch, in_hbm=(), out_hbm=(), flops=0, n_in=0, doc_hbm=False):
    vmem = pl.BlockSpec(memory_space=pltpu.VMEM)
    hbm = pl.BlockSpec(memory_space=pltpu.HBM)
    return pl.pallas_call(
        kernel,
        name=name,
        out_shape=[jax.ShapeDtypeStruct(s, d) for s, d in outs],
        in_specs=[hbm if doc_hbm else pl.BlockSpec(memory_space=pltpu.SMEM)]
        + [hbm if i in in_hbm else vmem for i in range(n_in)],
        out_specs=[hbm if i in out_hbm else vmem for i in range(len(outs))],
        scratch_shapes=scratch,
        cost_estimate=pl.CostEstimate(flops=flops, bytes_accessed=8 << 20, transcendentals=0),
        compiler_params=pltpu.CompilerParams(vmem_limit_bytes=16 << 20),
    )


def per_device(queries, keys, values, cotangent, doc_lengths):
    tokens, heads, head_width = queries.shape
    width = heads * head_width
    half = heads // 2
    n_groups = tokens // GROUP
    n_seq = lax.axis_size("seq")
    n_head = lax.axis_size("head")
    n_chips = n_seq // 2

    def pairs(x):
        return x.reshape(tokens * heads, head_width)

    q2, k2, v2, c2 = pairs(queries), pairs(keys), pairs(values), pairs(cotangent)
    full = (tokens, width)
    piece = (half, head_width, head_width)
    state_shape = (heads, head_width, head_width)
    flat = (tokens * heads, head_width)
    buf = pltpu.VMEM(flat, BF16)
    tmp = pltpu.VMEM((2, GROUP * heads, head_width), F32)
    sems = pltpu.SemaphoreType.DMA((2, n_groups))
    swap_pairs = [(i, i ^ 1) for i in range(n_seq)]

    def swap(x):
        return lax.ppermute(x, "seq", swap_pairs)

    def exchange(mine, send, weights, after):
        got = swap(send)
        chip_state, after = lax.optimization_barrier((weights[0] * mine + weights[1] * got, after))
        total = jnp.zeros(piece, F32)
        for k in range(1, n_chips):
            links = [(2 * i + c, 2 * j + c) for i, j in links_of(k, n_chips) for c in (0, 1)]
            total = total + weights[5 + k] * lax.ppermute(chip_state, "seq", links)
        return got, total, after

    def finish(mine, got, total, weights):
        return weights[2] * total + weights[3] * got, swap(weights[4] * total + weights[5] * mine)

    mm = 2 * tokens * heads * head_width * head_width
    table = ((5 + n_chips, 128), F32)
    state = pltpu.VMEM(state_shape, F32)
    table = ((5 + n_chips, 128), F32)
    turned = (width, tokens)
    group_states = (n_groups, heads, head_width, head_width)
    kd, vd, vt, mine, send, fore, back = call(
        functools.partial(state_kernel, n_seq),
        "shard_state",
        [(full, BF16), (full, BF16), (turned, BF16), (piece, F32), (piece, F32), table, table],
        [
            pltpu.SMEM(doc_lengths.shape, jnp.int32),
            buf,
            buf,
            tmp,
            tmp,
            state,
            sems,
            pltpu.SemaphoreType.DMA,
        ],
        n_in=2,
        in_hbm=(0, 1),
        doc_hbm=True,
        flops=mm,
    )(*(pltpu.with_memory_space_constraint(x, pltpu.HBM) for x in (doc_lengths, k2, v2)))
    got, total, (kd_b, vt_b) = exchange(mine, send, fore, (kd, vt))
    qd, qt, kt, ct, pt, o_local, sl = call(
        local_kernel,
        "local_mix",
        [
            (full, BF16),
            (turned, BF16),
            (turned, BF16),
            (turned, BF16),
            ((heads, tokens, GROUP), BF16),
            (turned, F32),
            (group_states, F32),
        ],
        [tmp, tmp],
        n_in=4,
        flops=6 * mm,
    )(doc_lengths, kd_b, vt_b, q2, c2)
    own, other = finish(mine, got, total, fore)
    o, sb, stats = call(
        stats_kernel,
        "mix_and_stats",
        [(turned, F32), (group_states, BF16), ((2, tokens), F32)],
        [state],
        n_in=6,
        flops=mm,
    )(doc_lengths, qt, o_local, ct, sl, own, other)
    stats = stats + sum(
        lax.ppermute(stats, "head", links_of(k, n_head)) for k in range(1, n_head)
    )
    dobt, inv, mine, send = call(
        functools.partial(norm_kernel, float(width * n_head)),
        "norm_back",
        [(turned, BF16), ((8, tokens), F32), (piece, F32), (piece, F32)],
        [state],
        n_in=4,
        flops=mm,
    )(doc_lengths, stats, o, ct, qd)
    got, total, (dobt_b, inv_b) = exchange(mine, send, back, (dobt, inv))
    dk, dv, rl, output, grad_q = call(
        grad_kernel,
        "local_grads",
        [(full, F32), (full, F32), (group_states, F32), (flat, BF16), (flat, BF16)],
        [tmp, tmp, buf, buf, sems],
        n_in=8,
        out_hbm=(3, 4),
        flops=12 * mm,
    )(doc_lengths, o, inv_b, dobt_b, pt, qd, kt, vd, sb)
    own, other = finish(mine, got, total, back)
    grad_k, grad_v = call(
        final_kernel,
        "final_grads",
        [(flat, BF16), (flat, BF16)],
        [state, tmp, tmp, buf, buf, sems],
        n_in=7,
        out_hbm=(0, 1),
        flops=2 * mm,
    )(doc_lengths, dk, dv, kd, vd, rl, own, other)
    return tuple(x.reshape(queries.shape) for x in (output, grad_q, grad_k, grad_v))


def solution(mesh):
    spec = P("seq", "head", None)
    return jax.shard_map(
        per_device,
        mesh=mesh,
        in_specs=(spec, spec, spec, spec, P()),
        out_specs=(spec, spec, spec, spec),
        check_vma=False,
    )
```

```python
import functools

import jax
import jax.numpy as jnp
from jax import lax
from jax.experimental import pallas as pl
from jax.experimental.pallas import tpu as pltpu
from jax.sharding import PartitionSpec as P

GROUP = 256
EPSILON = 1e-06
F32 = jnp.float32
BF16 = jnp.bfloat16

NN = (((1,), (0,)), ((), ()))
NT = (((1,), (1,)), ((), ()))
TN = (((0,), (0,)), ((), ()))


def dot(a, b, dims=NN):
    return lax.dot_general(a, b, dims, preferred_element_type=F32)


def doc_ends_of(doc_ref):
    ends, total = [], jnp.int32(0)
    for j in range(doc_ref.shape[0]):
        total = total + doc_ref[j]
        ends.append(total)
    return ends


def start_of(ends, place):
    found = jnp.int32(0)
    for end in ends:
        found = jnp.where(end <= place, end, found)
    return found


def end_of(ends, place):
    found = jnp.int32(2**30)
    for end in reversed(ends):
        found = jnp.where(end > place, end, found)
    return found


def rows_iota(width):
    return lax.broadcasted_iota(jnp.int32, (GROUP, width), 0)


def lanes_iota(rows):
    return lax.broadcasted_iota(jnp.int32, (rows, GROUP), 1)


def group_mask(ends, first):
    place = lanes_iota(8) + first
    begin = jnp.zeros((8, GROUP), jnp.int32)
    for end in ends:
        begin = jnp.where(place >= end, end, begin)
    begin = begin - first
    begin = jnp.concatenate([begin] * (GROUP // 8), axis=0)
    row = rows_iota(GROUP)
    return (row >= begin) & (row <= lanes_iota(GROUP))


def keep_where(keep, x):
    return jnp.where(keep, x.astype(F32), 0.0).astype(BF16)


def at(h):
    return slice(h * 128, (h + 1) * 128)


def turn(x):
    return x.astype(BF16).T


def pair_rows(g, heads):
    return pl.ds(pl.multiple_of(g * (GROUP * heads), GROUP * heads), GROUP * heads)


def split_heads(buf_ref, tmp_ref, g, heads):
    slot = g % tmp_ref.shape[0]
    tmp_ref[slot] = buf_ref[pair_rows(g, heads), :].astype(F32)
    return [tmp_ref[slot, pl.ds(h, GROUP, stride=heads), :] for h in range(heads)]


def group_rows(g):
    return pl.ds(pl.multiple_of(g * GROUP, GROUP), GROUP)


def source_of(index, step, size):
    if size & (size - 1):
        return (index + size - step) % size
    return index ^ step


def links_of(step, size):
    return [(source_of(i, step, size), i) for i in range(size)]


def weights_of(out_ref, ends, shard, tokens, n_seq, sign):
    core = shard % 2
    chip = shard // 2
    n_chips = n_seq // 2
    others = [source_of(chip, k, n_chips) for k in range(1, n_chips)]
    chip_first = (shard - core) * tokens
    middle = chip_first + tokens
    chip_end = middle + tokens
    if sign > 0:
        join = start_of(ends, chip_end - 1) < middle
        onward = start_of(ends, middle - 1) < chip_first
        begin = start_of(ends, chip_first - 1)
        same = [(other < chip) & (begin < (other + 1) * (2 * tokens)) for other in others]
        is_near = core == 0
    else:
        join = end_of(ends, chip_first) > middle
        onward = end_of(ends, middle) > chip_end
        end = end_of(ends, chip_end)
        same = [(other > chip) & (end > other * (2 * tokens)) for other in others]
        is_near = core == 1
    join, onward, is_near = (x.astype(F32) for x in (join, onward, is_near))
    far = 1.0 - is_near
    table = [
        is_near * join + far,
        is_near + far * join,
        is_near + far * onward,
        far,
        is_near * onward + far,
        is_near,
    ] + [x.astype(F32) for x in same]
    for i, x in enumerate(table):
        out_ref[pl.ds(i, 1), :] = jnp.full((1, 128), x, F32)


def state_kernel(
    n_seq, doc_hbm, k2_ref, v2_ref, kd_ref, vd_ref, vt_ref, mine_ref, send_ref, fore_ref, back_ref,
    doc_ref, bufk, bufv, tmpk, tmpv, acc, sems, doc_sem,
):
    tokens, width = kd_ref.shape
    heads = width // 128
    half = heads // 2
    n_groups = tokens // GROUP

    def fetches(g):
        rows = pair_rows(g, heads)
        return (
            pltpu.make_async_copy(k2_ref.at[rows], bufk.at[rows], sems.at[0, g]),
            pltpu.make_async_copy(v2_ref.at[rows], bufv.at[rows], sems.at[1, g]),
        )

    doc_copy = pltpu.make_async_copy(doc_hbm, doc_ref, doc_sem)
    doc_copy.start()
    for g in range(n_groups):
        for copy in fetches(g):
            copy.start()
    doc_copy.wait()
    shard = lax.axis_index("seq")
    core = shard % 2
    anchor = shard * tokens
    ends = doc_ends_of(doc_ref)
    weights_of(fore_ref, ends, shard, tokens, n_seq, 1)
    weights_of(back_ref, ends, shard, tokens, n_seq, -1)
    tail = start_of(ends, anchor + tokens - 1) - anchor

    def prepare(g):
        for copy in fetches(g):
            copy.wait()
        rows = group_rows(g)
        keep = rows_iota(128) + g * GROUP >= tail
        ks = split_heads(bufk, tmpk, g, heads)
        vs = split_heads(bufv, tmpv, g, heads)
        ready = []
        for h in range(heads):
            vt = turn(vs[h])
            kd_ref[rows, at(h)] = ks[h].astype(BF16)
            vd_ref[rows, at(h)] = vs[h].astype(BF16)
            vt_ref[at(h), rows] = vt
            ready.append((vt, jnp.where(keep, ks[h], 0.0).astype(BF16)))
        return ready

    total = [jnp.zeros((128, 128), F32) for _ in range(heads)]
    ahead = prepare(0)
    for g in range(n_groups):
        ready = ahead
        if g + 1 < n_groups:
            ahead = prepare(g + 1)
        total = [t + dot(vt, k) for t, (vt, k) in zip(total, ready)]
    for h in range(heads):
        acc[h] = total[h]
    mine_ref[...] = acc[pl.ds(core * half, half)]
    send_ref[...] = acc[pl.ds((1 - core) * half, half)]


def local_kernel(
    doc_ref, kd_ref, vt_ref, q2_ref, c2_ref, qd_ref, qt_ref, kt_ref, ct_ref, pt_ref, ol_ref, sl_ref,
    tmpq, tmpc,
):
    tokens, width = kd_ref.shape
    heads = width // 128
    n_groups = tokens // GROUP
    anchor = lax.axis_index("seq") * tokens
    ends = doc_ends_of(doc_ref)

    def prepare(g):
        rows = group_rows(g)
        qs = split_heads(q2_ref, tmpq, g, heads)
        cs = split_heads(c2_ref, tmpc, g, heads)
        qts = []
        for h in range(heads):
            qt = turn(qs[h])
            qd_ref[rows, at(h)] = qs[h].astype(BF16)
            qt_ref[at(h), rows] = qt
            kt_ref[at(h), rows] = turn(kd_ref[rows, at(h)])
            ct_ref[at(h), rows] = turn(cs[h])
            qts.append(qt)
        return qts

    def scores(g, qts):
        rows = group_rows(g)
        mask = group_mask(ends, anchor + g * GROUP)
        pts = []
        for h in range(heads):
            pt = jnp.where(mask, dot(kd_ref[rows, at(h)], qts[h]), 0.0).astype(BF16)
            pt_ref[h, rows, :] = pt
            pts.append(pt)
        return pts

    state = [jnp.zeros((128, 128), F32) for _ in range(heads)]
    next_pts = scores(0, prepare(0))
    next_qts = prepare(1) if n_groups > 1 else None
    for g in range(n_groups):
        pts = next_pts
        if g + 1 < n_groups:
            next_pts = scores(g + 1, next_qts)
        if g + 2 < n_groups:
            next_qts = prepare(g + 2)
        first = anchor + g * GROUP
        rows = group_rows(g)
        begin = start_of(ends, first + GROUP - 1)
        tail = rows_iota(128) >= begin - first
        kept = (begin < first).astype(F32)
        for h in range(heads):
            vt = vt_ref[at(h), rows]
            sl_ref[g, h] = state[h]
            state[h] = state[h] * kept + dot(vt, keep_where(tail, kd_ref[rows, at(h)]))
            ol_ref[at(h), rows] = dot(vt, pts[h])


def place_halves(core, out_ref, own_ref, other_ref):
    half = own_ref.shape[0]
    out_ref[pl.ds(core * half, half)] = own_ref[...]
    out_ref[pl.ds((1 - core) * half, half)] = other_ref[...]


def part_of(core, own, half):
    return (core if own else 1 - core) * half


def head_rows(head):
    return pl.ds(pl.multiple_of(head * 128, 128), 128)


def stats_kernel(own, doc_ref, qt_ref, ol_ref, ct_ref, sl_ref, state_ref, *refs):
    (before_ref, o_ref, sb_ref, st_ref) = refs if len(refs) == 4 else (None, *refs)
    width, tokens = qt_ref.shape
    half = state_ref.shape[0]
    n_groups = tokens // GROUP
    shard = lax.axis_index("seq")
    base = part_of(shard % 2, own, half)
    anchor = shard * tokens
    ends = doc_ends_of(doc_ref)

    def opened_terms(g):
        rows = group_rows(g)
        first = anchor + g * GROUP
        opened = lanes_iota(128) < end_of(ends, first - 1) - first
        same = (start_of(ends, first - 1) < anchor).astype(F32)
        terms = []
        for h in range(half):
            sb = (sl_ref[g, base + h] + same * state_ref[h]).astype(BF16)
            sb_ref[g, h] = sb
            terms.append(jnp.where(opened, dot(sb, qt_ref[head_rows(base + h), rows]), 0.0))
        return terms

    ahead = opened_terms(0)
    for g in range(n_groups):
        terms = ahead
        if g + 1 < n_groups:
            ahead = opened_terms(g + 1)
        rows = group_rows(g)
        squares = jnp.zeros((1, GROUP), F32)
        inner = jnp.zeros((1, GROUP), F32)
        for h in range(half):
            o = ol_ref[head_rows(base + h), rows] + terms[h]
            o_ref[at(h), rows] = o
            squares += jnp.sum(o * o, axis=0, keepdims=True)
            inner += jnp.sum(o * ct_ref[head_rows(base + h), rows].astype(F32), axis=0, keepdims=True)
        both = jnp.concatenate([squares, inner], axis=0)
        st_ref[:, rows] = both if before_ref is None else both + before_ref[:, rows]


def back_state(half, n_groups, prepare, qd_ref, base, out_ref):
    total = [jnp.zeros((128, 128), F32) for _ in range(half)]
    ahead = prepare(0)
    for g in range(n_groups):
        ready = ahead
        if g + 1 < n_groups:
            ahead = prepare(g + 1)
        total = [
            total[h] + dot(ready[h], qd_ref[group_rows(g), head_rows(base + h)]) for h in range(half)
        ]
    for h in range(half):
        out_ref[h] = total[h]


def norm_kernel(
    width_all, doc_ref, st_ref, o_ref, ct_ref, qd_ref, dobt_ref, rows_ref, send_ref
):
    tokens, width = qd_ref.shape
    half = send_ref.shape[0]
    shard = lax.axis_index("seq")
    base = part_of(shard % 2, False, half)
    anchor = shard * tokens
    ends = doc_ends_of(doc_ref)
    head_to = end_of(ends, anchor) - anchor

    def prepare(g):
        rows = group_rows(g)
        keep = lanes_iota(128) + g * GROUP < head_to
        total = st_ref[:, rows] * (1.0 / width_all)
        inv = lax.rsqrt(total[0:1] + EPSILON)
        slope = total[1:2] * inv * inv * inv
        rows_ref[:, rows] = jnp.concatenate([inv, slope] * 4, axis=0)
        ready = []
        for h in range(half):
            dob = inv * ct_ref[head_rows(base + h), rows].astype(F32) - slope * o_ref[at(h), rows]
            dobt_ref[at(h), rows] = dob.astype(BF16)
            ready.append(jnp.where(keep, dob, 0.0).astype(BF16))
        return ready

    back_state(half, tokens // GROUP, prepare, qd_ref, base, send_ref)


def merge_kernel(
    doc_ref, rows_ref, own_ref, other_ref, ct_ref, qd_ref, dob_other_ref, sb_own_ref, sb_other_ref,
    dobt_ref, normed_ref, sb_ref, mine_ref,
):
    tokens, width = qd_ref.shape
    half = mine_ref.shape[0]
    shard = lax.axis_index("seq")
    core = shard % 2
    base, far = part_of(core, True, half), part_of(core, False, half)
    anchor = shard * tokens
    ends = doc_ends_of(doc_ref)
    head_to = end_of(ends, anchor) - anchor

    def prepare(g):
        rows = group_rows(g)
        keep = lanes_iota(128) + g * GROUP < head_to
        inv = rows_ref[0:1, rows]
        slope = rows_ref[1:2, rows]
        ready = []
        for h in range(half):
            mine, others = head_rows(base + h), head_rows(far + h)
            o = own_ref[at(h), rows]
            dob = inv * ct_ref[mine, rows].astype(F32) - slope * o
            dobt_ref[mine, rows] = dob.astype(BF16)
            dobt_ref[others, rows] = dob_other_ref[at(h), rows]
            normed_ref[mine, rows] = (o * inv).astype(BF16)
            normed_ref[others, rows] = (other_ref[at(h), rows] * inv).astype(BF16)
            sb_ref[g, base + h] = sb_own_ref[g, h]
            sb_ref[g, far + h] = sb_other_ref[g, h]
            ready.append(jnp.where(keep, dob, 0.0).astype(BF16))
        return ready

    back_state(half, tokens // GROUP, prepare, qd_ref, base, mine_ref)


def grad_kernel(
    doc_ref, normed_ref, dobt_ref, pt_ref, qd_ref, kt_ref, vd_ref, sb_ref,
    dk_ref, dv_ref, rl_ref, out_ref, gq_ref, tmpo, tmpq, bufo, bufq, sems,
):
    tokens, width = qd_ref.shape
    heads = width // 128
    n_groups = tokens // GROUP
    anchor = lax.axis_index("seq") * tokens
    ends = doc_ends_of(doc_ref)

    def scores(g):
        rows = group_rows(g)
        mask = group_mask(ends, anchor + g * GROUP)
        return [
            jnp.where(mask, dot(vd_ref[rows, at(h)], dobt_ref[at(h), rows]), 0.0).astype(BF16)
            for h in range(heads)
        ]

    state = [jnp.zeros((128, 128), F32) for _ in range(heads)]
    started = []
    ahead = scores(n_groups - 1)
    for g in reversed(range(n_groups)):
        dpts = ahead
        slot = g % tmpq.shape[0]
        first = anchor + g * GROUP
        rows = group_rows(g)
        pairs = pair_rows(g, heads)
        opened = lanes_iota(128) < end_of(ends, first - 1) - first
        end = end_of(ends, first)
        head_part = lanes_iota(128) < end - first
        kept = (end > first + GROUP).astype(F32)
        for h in range(heads):
            mine = pl.ds(h, GROUP, stride=heads)
            dv_ref[rows, at(h)] = dot(pt_ref[h, rows, :], turn(dobt_ref[at(h), rows]))
            tmpo[slot, mine, :] = normed_ref[at(h), rows].T.astype(F32)
        bufo[pairs, :] = tmpo[slot].astype(BF16)
        if g > 0:
            ahead = scores(g - 1)
        near, grown = [], []
        for h in range(heads):
            dobt = dobt_ref[at(h), rows]
            near.append(jnp.where(opened, dot(turn(sb_ref[g, h]), dobt), 0.0))
            grown.append(dot(keep_where(head_part, dobt), qd_ref[rows, at(h)]))
        for h in range(heads):
            mine = pl.ds(h, GROUP, stride=heads)
            dk_ref[rows, at(h)] = dot(dpts[h], qd_ref[rows, at(h)])
            gq = dot(kt_ref[at(h), rows], dpts[h]) + near[h]
            tmpq[slot, mine, :] = turn(gq).astype(F32)
            rl_ref[g, h] = state[h]
            state[h] = state[h] * kept + grown[h]
        bufq[pairs, :] = tmpq[slot].astype(BF16)
        for n, (buf, out) in enumerate(((bufo, out_ref), (bufq, gq_ref))):
            copy = pltpu.make_async_copy(buf.at[pairs], out.at[pairs], sems.at[n, g])
            copy.start()
            started.append(copy)
    for copy in started:
        copy.wait()


def final_kernel(
    doc_ref, dk_ref, dv_ref, kd_ref, vd_ref, rl_ref, own_ref, other_ref, gk_ref, gv_ref,
    rin, tmpk, tmpv, bufk, bufv, sems,
):
    tokens, width = kd_ref.shape
    heads = width // 128
    n_groups = tokens // GROUP
    shard = lax.axis_index("seq")
    anchor = shard * tokens
    ends = doc_ends_of(doc_ref)
    place_halves(shard % 2, rin, own_ref, other_ref)

    def closing_terms(g):
        rows = group_rows(g)
        after = anchor + (g + 1) * GROUP
        closing = rows_iota(128) + (after - GROUP) >= start_of(ends, after)
        same = (end_of(ends, after) > anchor + tokens).astype(F32)
        terms = []
        for h in range(heads):
            rb = (rl_ref[g, h] + same * rin[h]).astype(BF16)
            terms.append(
                (
                    jnp.where(closing, dot(vd_ref[rows, at(h)], rb), 0.0),
                    jnp.where(closing, dot(kd_ref[rows, at(h)], rb, NT), 0.0),
                )
            )
        return terms

    started = []
    ahead = closing_terms(0)
    for g in range(n_groups):
        terms = ahead
        if g + 1 < n_groups:
            ahead = closing_terms(g + 1)
        rows = group_rows(g)
        pairs = pair_rows(g, heads)
        slot = g % tmpk.shape[0]
        for h in range(heads):
            mine = pl.ds(h, GROUP, stride=heads)
            tmpk[slot, mine, :] = dk_ref[rows, at(h)] + terms[h][0]
            tmpv[slot, mine, :] = dv_ref[rows, at(h)] + terms[h][1]
        bufk[pairs, :] = tmpk[slot].astype(BF16)
        bufv[pairs, :] = tmpv[slot].astype(BF16)
        for n, (buf, out) in enumerate(((bufk, gk_ref), (bufv, gv_ref))):
            copy = pltpu.make_async_copy(buf.at[pairs], out.at[pairs], sems.at[n, g])
            copy.start()
            started.append(copy)
    for copy in started:
        copy.wait()


def call(kernel, name, outs, scratch, in_hbm=(), out_hbm=(), flops=0, n_in=0, doc_hbm=False):
    vmem = pl.BlockSpec(memory_space=pltpu.VMEM)
    hbm = pl.BlockSpec(memory_space=pltpu.HBM)
    return pl.pallas_call(
        kernel,
        name=name,
        out_shape=[jax.ShapeDtypeStruct(s, d) for s, d in outs],
        in_specs=[hbm if doc_hbm else pl.BlockSpec(memory_space=pltpu.SMEM)]
        + [hbm if i in in_hbm else vmem for i in range(n_in)],
        out_specs=[hbm if i in out_hbm else vmem for i in range(len(outs))],
        scratch_shapes=scratch,
        cost_estimate=pl.CostEstimate(flops=flops, bytes_accessed=8 << 20, transcendentals=0),
        compiler_params=pltpu.CompilerParams(vmem_limit_bytes=16 << 20),
    )


def per_device(queries, keys, values, cotangent, doc_lengths):
    tokens, heads, head_width = queries.shape
    width = heads * head_width
    half = heads // 2
    n_groups = tokens // GROUP
    n_seq = lax.axis_size("seq")
    n_head = lax.axis_size("head")
    n_chips = n_seq // 2

    def pairs(x):
        return x.reshape(tokens * heads, head_width)

    q2, k2, v2, c2 = pairs(queries), pairs(keys), pairs(values), pairs(cotangent)
    full = (tokens, width)
    piece = (half, head_width, head_width)
    state_shape = (heads, head_width, head_width)
    flat = (tokens * heads, head_width)
    buf = pltpu.VMEM(flat, BF16)
    tmp = pltpu.VMEM((2, GROUP * heads, head_width), F32)
    sems = pltpu.SemaphoreType.DMA((2, n_groups))
    swap_pairs = [(i, i ^ 1) for i in range(n_seq)]

    def swap(x):
        return lax.ppermute(x, "seq", swap_pairs)

    def exchange(mine, send, weights, after):
        got = swap(send)
        chip_state, after = lax.optimization_barrier((weights[0] * mine + weights[1] * got, after))
        total = jnp.zeros(piece, F32)
        for k in range(1, n_chips):
            links = [(2 * i + c, 2 * j + c) for i, j in links_of(k, n_chips) for c in (0, 1)]
            total = total + weights[5 + k] * lax.ppermute(chip_state, "seq", links)
        return got, total, after

    def finish(mine, got, total, weights):
        return weights[2] * total + weights[3] * got, swap(weights[4] * total + weights[5] * mine)

    mm = 2 * tokens * heads * head_width * head_width
    table = ((5 + n_chips, 128), F32)
    state = pltpu.VMEM(state_shape, F32)
    table = ((5 + n_chips, 128), F32)
    turned = (width, tokens)
    group_states = (n_groups, heads, head_width, head_width)
    kd, vd, vt, mine, send, fore, back = call(
        functools.partial(state_kernel, n_seq),
        "shard_state",
        [(full, BF16), (full, BF16), (turned, BF16), (piece, F32), (piece, F32), table, table],
        [
            pltpu.SMEM(doc_lengths.shape, jnp.int32),
            buf,
            buf,
            tmp,
            tmp,
            state,
            sems,
            pltpu.SemaphoreType.DMA,
        ],
        n_in=2,
        in_hbm=(0, 1),
        doc_hbm=True,
        flops=mm,
    )(*(pltpu.with_memory_space_constraint(x, pltpu.HBM) for x in (doc_lengths, k2, v2)))
    got, total, (kd_b, vt_b, q2_b, c2_b) = exchange(mine, send, fore, (kd, vt, q2, c2))
    qd, qt, kt, ct, pt, o_local, sl = call(
        local_kernel,
        "local_mix",
        [
            (full, BF16),
            (turned, BF16),
            (turned, BF16),
            (turned, BF16),
            ((heads, tokens, GROUP), BF16),
            (turned, F32),
            (group_states, F32),
        ],
        [tmp, tmp],
        n_in=4,
        flops=6 * mm,
    )(doc_lengths, kd_b, vt_b, q2_b, c2_b)
    total, o_local = lax.optimization_barrier((total, o_local))
    own, other = finish(mine, got, total, fore)
    half_turned = (half * head_width, tokens)
    half_states = (n_groups, half, head_width, head_width)

    def part(is_own, states, before, name):
        return call(
            functools.partial(stats_kernel, is_own),
            name,
            [(half_turned, F32), (half_states, BF16), ((2, tokens), F32)],
            [],
            n_in=5 + len(before),
            flops=mm // 2,
        )(doc_lengths, qt, o_local, ct, sl, states, *before)

    o_own, sb_own, stats = part(True, own, (), "mix_own")
    o_other, sb_other, stats = part(False, other, (stats,), "mix_other")
    stats = stats + sum(
        lax.ppermute(stats, "head", links_of(k, n_head)) for k in range(1, n_head)
    )
    dob_other, factors, send = call(
        functools.partial(norm_kernel, float(width * n_head)),
        "norm_other",
        [(half_turned, BF16), ((8, tokens), F32), (piece, F32)],
        [],
        n_in=4,
        flops=mm // 2,
    )(doc_lengths, stats, o_other, ct, qd)
    dobt, normed, sb, mine = call(
        merge_kernel,
        "norm_own",
        [(turned, BF16), (turned, BF16), (group_states, BF16), (piece, F32)],
        [],
        n_in=8,
        flops=mm // 2,
    )(doc_lengths, factors, o_own, o_other, ct, qd, dob_other, sb_own, sb_other)
    got, total, (dobt_b, normed_b) = exchange(mine, send, back, (dobt, normed))
    dk, dv, rl, output, grad_q = call(
        grad_kernel,
        "local_grads",
        [(full, F32), (full, F32), (group_states, F32), (flat, BF16), (flat, BF16)],
        [tmp, tmp, buf, buf, sems],
        n_in=7,
        out_hbm=(3, 4),
        flops=12 * mm,
    )(doc_lengths, normed_b, dobt_b, pt, qd, kt, vd, sb)
    total, dk = lax.optimization_barrier((total, dk))
    own, other = finish(mine, got, total, back)
    grad_k, grad_v = call(
        final_kernel,
        "final_grads",
        [(flat, BF16), (flat, BF16)],
        [state, tmp, tmp, buf, buf, sems],
        n_in=7,
        out_hbm=(0, 1),
        flops=2 * mm,
    )(doc_lengths, dk, dv, kd, vd, rl, own, other)
    return tuple(x.reshape(queries.shape) for x in (output, grad_q, grad_k, grad_v))


def solution(mesh):
    spec = P("seq", "head", None)
    return jax.shard_map(
        per_device,
        mesh=mesh,
        in_specs=(spec, spec, spec, spec, P()),
        out_specs=(spec, spec, spec, spec),
        check_vma=False,
    )
```

```python
import functools

import jax
import jax.numpy as jnp
from jax import lax
from jax.experimental import pallas as pl
from jax.experimental.pallas import tpu as pltpu
from jax.sharding import PartitionSpec as P

GROUP = 256
EPSILON = 1e-06
OPENED, SAME_OPENED, HEAD, KEPT, SHARD_HEAD, CLOSING, SAME_CLOSING, BEGIN = range(8)
F32 = jnp.float32
BF16 = jnp.bfloat16

NN = (((1,), (0,)), ((), ()))
NT = (((1,), (1,)), ((), ()))
TN = (((0,), (0,)), ((), ()))


def dot(a, b, dims=NN):
    return lax.dot_general(a, b, dims, preferred_element_type=F32)


def doc_ends_of(doc_ref):
    ends, total = [], jnp.int32(0)
    for j in range(doc_ref.shape[0]):
        total = total + doc_ref[j]
        ends.append(total)
    return ends


def start_of(ends, place):
    found = jnp.int32(0)
    for end in ends:
        found = jnp.where(end <= place, end, found)
    return found


def end_of(ends, place):
    found = jnp.int32(2**30)
    for end in reversed(ends):
        found = jnp.where(end > place, end, found)
    return found


def rows_iota(width):
    return lax.broadcasted_iota(jnp.int32, (GROUP, width), 0)


def lanes_iota(rows):
    return lax.broadcasted_iota(jnp.int32, (rows, GROUP), 1)


def begin_row(ends, first):
    place = lanes_iota(8) + first
    begin = jnp.zeros((8, GROUP), jnp.int32)
    for end in ends:
        begin = jnp.where(place >= end, end, begin)
    return begin - first


def group_mask(begin):
    row = rows_iota(GROUP)
    return (row >= begin) & (row <= lanes_iota(GROUP))


def write_table(table_ref, ends, anchor, tokens):
    for g in range(tokens // GROUP):
        first = anchor + g * GROUP
        after = first + GROUP
        numbers = {
            OPENED: end_of(ends, first - 1) - first,
            SAME_OPENED: (start_of(ends, first - 1) < anchor).astype(jnp.int32),
            HEAD: end_of(ends, first) - first,
            KEPT: (end_of(ends, first) > after).astype(jnp.int32),
            SHARD_HEAD: end_of(ends, anchor) - first,
            CLOSING: start_of(ends, after) - first,
            SAME_CLOSING: (end_of(ends, after) > anchor + tokens).astype(jnp.int32),
        }
        for kind, number in numbers.items():
            table_ref[kind, pl.ds(g, 1), :] = jnp.full((1, GROUP), number, jnp.int32)
        table_ref[BEGIN, pl.ds(g, 1), :] = begin_row(ends, first)[:1]


def known(table_ref, kind, g, width=GROUP):
    return table_ref[kind, pl.ds(g, 1), :width]


def factor(table_ref, kind, g):
    return known(table_ref, kind, g, 128).astype(F32)


def keep_where(keep, x):
    return jnp.where(keep, x.astype(F32), 0.0).astype(BF16)


def at(h):
    return slice(h * 128, (h + 1) * 128)


def turn(x):
    return x.astype(BF16).T


def pair_rows(g, heads):
    return pl.ds(pl.multiple_of(g * (GROUP * heads), GROUP * heads), GROUP * heads)


def split_heads(buf_ref, tmp_ref, g, heads):
    slot = g % tmp_ref.shape[0]
    tmp_ref[slot] = buf_ref[pair_rows(g, heads), :].astype(F32)
    return [tmp_ref[slot, pl.ds(h, GROUP, stride=heads), :] for h in range(heads)]


def group_rows(g):
    return pl.ds(pl.multiple_of(g * GROUP, GROUP), GROUP)


def source_of(index, step, size):
    if size & (size - 1):
        return (index + size - step) % size
    return index ^ step


def links_of(step, size):
    return [(source_of(i, step, size), i) for i in range(size)]


def weights_of(out_ref, ends, shard, tokens, n_seq, sign):
    core = shard % 2
    chip = shard // 2
    n_chips = n_seq // 2
    others = [source_of(chip, k, n_chips) for k in range(1, n_chips)]
    chip_first = (shard - core) * tokens
    middle = chip_first + tokens
    chip_end = middle + tokens
    if sign > 0:
        join = start_of(ends, chip_end - 1) < middle
        onward = start_of(ends, middle - 1) < chip_first
        begin = start_of(ends, chip_first - 1)
        same = [(other < chip) & (begin < (other + 1) * (2 * tokens)) for other in others]
        is_near = core == 0
    else:
        join = end_of(ends, chip_first) > middle
        onward = end_of(ends, middle) > chip_end
        end = end_of(ends, chip_end)
        same = [(other > chip) & (end > other * (2 * tokens)) for other in others]
        is_near = core == 1
    join, onward, is_near = (x.astype(F32) for x in (join, onward, is_near))
    far = 1.0 - is_near
    table = [
        is_near * join + far,
        is_near + far * join,
        is_near + far * onward,
        far,
        is_near * onward + far,
        is_near,
    ] + [x.astype(F32) for x in same]
    for i, x in enumerate(table):
        out_ref[pl.ds(i, 1), :] = jnp.full((1, 128), x, F32)


def state_kernel(
    n_seq, doc_hbm, k2_ref, v2_ref, kd_ref, vd_ref, vt_ref, mine_ref, send_ref, fore_ref, back_ref,
    doc_ref, bufk, bufv, tmpk, tmpv, acc, sems, doc_sem,
):
    tokens, width = kd_ref.shape
    heads = width // 128
    half = heads // 2
    n_groups = tokens // GROUP

    def fetches(g):
        rows = pair_rows(g, heads)
        return (
            pltpu.make_async_copy(k2_ref.at[rows], bufk.at[rows], sems.at[0, g]),
            pltpu.make_async_copy(v2_ref.at[rows], bufv.at[rows], sems.at[1, g]),
        )

    doc_copy = pltpu.make_async_copy(doc_hbm, doc_ref, doc_sem)
    doc_copy.start()
    for g in range(n_groups):
        for copy in fetches(g):
            copy.start()
    doc_copy.wait()
    shard = lax.axis_index("seq")
    core = shard % 2
    anchor = shard * tokens
    ends = doc_ends_of(doc_ref)
    weights_of(fore_ref, ends, shard, tokens, n_seq, 1)
    weights_of(back_ref, ends, shard, tokens, n_seq, -1)
    tail = start_of(ends, anchor + tokens - 1) - anchor

    def prepare(g):
        for copy in fetches(g):
            copy.wait()
        rows = group_rows(g)
        keep = rows_iota(128) + g * GROUP >= tail
        ks = split_heads(bufk, tmpk, g, heads)
        vs = split_heads(bufv, tmpv, g, heads)
        ready = []
        for h in range(heads):
            vt = turn(vs[h])
            kd_ref[rows, at(h)] = ks[h].astype(BF16)
            vd_ref[rows, at(h)] = vs[h].astype(BF16)
            vt_ref[at(h), rows] = vt
            ready.append((vt, jnp.where(keep, ks[h], 0.0).astype(BF16)))
        return ready

    total = [jnp.zeros((128, 128), F32) for _ in range(heads)]
    ahead = prepare(0)
    for g in range(n_groups):
        ready = ahead
        if g + 1 < n_groups:
            ahead = prepare(g + 1)
        total = [t + dot(vt, k) for t, (vt, k) in zip(total, ready)]
    for h in range(heads):
        acc[h] = total[h]
    mine_ref[...] = acc[pl.ds(core * half, half)]
    send_ref[...] = acc[pl.ds((1 - core) * half, half)]


def local_kernel(
    doc_ref, kd_ref, vt_ref, q2_ref, c2_ref, qd_ref, qt_ref, kt_ref, ct_ref, pt_ref, ol_ref, sl_ref, table_ref,
    tmpq, tmpc,
):
    tokens, width = kd_ref.shape
    heads = width // 128
    n_groups = tokens // GROUP
    anchor = lax.axis_index("seq") * tokens
    ends = doc_ends_of(doc_ref)

    def prepare(g):
        rows = group_rows(g)
        qs = split_heads(q2_ref, tmpq, g, heads)
        cs = split_heads(c2_ref, tmpc, g, heads)
        qts = []
        for h in range(heads):
            qt = turn(qs[h])
            qd_ref[rows, at(h)] = qs[h].astype(BF16)
            qt_ref[at(h), rows] = qt
            kt_ref[at(h), rows] = turn(kd_ref[rows, at(h)])
            ct_ref[at(h), rows] = turn(cs[h])
            qts.append(qt)
        return qts

    def scores(g, qts):
        rows = group_rows(g)
        mask = group_mask(known(table_ref, BEGIN, g))
        pts = []
        for h in range(heads):
            pt = jnp.where(mask, dot(kd_ref[rows, at(h)], qts[h]), 0.0).astype(BF16)
            pt_ref[h, rows, :] = pt
            pts.append(pt)
        return pts

    write_table(table_ref, ends, anchor, tokens)
    state = [jnp.zeros((128, 128), F32) for _ in range(heads)]
    next_pts = scores(0, prepare(0))
    next_qts = prepare(1) if n_groups > 1 else None
    for g in range(n_groups):
        pts = next_pts
        if g + 1 < n_groups:
            next_pts = scores(g + 1, next_qts)
        if g + 2 < n_groups:
            next_qts = prepare(g + 2)
        first = anchor + g * GROUP
        rows = group_rows(g)
        begin = start_of(ends, first + GROUP - 1)
        tail = rows_iota(128) >= begin - first
        kept = (begin < first).astype(F32)
        for h in range(heads):
            vt = vt_ref[at(h), rows]
            sl_ref[g, h] = state[h]
            state[h] = state[h] * kept + dot(vt, keep_where(tail, kd_ref[rows, at(h)]))
            ol_ref[at(h), rows] = dot(vt, pts[h])


def place_halves(core, out_ref, own_ref, other_ref):
    half = own_ref.shape[0]
    out_ref[pl.ds(core * half, half)] = own_ref[...]
    out_ref[pl.ds((1 - core) * half, half)] = other_ref[...]


def part_of(core, own, half):
    return (core if own else 1 - core) * half


def head_rows(head):
    return pl.ds(pl.multiple_of(head * 128, 128), 128)


def stats_kernel(own, table_ref, qt_ref, ol_ref, ct_ref, sl_ref, state_ref, *refs):
    (before_ref, o_ref, sb_ref, st_ref) = refs if len(refs) == 4 else (None, *refs)
    width, tokens = qt_ref.shape
    half = state_ref.shape[0]
    n_groups = tokens // GROUP
    base = part_of(lax.axis_index("seq") % 2, own, half)

    def opened_terms(g):
        rows = group_rows(g)
        opened = lanes_iota(128) < known(table_ref, OPENED, g)
        same = factor(table_ref, SAME_OPENED, g)
        terms = []
        for h in range(half):
            sb = (sl_ref[g, base + h] + same * state_ref[h]).astype(BF16)
            sb_ref[g, h] = sb
            terms.append(jnp.where(opened, dot(sb, qt_ref[head_rows(base + h), rows]), 0.0))
        return terms

    ahead = opened_terms(0)
    for g in range(n_groups):
        terms = ahead
        if g + 1 < n_groups:
            ahead = opened_terms(g + 1)
        rows = group_rows(g)
        squares = jnp.zeros((1, GROUP), F32)
        inner = jnp.zeros((1, GROUP), F32)
        for h in range(half):
            o = ol_ref[head_rows(base + h), rows] + terms[h]
            o_ref[at(h), rows] = o
            squares += jnp.sum(o * o, axis=0, keepdims=True)
            inner += jnp.sum(o * ct_ref[head_rows(base + h), rows].astype(F32), axis=0, keepdims=True)
        both = jnp.concatenate([squares, inner], axis=0)
        st_ref[:, rows] = both if before_ref is None else both + before_ref[:, rows]


def back_state(half, n_groups, prepare, qd_ref, base, out_ref):
    total = [jnp.zeros((128, 128), F32) for _ in range(half)]
    ahead = prepare(0)
    for g in range(n_groups):
        ready = ahead
        if g + 1 < n_groups:
            ahead = prepare(g + 1)
        total = [
            total[h] + dot(ready[h], qd_ref[group_rows(g), head_rows(base + h)]) for h in range(half)
        ]
    for h in range(half):
        out_ref[h] = total[h]


def norm_kernel(
    width_all, table_ref, st_ref, o_ref, ct_ref, qd_ref, dobt_ref, rows_ref, send_ref
):
    tokens, width = qd_ref.shape
    half = send_ref.shape[0]
    base = part_of(lax.axis_index("seq") % 2, False, half)

    def prepare(g):
        rows = group_rows(g)
        keep = lanes_iota(128) < known(table_ref, SHARD_HEAD, g)
        total = st_ref[:, rows] * (1.0 / width_all)
        inv = lax.rsqrt(total[0:1] + EPSILON)
        slope = total[1:2] * inv * inv * inv
        rows_ref[:, rows] = jnp.concatenate([inv, slope] * 4, axis=0)
        ready = []
        for h in range(half):
            dob = inv * ct_ref[head_rows(base + h), rows].astype(F32) - slope * o_ref[at(h), rows]
            dobt_ref[at(h), rows] = dob.astype(BF16)
            ready.append(jnp.where(keep, dob, 0.0).astype(BF16))
        return ready

    back_state(half, tokens // GROUP, prepare, qd_ref, base, send_ref)


def merge_kernel(
    table_ref, rows_ref, own_ref, other_ref, ct_ref, qd_ref, dob_other_ref, sb_own_ref, sb_other_ref,
    dobt_ref, normed_ref, sb_ref, mine_ref,
):
    tokens, width = qd_ref.shape
    half = mine_ref.shape[0]
    core = lax.axis_index("seq") % 2
    base, far = part_of(core, True, half), part_of(core, False, half)

    def prepare(g):
        rows = group_rows(g)
        keep = lanes_iota(128) < known(table_ref, SHARD_HEAD, g)
        inv = rows_ref[0:1, rows]
        slope = rows_ref[1:2, rows]
        ready = []
        for h in range(half):
            mine, others = head_rows(base + h), head_rows(far + h)
            o = own_ref[at(h), rows]
            dob = inv * ct_ref[mine, rows].astype(F32) - slope * o
            dobt_ref[mine, rows] = dob.astype(BF16)
            dobt_ref[others, rows] = dob_other_ref[at(h), rows]
            normed_ref[mine, rows] = (o * inv).astype(BF16)
            normed_ref[others, rows] = (other_ref[at(h), rows] * inv).astype(BF16)
            sb_ref[g, base + h] = sb_own_ref[g, h]
            sb_ref[g, far + h] = sb_other_ref[g, h]
            ready.append(jnp.where(keep, dob, 0.0).astype(BF16))
        return ready

    back_state(half, tokens // GROUP, prepare, qd_ref, base, mine_ref)


def grad_kernel(groups, *refs):
    table_ref, normed_ref, dobt_ref, pt_ref, qd_ref, kt_ref, vd_ref, sb_ref, *refs = refs
    width = dobt_ref.shape[0]
    heads = width // 128
    n_groups = dobt_ref.shape[1] // GROUP
    state = [jnp.zeros((128, 128), F32) for _ in range(heads)]
    if groups.stop < n_groups:
        state_ref, _, _, *refs = refs
        state = [state_ref[h] for h in range(heads)]
    left_ref = None
    if groups.start > 0:
        left_ref, *refs = refs
    dk_ref, dv_ref, rl_ref, out_ref, gq_ref, tmpo, tmpq, bufo, bufq, sems = refs

    def scores(g):
        rows = group_rows(g)
        mask = group_mask(known(table_ref, BEGIN, g))
        return [
            jnp.where(mask, dot(vd_ref[rows, at(h)], dobt_ref[at(h), rows]), 0.0).astype(BF16)
            for h in range(heads)
        ]

    started = []
    ahead = scores(groups[-1])
    for g in reversed(groups):
        dpts = ahead
        slot = g % tmpq.shape[0]
        rows = group_rows(g)
        here = group_rows(g - groups.start)
        buffered = pair_rows(g - groups.start, heads)
        opened = lanes_iota(128) < known(table_ref, OPENED, g)
        head_part = lanes_iota(128) < known(table_ref, HEAD, g)
        kept = factor(table_ref, KEPT, g)
        for h in range(heads):
            mine = pl.ds(h, GROUP, stride=heads)
            dv_ref[here, at(h)] = dot(pt_ref[h, rows, :], turn(dobt_ref[at(h), rows]))
            tmpo[slot, mine, :] = normed_ref[at(h), rows].T.astype(F32)
        bufo[buffered, :] = tmpo[slot].astype(BF16)
        if g > groups.start:
            ahead = scores(g - 1)
        near, grown = [], []
        for h in range(heads):
            dobt = dobt_ref[at(h), rows]
            near.append(jnp.where(opened, dot(turn(sb_ref[g, h]), dobt), 0.0))
            grown.append(dot(keep_where(head_part, dobt), qd_ref[rows, at(h)]))
        for h in range(heads):
            mine = pl.ds(h, GROUP, stride=heads)
            dk_ref[here, at(h)] = dot(dpts[h], qd_ref[rows, at(h)])
            gq = dot(kt_ref[at(h), rows], dpts[h]) + near[h]
            tmpq[slot, mine, :] = turn(gq).astype(F32)
            rl_ref[g - groups.start, h] = state[h]
            state[h] = state[h] * kept + grown[h]
        bufq[buffered, :] = tmpq[slot].astype(BF16)
        for n, (buf, out) in enumerate(((bufo, out_ref), (bufq, gq_ref))):
            copy = pltpu.make_async_copy(
                buf.at[buffered], out.at[pair_rows(g, heads)], sems.at[n, g]
            )
            copy.start()
            started.append(copy)
    if left_ref is not None:
        for h in range(heads):
            left_ref[h] = state[h]
    for copy in started:
        copy.wait()


def final_kernel(table_ref, kd_ref, vd_ref, own_ref, other_ref, *refs):
    *parts, gk_ref, gv_ref, rin, tmpk, tmpv, bufk, bufv, sems = refs
    tokens, width = kd_ref.shape
    heads = width // 128
    n_groups = tokens // GROUP
    place_halves(lax.axis_index("seq") % 2, rin, own_ref, other_ref)
    held = []
    for dk_ref, dv_ref, rl_ref in zip(parts[0::3], parts[1::3], parts[2::3]):
        held += [(dk_ref, dv_ref, rl_ref, i) for i in range(rl_ref.shape[0])]

    def closing_terms(g):
        rows = group_rows(g)
        rl_ref, i = held[g][2:]
        closing = rows_iota(128) >= known(table_ref, CLOSING, g, 128)
        same = factor(table_ref, SAME_CLOSING, g)
        terms = []
        for h in range(heads):
            rb = (rl_ref[i, h] + same * rin[h]).astype(BF16)
            terms.append(
                (
                    jnp.where(closing, dot(vd_ref[rows, at(h)], rb), 0.0),
                    jnp.where(closing, dot(kd_ref[rows, at(h)], rb, NT), 0.0),
                )
            )
        return terms

    started = []
    ahead = closing_terms(0)
    for g in range(n_groups):
        terms = ahead
        if g + 1 < n_groups:
            ahead = closing_terms(g + 1)
        dk_ref, dv_ref, _, i = held[g]
        pairs = pair_rows(g, heads)
        slot = g % tmpk.shape[0]
        for h in range(heads):
            mine = pl.ds(h, GROUP, stride=heads)
            tmpk[slot, mine, :] = dk_ref[group_rows(i), at(h)] + terms[h][0]
            tmpv[slot, mine, :] = dv_ref[group_rows(i), at(h)] + terms[h][1]
        bufk[pairs, :] = tmpk[slot].astype(BF16)
        bufv[pairs, :] = tmpv[slot].astype(BF16)
        for n, (buf, out) in enumerate(((bufk, gk_ref), (bufv, gv_ref))):
            copy = pltpu.make_async_copy(buf.at[pairs], out.at[pairs], sems.at[n, g])
            copy.start()
            started.append(copy)
    for copy in started:
        copy.wait()


def call(kernel, name, outs, scratch, n_in, in_hbm=(), out_hbm=(), in_smem=(), alias=None, flops=0):
    vmem = pl.BlockSpec(memory_space=pltpu.VMEM)
    hbm = pl.BlockSpec(memory_space=pltpu.HBM)
    smem = pl.BlockSpec(memory_space=pltpu.SMEM)
    return pl.pallas_call(
        kernel,
        name=name,
        out_shape=[jax.ShapeDtypeStruct(s, d) for s, d in outs],
        in_specs=[hbm if i in in_hbm else smem if i in in_smem else vmem for i in range(n_in)],
        out_specs=[hbm if i in out_hbm else vmem for i in range(len(outs))],
        scratch_shapes=scratch,
        input_output_aliases=alias or {},
        cost_estimate=pl.CostEstimate(flops=flops, bytes_accessed=8 << 20, transcendentals=0),
        compiler_params=pltpu.CompilerParams(vmem_limit_bytes=16 << 20),
    )


def per_device(queries, keys, values, cotangent, doc_lengths):
    tokens, heads, head_width = queries.shape
    width = heads * head_width
    half = heads // 2
    n_groups = tokens // GROUP
    n_seq = lax.axis_size("seq")
    n_head = lax.axis_size("head")
    n_chips = n_seq // 2

    def pairs(x):
        return x.reshape(tokens * heads, head_width)

    q2, k2, v2, c2 = pairs(queries), pairs(keys), pairs(values), pairs(cotangent)
    full = (tokens, width)
    piece = (half, head_width, head_width)
    state_shape = (heads, head_width, head_width)
    flat = (tokens * heads, head_width)
    buf = pltpu.VMEM(flat, BF16)
    tmp = pltpu.VMEM((2, GROUP * heads, head_width), F32)
    sems = pltpu.SemaphoreType.DMA((2, n_groups))
    swap_pairs = [(i, i ^ 1) for i in range(n_seq)]

    def swap(x):
        return lax.ppermute(x, "seq", swap_pairs)

    def exchange(mine, send, weights, after):
        got = swap(send)
        chip_state, after = lax.optimization_barrier((weights[0] * mine + weights[1] * got, after))
        total = jnp.zeros(piece, F32)
        for k in range(1, n_chips):
            links = [(2 * i + c, 2 * j + c) for i, j in links_of(k, n_chips) for c in (0, 1)]
            total = total + weights[5 + k] * lax.ppermute(chip_state, "seq", links)
        return got, total, after

    def finish(mine, got, total, weights):
        return weights[2] * total + weights[3] * got, swap(weights[4] * total + weights[5] * mine)

    mm = 2 * tokens * heads * head_width * head_width
    table = ((5 + n_chips, 128), F32)
    state = pltpu.VMEM(state_shape, F32)
    table = ((5 + n_chips, 128), F32)
    turned = (width, tokens)
    group_states = (n_groups, heads, head_width, head_width)
    kd, vd, vt, mine, send, fore, back = call(
        functools.partial(state_kernel, n_seq),
        "shard_state",
        [(full, BF16), (full, BF16), (turned, BF16), (piece, F32), (piece, F32), table, table],
        [
            pltpu.SMEM(doc_lengths.shape, jnp.int32),
            buf,
            buf,
            tmp,
            tmp,
            state,
            sems,
            pltpu.SemaphoreType.DMA,
        ],
        n_in=3,
        in_hbm=(0, 1, 2),
        flops=mm,
    )(*(pltpu.with_memory_space_constraint(x, pltpu.HBM) for x in (doc_lengths, k2, v2)))
    got, total, (kd_b, vt_b, q2_b, c2_b) = exchange(mine, send, fore, (kd, vt, q2, c2))
    facts = (8, n_groups, GROUP)
    qd, qt, kt, ct, pt, o_local, sl, known_of = call(
        local_kernel,
        "local_mix",
        [
            (full, BF16),
            (turned, BF16),
            (turned, BF16),
            (turned, BF16),
            ((heads, tokens, GROUP), BF16),
            (turned, F32),
            (group_states, F32),
            (facts, jnp.int32),
        ],
        [tmp, tmp],
        n_in=5,
        in_smem=(0,),
        flops=6 * mm,
    )(doc_lengths, kd_b, vt_b, q2_b, c2_b)
    total, o_local = lax.optimization_barrier((total, o_local))
    own, other = finish(mine, got, total, fore)
    half_turned = (half * head_width, tokens)
    half_states = (n_groups, half, head_width, head_width)

    def part(is_own, states, before, name):
        return call(
            functools.partial(stats_kernel, is_own),
            name,
            [(half_turned, F32), (half_states, BF16), ((2, tokens), F32)],
            [],
            n_in=6 + len(before),
            flops=mm // 2,
        )(known_of, qt, o_local, ct, sl, states, *before)

    o_own, sb_own, stats = part(True, own, (), "mix_own")
    o_other, sb_other, stats = part(False, other, (stats,), "mix_other")
    stats = stats + sum(
        lax.ppermute(stats, "head", links_of(k, n_head)) for k in range(1, n_head)
    )
    dob_other, factors, send = call(
        functools.partial(norm_kernel, float(width * n_head)),
        "norm_other",
        [(half_turned, BF16), ((8, tokens), F32), (piece, F32)],
        [],
        n_in=5,
        flops=mm // 2,
    )(known_of, stats, o_other, ct, qd)
    dobt, normed, sb, mine = call(
        merge_kernel,
        "norm_own",
        [(turned, BF16), (turned, BF16), (group_states, BF16), (piece, F32)],
        [],
        n_in=9,
        flops=mm // 2,
    )(known_of, factors, o_own, o_other, ct, qd, dob_other, sb_own, sb_other)
    got, total, (dobt_b, normed_b) = exchange(mine, send, back, (dobt, normed))
    cut = max(1, n_groups // 4)
    earlier, later = range(0, cut), range(cut, n_groups)

    def grads(groups, name, before):
        count = len(groups)
        held = (count * GROUP, width)
        left = [(state_shape, F32)] if groups.start else []
        kept = [(held, F32), (held, F32), ((count, *state_shape), F32)]
        whole = len(left) + len(kept)
        return call(
            functools.partial(grad_kernel, groups),
            name,
            [*left, *kept, (flat, BF16), (flat, BF16)],
            [tmp, tmp, pltpu.VMEM((count * GROUP * heads, head_width), BF16)]
            + [pltpu.VMEM((count * GROUP * heads, head_width), BF16), sems],
            n_in=8 + len(before),
            in_hbm=(9, 10),
            out_hbm=(whole, whole + 1),
            alias={9: whole, 10: whole + 1} if before else None,
            flops=count * mm,
        )(known_of, normed_b, dobt_b, pt, qd, kt, vd, sb, *before)

    left, dk1, dv1, rl1, output, grad_q = grads(later, "grads_later", ())
    total, left = lax.optimization_barrier((total, left))
    own, other = finish(mine, got, total, back)
    dk0, dv0, rl0, output, grad_q = grads(earlier, "grads_earlier", (left, output, grad_q))
    grad_k, grad_v = call(
        final_kernel,
        "final_grads",
        [(flat, BF16), (flat, BF16)],
        [state, tmp, tmp, buf, buf, sems],
        n_in=11,
        out_hbm=(0, 1),
        flops=2 * mm,
    )(known_of, kd, vd, own, other, dk0, dv0, rl0, dk1, dv1, rl1)
    return tuple(x.reshape(queries.shape) for x in (output, grad_q, grad_k, grad_v))


def solution(mesh):
    spec = P("seq", "head", None)
    return jax.shard_map(
        per_device,
        mesh=mesh,
        in_specs=(spec, spec, spec, spec, P()),
        out_specs=(spec, spec, spec, spec),
        check_vma=False,
    )
```

```python
import functools

import jax
import jax.numpy as jnp
from jax import lax
from jax.experimental import pallas as pl
from jax.experimental.pallas import tpu as pltpu
from jax.sharding import PartitionSpec as P

GROUP = 256
EPSILON = 1e-06
OPENED, SAME_OPENED, HEAD, KEPT, SHARD_HEAD, CLOSING, SAME_CLOSING, BEGIN = range(8)
F32 = jnp.float32
BF16 = jnp.bfloat16

NN = (((1,), (0,)), ((), ()))
NT = (((1,), (1,)), ((), ()))
TN = (((0,), (0,)), ((), ()))


def dot(a, b, dims=NN):
    return lax.dot_general(a, b, dims, preferred_element_type=F32)


def doc_ends_of(doc_ref):
    ends, total = [], jnp.int32(0)
    for j in range(doc_ref.shape[0]):
        total = total + doc_ref[j]
        ends.append(total)
    return ends


def start_of(ends, place):
    found = jnp.int32(0)
    for end in ends:
        found = jnp.where(end <= place, end, found)
    return found


def end_of(ends, place):
    found = jnp.int32(2**30)
    for end in reversed(ends):
        found = jnp.where(end > place, end, found)
    return found


def rows_iota(width):
    return lax.broadcasted_iota(jnp.int32, (GROUP, width), 0)


def lanes_iota(rows):
    return lax.broadcasted_iota(jnp.int32, (rows, GROUP), 1)


def begin_row(ends, first):
    place = lanes_iota(8) + first
    begin = jnp.zeros((8, GROUP), jnp.int32)
    for end in ends:
        begin = jnp.where(place >= end, end, begin)
    return begin - first


def group_mask(begin):
    row = rows_iota(GROUP)
    return (row >= begin) & (row <= lanes_iota(GROUP))


def write_table(table_ref, ends, anchor, tokens):
    for g in range(tokens // GROUP):
        first = anchor + g * GROUP
        after = first + GROUP
        numbers = {
            OPENED: end_of(ends, first - 1) - first,
            SAME_OPENED: (start_of(ends, first - 1) < anchor).astype(jnp.int32),
            HEAD: end_of(ends, first) - first,
            KEPT: (end_of(ends, first) > after).astype(jnp.int32),
            SHARD_HEAD: end_of(ends, anchor) - first,
            CLOSING: start_of(ends, after) - first,
            SAME_CLOSING: (end_of(ends, after) > anchor + tokens).astype(jnp.int32),
        }
        for kind, number in numbers.items():
            table_ref[kind, pl.ds(g, 1), :] = jnp.full((1, GROUP), number, jnp.int32)
        table_ref[BEGIN, pl.ds(g, 1), :] = begin_row(ends, first)[:1]


def known(table_ref, kind, g, width=GROUP):
    return table_ref[kind, pl.ds(g, 1), :width]


def factor(table_ref, kind, g):
    return known(table_ref, kind, g, 128).astype(F32)


def keep_where(keep, x):
    return jnp.where(keep, x.astype(F32), 0.0).astype(BF16)


def at(h):
    return slice(h * 128, (h + 1) * 128)


def turn(x):
    return x.astype(BF16).T


def pair_rows(g, heads):
    return pl.ds(pl.multiple_of(g * (GROUP * heads), GROUP * heads), GROUP * heads)


def split_heads(buf_ref, tmp_ref, g, heads):
    slot = g % tmp_ref.shape[0]
    tmp_ref[slot] = buf_ref[pair_rows(g, heads), :].astype(F32)
    return [tmp_ref[slot, pl.ds(h, GROUP, stride=heads), :] for h in range(heads)]


def group_rows(g):
    return pl.ds(pl.multiple_of(g * GROUP, GROUP), GROUP)


def source_of(index, step, size):
    if size & (size - 1):
        return (index + size - step) % size
    return index ^ step


def links_of(step, size):
    return [(source_of(i, step, size), i) for i in range(size)]


def weights_of(out_ref, ends, shard, tokens, n_seq, sign):
    core = shard % 2
    chip = shard // 2
    n_chips = n_seq // 2
    others = [source_of(chip, k, n_chips) for k in range(1, n_chips)]
    chip_first = (shard - core) * tokens
    middle = chip_first + tokens
    chip_end = middle + tokens
    if sign > 0:
        join = start_of(ends, chip_end - 1) < middle
        onward = start_of(ends, middle - 1) < chip_first
        begin = start_of(ends, chip_first - 1)
        same = [(other < chip) & (begin < (other + 1) * (2 * tokens)) for other in others]
        is_near = core == 0
    else:
        join = end_of(ends, chip_first) > middle
        onward = end_of(ends, middle) > chip_end
        end = end_of(ends, chip_end)
        same = [(other > chip) & (end > other * (2 * tokens)) for other in others]
        is_near = core == 1
    join, onward, is_near = (x.astype(F32) for x in (join, onward, is_near))
    far = 1.0 - is_near
    table = [
        is_near * join + far,
        is_near + far * join,
        is_near + far * onward,
        far,
        is_near * onward + far,
        is_near,
    ] + [x.astype(F32) for x in same]
    for i, x in enumerate(table):
        out_ref[pl.ds(i, 1), :] = jnp.full((1, 128), x, F32)


def state_kernel(
    n_seq, doc_hbm, k2_ref, v2_ref, kd_ref, vd_ref, vt_ref, mine_ref, send_ref, fore_ref, back_ref,
    doc_ref, bufk, bufv, tmpk, tmpv, acc, sems, doc_sem,
):
    tokens, width = kd_ref.shape
    heads = width // 128
    half = heads // 2
    n_groups = tokens // GROUP

    sizes = [max(1, n_groups // 6), max(1, n_groups // 3)]
    sizes = [*sizes, n_groups - sum(sizes)] if n_groups > 2 else [1] * n_groups
    chunks = {sum(sizes[:i]): size for i, size in enumerate(sizes)}

    def fetches(g):
        if g not in chunks:
            return ()
        rows = pl.ds(g * GROUP * heads, chunks[g] * GROUP * heads)
        return (
            pltpu.make_async_copy(k2_ref.at[rows], bufk.at[rows], sems.at[0, g]),
            pltpu.make_async_copy(v2_ref.at[rows], bufv.at[rows], sems.at[1, g]),
        )

    doc_copy = pltpu.make_async_copy(doc_hbm, doc_ref, doc_sem)
    doc_copy.start()
    for g in range(n_groups):
        for copy in fetches(g):
            copy.start()
    doc_copy.wait()
    shard = lax.axis_index("seq")
    core = shard % 2
    anchor = shard * tokens
    ends = doc_ends_of(doc_ref)
    weights_of(fore_ref, ends, shard, tokens, n_seq, 1)
    weights_of(back_ref, ends, shard, tokens, n_seq, -1)
    tail = start_of(ends, anchor + tokens - 1) - anchor

    def prepare(g):
        for copy in fetches(g):
            copy.wait()
        rows = group_rows(g)
        keep = rows_iota(128) + g * GROUP >= tail
        ks = split_heads(bufk, tmpk, g, heads)
        vs = split_heads(bufv, tmpv, g, heads)
        ready = []
        for h in range(heads):
            vt = turn(vs[h])
            kd_ref[rows, at(h)] = ks[h].astype(BF16)
            vd_ref[rows, at(h)] = vs[h].astype(BF16)
            vt_ref[at(h), rows] = vt
            ready.append((vt, jnp.where(keep, ks[h], 0.0).astype(BF16)))
        return ready

    total = [jnp.zeros((128, 128), F32) for _ in range(heads)]
    ahead = prepare(0)
    for g in range(n_groups):
        ready = ahead
        if g + 1 < n_groups:
            ahead = prepare(g + 1)
        total = [t + dot(vt, k) for t, (vt, k) in zip(total, ready)]
    for h in range(heads):
        acc[h] = total[h]
    mine_ref[...] = acc[pl.ds(core * half, half)]
    send_ref[...] = acc[pl.ds((1 - core) * half, half)]


def local_kernel(
    doc_ref, kd_ref, vt_ref, q2_ref, c2_ref, qd_ref, qt_ref, kt_ref, ct_ref, pt_ref, ol_ref, sl_ref, table_ref,
    tmpq, tmpc,
):
    tokens, width = kd_ref.shape
    heads = width // 128
    n_groups = tokens // GROUP
    anchor = lax.axis_index("seq") * tokens
    ends = doc_ends_of(doc_ref)

    def prepare(g):
        rows = group_rows(g)
        qs = split_heads(q2_ref, tmpq, g, heads)
        cs = split_heads(c2_ref, tmpc, g, heads)
        qts = []
        for h in range(heads):
            qt = turn(qs[h])
            qd_ref[rows, at(h)] = qs[h].astype(BF16)
            qt_ref[at(h), rows] = qt
            kt_ref[at(h), rows] = turn(kd_ref[rows, at(h)])
            ct_ref[at(h), rows] = turn(cs[h])
            qts.append(qt)
        return qts

    def scores(g, qts):
        rows = group_rows(g)
        mask = group_mask(known(table_ref, BEGIN, g))
        pts = []
        for h in range(heads):
            pt = jnp.where(mask, dot(kd_ref[rows, at(h)], qts[h]), 0.0).astype(BF16)
            pt_ref[h, rows, :] = pt
            pts.append(pt)
        return pts

    write_table(table_ref, ends, anchor, tokens)
    state = [jnp.zeros((128, 128), F32) for _ in range(heads)]
    next_pts = scores(0, prepare(0))
    next_qts = prepare(1) if n_groups > 1 else None
    for g in range(n_groups):
        pts = next_pts
        if g + 1 < n_groups:
            next_pts = scores(g + 1, next_qts)
        if g + 2 < n_groups:
            next_qts = prepare(g + 2)
        first = anchor + g * GROUP
        rows = group_rows(g)
        begin = start_of(ends, first + GROUP - 1)
        tail = rows_iota(128) >= begin - first
        kept = (begin < first).astype(F32)
        for h in range(heads):
            vt = vt_ref[at(h), rows]
            sl_ref[g, h] = state[h]
            state[h] = state[h] * kept + dot(vt, keep_where(tail, kd_ref[rows, at(h)]))
            ol_ref[at(h), rows] = dot(vt, pts[h])


def place_halves(core, out_ref, own_ref, other_ref):
    half = own_ref.shape[0]
    out_ref[pl.ds(core * half, half)] = own_ref[...]
    out_ref[pl.ds((1 - core) * half, half)] = other_ref[...]


def part_of(core, own, half):
    return (core if own else 1 - core) * half


def head_rows(head):
    return pl.ds(pl.multiple_of(head * 128, 128), 128)


def stats_kernel(own, table_ref, qt_ref, ol_ref, ct_ref, sl_ref, state_ref, *refs):
    (before_ref, o_ref, sb_ref, st_ref) = refs if len(refs) == 4 else (None, *refs)
    width, tokens = qt_ref.shape
    half = state_ref.shape[0]
    n_groups = tokens // GROUP
    base = part_of(lax.axis_index("seq") % 2, own, half)

    def opened_terms(g):
        rows = group_rows(g)
        opened = lanes_iota(128) < known(table_ref, OPENED, g)
        same = factor(table_ref, SAME_OPENED, g)
        terms = []
        for h in range(half):
            sb = (sl_ref[g, base + h] + same * state_ref[h]).astype(BF16)
            sb_ref[g, h] = sb
            terms.append(jnp.where(opened, dot(sb, qt_ref[head_rows(base + h), rows]), 0.0))
        return terms

    ahead = opened_terms(0)
    for g in range(n_groups):
        terms = ahead
        if g + 1 < n_groups:
            ahead = opened_terms(g + 1)
        rows = group_rows(g)
        squares = jnp.zeros((1, GROUP), F32)
        inner = jnp.zeros((1, GROUP), F32)
        for h in range(half):
            o = ol_ref[head_rows(base + h), rows] + terms[h]
            o_ref[at(h), rows] = o
            squares += jnp.sum(o * o, axis=0, keepdims=True)
            inner += jnp.sum(o * ct_ref[head_rows(base + h), rows].astype(F32), axis=0, keepdims=True)
        both = jnp.concatenate([squares, inner], axis=0)
        st_ref[:, rows] = both if before_ref is None else both + before_ref[:, rows]


def back_state(half, n_groups, prepare, qd_ref, base, out_ref):
    total = [jnp.zeros((128, 128), F32) for _ in range(half)]
    ahead = prepare(0)
    for g in range(n_groups):
        ready = ahead
        if g + 1 < n_groups:
            ahead = prepare(g + 1)
        total = [
            total[h] + dot(ready[h], qd_ref[group_rows(g), head_rows(base + h)]) for h in range(half)
        ]
    for h in range(half):
        out_ref[h] = total[h]


def norm_kernel(
    width_all, table_ref, st_ref, o_ref, ct_ref, qd_ref, dobt_ref, rows_ref, send_ref
):
    tokens, width = qd_ref.shape
    half = send_ref.shape[0]
    base = part_of(lax.axis_index("seq") % 2, False, half)

    def prepare(g):
        rows = group_rows(g)
        keep = lanes_iota(128) < known(table_ref, SHARD_HEAD, g)
        total = st_ref[:, rows] * (1.0 / width_all)
        inv = lax.rsqrt(total[0:1] + EPSILON)
        slope = total[1:2] * inv * inv * inv
        rows_ref[:, rows] = jnp.concatenate([inv, slope] * 4, axis=0)
        ready = []
        for h in range(half):
            dob = inv * ct_ref[head_rows(base + h), rows].astype(F32) - slope * o_ref[at(h), rows]
            dobt_ref[at(h), rows] = dob.astype(BF16)
            ready.append(jnp.where(keep, dob, 0.0).astype(BF16))
        return ready

    back_state(half, tokens // GROUP, prepare, qd_ref, base, send_ref)


def merge_kernel(
    table_ref, rows_ref, own_ref, other_ref, ct_ref, qd_ref, dob_other_ref, sb_own_ref, sb_other_ref,
    dobt_ref, normed_ref, sb_ref, mine_ref,
):
    tokens, width = qd_ref.shape
    half = mine_ref.shape[0]
    core = lax.axis_index("seq") % 2
    base, far = part_of(core, True, half), part_of(core, False, half)

    def prepare(g):
        rows = group_rows(g)
        keep = lanes_iota(128) < known(table_ref, SHARD_HEAD, g)
        inv = rows_ref[0:1, rows]
        slope = rows_ref[1:2, rows]
        ready = []
        for h in range(half):
            mine, others = head_rows(base + h), head_rows(far + h)
            o = own_ref[at(h), rows]
            dob = inv * ct_ref[mine, rows].astype(F32) - slope * o
            dobt_ref[mine, rows] = dob.astype(BF16)
            dobt_ref[others, rows] = dob_other_ref[at(h), rows]
            normed_ref[mine, rows] = (o * inv).astype(BF16)
            normed_ref[others, rows] = (other_ref[at(h), rows] * inv).astype(BF16)
            sb_ref[g, base + h] = sb_own_ref[g, h]
            sb_ref[g, far + h] = sb_other_ref[g, h]
            ready.append(jnp.where(keep, dob, 0.0).astype(BF16))
        return ready

    back_state(half, tokens // GROUP, prepare, qd_ref, base, mine_ref)


def grad_kernel(groups, *refs):
    table_ref, normed_ref, dobt_ref, pt_ref, qd_ref, kt_ref, vd_ref, sb_ref, *refs = refs
    width = dobt_ref.shape[0]
    heads = width // 128
    n_groups = dobt_ref.shape[1] // GROUP
    state = [jnp.zeros((128, 128), F32) for _ in range(heads)]
    if groups.stop < n_groups:
        state_ref, _, _, *refs = refs
        state = [state_ref[h] for h in range(heads)]
    left_ref = None
    if groups.start > 0:
        left_ref, *refs = refs
    dk_ref, dv_ref, rl_ref, out_ref, gq_ref, tmpo, tmpq, bufo, bufq, sems = refs

    def scores(g):
        rows = group_rows(g)
        mask = group_mask(known(table_ref, BEGIN, g))
        return [
            jnp.where(mask, dot(vd_ref[rows, at(h)], dobt_ref[at(h), rows]), 0.0).astype(BF16)
            for h in range(heads)
        ]

    started = []
    ahead = scores(groups[-1])
    for g in reversed(groups):
        dpts = ahead
        slot = g % tmpq.shape[0]
        rows = group_rows(g)
        here = group_rows(g - groups.start)
        buffered = pair_rows(g - groups.start, heads)
        opened = lanes_iota(128) < known(table_ref, OPENED, g)
        head_part = lanes_iota(128) < known(table_ref, HEAD, g)
        kept = factor(table_ref, KEPT, g)
        for h in range(heads):
            mine = pl.ds(h, GROUP, stride=heads)
            dv_ref[here, at(h)] = dot(pt_ref[h, rows, :], turn(dobt_ref[at(h), rows]))
            tmpo[slot, mine, :] = normed_ref[at(h), rows].T.astype(F32)
        bufo[buffered, :] = tmpo[slot].astype(BF16)
        if g > groups.start:
            ahead = scores(g - 1)
        near, grown = [], []
        for h in range(heads):
            dobt = dobt_ref[at(h), rows]
            near.append(jnp.where(opened, dot(turn(sb_ref[g, h]), dobt), 0.0))
            grown.append(dot(keep_where(head_part, dobt), qd_ref[rows, at(h)]))
        for h in range(heads):
            mine = pl.ds(h, GROUP, stride=heads)
            dk_ref[here, at(h)] = dot(dpts[h], qd_ref[rows, at(h)])
            gq = dot(kt_ref[at(h), rows], dpts[h]) + near[h]
            tmpq[slot, mine, :] = turn(gq).astype(F32)
            rl_ref[g - groups.start, h] = state[h]
            state[h] = state[h] * kept + grown[h]
        bufq[buffered, :] = tmpq[slot].astype(BF16)
        for n, (buf, out) in enumerate(((bufo, out_ref), (bufq, gq_ref))):
            copy = pltpu.make_async_copy(
                buf.at[buffered], out.at[pair_rows(g, heads)], sems.at[n, g]
            )
            copy.start()
            started.append(copy)
    if left_ref is not None:
        for h in range(heads):
            left_ref[h] = state[h]
    for copy in started:
        copy.wait()


def final_kernel(table_ref, kd_ref, vd_ref, own_ref, other_ref, *refs):
    *parts, gk_ref, gv_ref, rin, tmpk, tmpv, bufk, bufv, sems = refs
    tokens, width = kd_ref.shape
    heads = width // 128
    n_groups = tokens // GROUP
    place_halves(lax.axis_index("seq") % 2, rin, own_ref, other_ref)
    held = []
    for dk_ref, dv_ref, rl_ref in zip(parts[0::3], parts[1::3], parts[2::3]):
        held += [(dk_ref, dv_ref, rl_ref, i) for i in range(rl_ref.shape[0])]

    def closing_terms(g):
        rows = group_rows(g)
        rl_ref, i = held[g][2:]
        closing = rows_iota(128) >= known(table_ref, CLOSING, g, 128)
        same = factor(table_ref, SAME_CLOSING, g)
        terms = []
        for h in range(heads):
            rb = (rl_ref[i, h] + same * rin[h]).astype(BF16)
            terms.append(
                (
                    jnp.where(closing, dot(vd_ref[rows, at(h)], rb), 0.0),
                    jnp.where(closing, dot(kd_ref[rows, at(h)], rb, NT), 0.0),
                )
            )
        return terms

    started = []
    ahead = closing_terms(0)
    for g in range(n_groups):
        terms = ahead
        if g + 1 < n_groups:
            ahead = closing_terms(g + 1)
        dk_ref, dv_ref, _, i = held[g]
        pairs = pair_rows(g, heads)
        slot = g % tmpk.shape[0]
        for h in range(heads):
            mine = pl.ds(h, GROUP, stride=heads)
            tmpk[slot, mine, :] = dk_ref[group_rows(i), at(h)] + terms[h][0]
            tmpv[slot, mine, :] = dv_ref[group_rows(i), at(h)] + terms[h][1]
        bufk[pairs, :] = tmpk[slot].astype(BF16)
        bufv[pairs, :] = tmpv[slot].astype(BF16)
        for n, (buf, out) in enumerate(((bufk, gk_ref), (bufv, gv_ref))):
            copy = pltpu.make_async_copy(buf.at[pairs], out.at[pairs], sems.at[n, g])
            copy.start()
            started.append(copy)
    for copy in started:
        copy.wait()


def call(kernel, name, outs, scratch, n_in, in_hbm=(), out_hbm=(), in_smem=(), alias=None, flops=0):
    vmem = pl.BlockSpec(memory_space=pltpu.VMEM)
    hbm = pl.BlockSpec(memory_space=pltpu.HBM)
    smem = pl.BlockSpec(memory_space=pltpu.SMEM)
    return pl.pallas_call(
        kernel,
        name=name,
        out_shape=[jax.ShapeDtypeStruct(s, d) for s, d in outs],
        in_specs=[hbm if i in in_hbm else smem if i in in_smem else vmem for i in range(n_in)],
        out_specs=[hbm if i in out_hbm else vmem for i in range(len(outs))],
        scratch_shapes=scratch,
        input_output_aliases=alias or {},
        cost_estimate=pl.CostEstimate(flops=flops, bytes_accessed=8 << 20, transcendentals=0),
        compiler_params=pltpu.CompilerParams(vmem_limit_bytes=16 << 20),
    )


def per_device(queries, keys, values, cotangent, doc_lengths):
    tokens, heads, head_width = queries.shape
    width = heads * head_width
    half = heads // 2
    n_groups = tokens // GROUP
    n_seq = lax.axis_size("seq")
    n_head = lax.axis_size("head")
    n_chips = n_seq // 2

    def pairs(x):
        return x.reshape(tokens * heads, head_width)

    q2, k2, v2, c2 = pairs(queries), pairs(keys), pairs(values), pairs(cotangent)
    full = (tokens, width)
    piece = (half, head_width, head_width)
    state_shape = (heads, head_width, head_width)
    flat = (tokens * heads, head_width)
    buf = pltpu.VMEM(flat, BF16)
    tmp = pltpu.VMEM((2, GROUP * heads, head_width), F32)
    sems = pltpu.SemaphoreType.DMA((2, n_groups))
    swap_pairs = [(i, i ^ 1) for i in range(n_seq)]

    def swap(x):
        return lax.ppermute(x, "seq", swap_pairs)

    def exchange(mine, send, weights, after):
        got = swap(send)
        chip_state, after = lax.optimization_barrier((weights[0] * mine + weights[1] * got, after))
        total = jnp.zeros(piece, F32)
        for k in range(1, n_chips):
            links = [(2 * i + c, 2 * j + c) for i, j in links_of(k, n_chips) for c in (0, 1)]
            total = total + weights[5 + k] * lax.ppermute(chip_state, "seq", links)
        return got, total, after

    def finish(mine, got, total, weights):
        return weights[2] * total + weights[3] * got, swap(weights[4] * total + weights[5] * mine)

    mm = 2 * tokens * heads * head_width * head_width
    table = ((5 + n_chips, 128), F32)
    state = pltpu.VMEM(state_shape, F32)
    table = ((5 + n_chips, 128), F32)
    turned = (width, tokens)
    group_states = (n_groups, heads, head_width, head_width)
    kd, vd, vt, mine, send, fore, back = call(
        functools.partial(state_kernel, n_seq),
        "shard_state",
        [(full, BF16), (full, BF16), (turned, BF16), (piece, F32), (piece, F32), table, table],
        [
            pltpu.SMEM(doc_lengths.shape, jnp.int32),
            buf,
            buf,
            tmp,
            tmp,
            state,
            sems,
            pltpu.SemaphoreType.DMA,
        ],
        n_in=3,
        in_hbm=(0, 1, 2),
        flops=mm,
    )(*(pltpu.with_memory_space_constraint(x, pltpu.HBM) for x in (doc_lengths, k2, v2)))
    got, total, (kd_b, vt_b, q2_b, c2_b) = exchange(mine, send, fore, (kd, vt, q2, c2))
    facts = (8, n_groups, GROUP)
    qd, qt, kt, ct, pt, o_local, sl, known_of = call(
        local_kernel,
        "local_mix",
        [
            (full, BF16),
            (turned, BF16),
            (turned, BF16),
            (turned, BF16),
            ((heads, tokens, GROUP), BF16),
            (turned, F32),
            (group_states, F32),
            (facts, jnp.int32),
        ],
        [tmp, tmp],
        n_in=5,
        in_smem=(0,),
        flops=6 * mm,
    )(doc_lengths, kd_b, vt_b, q2_b, c2_b)
    total, o_local = lax.optimization_barrier((total, o_local))
    own, other = finish(mine, got, total, fore)
    half_turned = (half * head_width, tokens)
    half_states = (n_groups, half, head_width, head_width)

    def part(is_own, states, before, name):
        return call(
            functools.partial(stats_kernel, is_own),
            name,
            [(half_turned, F32), (half_states, BF16), ((2, tokens), F32)],
            [],
            n_in=6 + len(before),
            flops=mm // 2,
        )(known_of, qt, o_local, ct, sl, states, *before)

    o_own, sb_own, stats = part(True, own, (), "mix_own")
    o_other, sb_other, stats = part(False, other, (stats,), "mix_other")
    stats = stats + sum(
        lax.ppermute(stats, "head", links_of(k, n_head)) for k in range(1, n_head)
    )
    dob_other, factors, send = call(
        functools.partial(norm_kernel, float(width * n_head)),
        "norm_other",
        [(half_turned, BF16), ((8, tokens), F32), (piece, F32)],
        [],
        n_in=5,
        flops=mm // 2,
    )(known_of, stats, o_other, ct, qd)
    dobt, normed, sb, mine = call(
        merge_kernel,
        "norm_own",
        [(turned, BF16), (turned, BF16), (group_states, BF16), (piece, F32)],
        [],
        n_in=9,
        flops=mm // 2,
    )(known_of, factors, o_own, o_other, ct, qd, dob_other, sb_own, sb_other)
    got, total, (dobt_b, normed_b) = exchange(mine, send, back, (dobt, normed))
    cut = max(1, n_groups // 4)
    earlier, later = range(0, cut), range(cut, n_groups)

    def grads(groups, name, before):
        count = len(groups)
        held = (count * GROUP, width)
        left = [(state_shape, F32)] if groups.start else []
        kept = [(held, F32), (held, F32), ((count, *state_shape), F32)]
        whole = len(left) + len(kept)
        return call(
            functools.partial(grad_kernel, groups),
            name,
            [*left, *kept, (flat, BF16), (flat, BF16)],
            [tmp, tmp, pltpu.VMEM((count * GROUP * heads, head_width), BF16)]
            + [pltpu.VMEM((count * GROUP * heads, head_width), BF16), sems],
            n_in=8 + len(before),
            in_hbm=(9, 10),
            out_hbm=(whole, whole + 1),
            alias={9: whole, 10: whole + 1} if before else None,
            flops=count * mm,
        )(known_of, normed_b, dobt_b, pt, qd, kt, vd, sb, *before)

    left, dk1, dv1, rl1, output, grad_q = grads(later, "grads_later", ())
    total, left = lax.optimization_barrier((total, left))
    own, other = finish(mine, got, total, back)
    dk0, dv0, rl0, output, grad_q = grads(earlier, "grads_earlier", (left, output, grad_q))
    grad_k, grad_v = call(
        final_kernel,
        "final_grads",
        [(flat, BF16), (flat, BF16)],
        [state, tmp, tmp, buf, buf, sems],
        n_in=11,
        out_hbm=(0, 1),
        flops=2 * mm,
    )(known_of, kd, vd, own, other, dk0, dv0, rl0, dk1, dv1, rl1)
    return tuple(x.reshape(queries.shape) for x in (output, grad_q, grad_k, grad_v))


def solution(mesh):
    spec = P("seq", "head", None)
    return jax.shard_map(
        per_device,
        mesh=mesh,
        in_specs=(spec, spec, spec, spec, P()),
        out_specs=(spec, spec, spec, spec),
        check_vma=False,
    )
```

```python
import functools

import jax
import jax.numpy as jnp
from jax import lax
from jax.experimental import pallas as pl
from jax.experimental.pallas import tpu as pltpu
from jax.sharding import PartitionSpec as P

GROUP = 256
EPSILON = 1e-06
OPENED, SAME_OPENED, HEAD, KEPT, SHARD_HEAD, CLOSING, SAME_CLOSING, BEGIN = range(8)
F32 = jnp.float32
BF16 = jnp.bfloat16

NN = (((1,), (0,)), ((), ()))
NT = (((1,), (1,)), ((), ()))
TN = (((0,), (0,)), ((), ()))


def dot(a, b, dims=NN):
    return lax.dot_general(a, b, dims, preferred_element_type=F32)


def doc_ends_of(doc_ref):
    ends, total = [], jnp.int32(0)
    for j in range(doc_ref.shape[0]):
        total = total + doc_ref[j]
        ends.append(total)
    return ends


def start_of(ends, place):
    found = jnp.int32(0)
    for end in ends:
        found = jnp.where(end <= place, end, found)
    return found


def end_of(ends, place):
    found = jnp.int32(2**30)
    for end in reversed(ends):
        found = jnp.where(end > place, end, found)
    return found


def rows_iota(width):
    return lax.broadcasted_iota(jnp.int32, (GROUP, width), 0)


def lanes_iota(rows):
    return lax.broadcasted_iota(jnp.int32, (rows, GROUP), 1)


def begin_row(ends, first):
    place = lanes_iota(8) + first
    begin = jnp.zeros((8, GROUP), jnp.int32)
    for end in ends:
        begin = jnp.where(place >= end, end, begin)
    return begin - first


def group_mask(begin):
    row = rows_iota(GROUP)
    return (row >= begin) & (row <= lanes_iota(GROUP))


def write_table(table_ref, ends, anchor, tokens):
    for g in range(tokens // GROUP):
        first = anchor + g * GROUP
        after = first + GROUP
        numbers = {
            OPENED: end_of(ends, first - 1) - first,
            SAME_OPENED: (start_of(ends, first - 1) < anchor).astype(jnp.int32),
            HEAD: end_of(ends, first) - first,
            KEPT: (end_of(ends, first) > after).astype(jnp.int32),
            SHARD_HEAD: end_of(ends, anchor) - first,
            CLOSING: start_of(ends, after) - first,
            SAME_CLOSING: (end_of(ends, after) > anchor + tokens).astype(jnp.int32),
        }
        for kind, number in numbers.items():
            table_ref[kind, pl.ds(g, 1), :] = jnp.full((1, GROUP), number, jnp.int32)
        table_ref[BEGIN, pl.ds(g, 1), :] = begin_row(ends, first)[:1]


def known(table_ref, kind, g, width=GROUP):
    return table_ref[kind, pl.ds(g, 1), :width]


def factor(table_ref, kind, g):
    return known(table_ref, kind, g, 128).astype(F32)


def keep_where(keep, x):
    return jnp.where(keep, x.astype(F32), 0.0).astype(BF16)


def at(h):
    return slice(h * 128, (h + 1) * 128)


def turn(x):
    return x.astype(BF16).T


def pair_rows(g, heads):
    return pl.ds(pl.multiple_of(g * (GROUP * heads), GROUP * heads), GROUP * heads)


def split_heads(buf_ref, tmp_ref, g, heads):
    slot = g % tmp_ref.shape[0]
    tmp_ref[slot] = buf_ref[pair_rows(g, heads), :].astype(F32)
    return [tmp_ref[slot, pl.ds(h, GROUP, stride=heads), :] for h in range(heads)]


def group_rows(g):
    return pl.ds(pl.multiple_of(g * GROUP, GROUP), GROUP)


def source_of(index, step, size):
    if size & (size - 1):
        return (index + size - step) % size
    return index ^ step


def links_of(step, size):
    return [(source_of(i, step, size), i) for i in range(size)]


def weights_of(out_ref, ends, shard, tokens, n_seq, sign):
    core = shard % 2
    chip = shard // 2
    n_chips = n_seq // 2
    others = [source_of(chip, k, n_chips) for k in range(1, n_chips)]
    chip_first = (shard - core) * tokens
    middle = chip_first + tokens
    chip_end = middle + tokens
    if sign > 0:
        join = start_of(ends, chip_end - 1) < middle
        onward = start_of(ends, middle - 1) < chip_first
        begin = start_of(ends, chip_first - 1)
        same = [(other < chip) & (begin < (other + 1) * (2 * tokens)) for other in others]
        is_near = core == 0
    else:
        join = end_of(ends, chip_first) > middle
        onward = end_of(ends, middle) > chip_end
        end = end_of(ends, chip_end)
        same = [(other > chip) & (end > other * (2 * tokens)) for other in others]
        is_near = core == 1
    join, onward, is_near = (x.astype(F32) for x in (join, onward, is_near))
    far = 1.0 - is_near
    table = [
        is_near * join + far,
        is_near + far * join,
        is_near + far * onward,
        far,
        is_near * onward + far,
        is_near,
    ] + [x.astype(F32) for x in same]
    for i, x in enumerate(table):
        out_ref[pl.ds(i, 1), :] = jnp.full((1, 128), x, F32)


def state_kernel(
    n_seq, doc_hbm, k2_ref, v2_ref, bufk, bufv, vt_ref, mine_ref, send_ref, fore_ref, back_ref,
    doc_ref, tmpk, tmpv, acc, sems, doc_sem,
):
    width, tokens = vt_ref.shape
    heads = width // 128
    half = heads // 2
    n_groups = tokens // GROUP

    sizes = [max(1, n_groups // 6), max(1, n_groups // 3)]
    sizes = [*sizes, n_groups - sum(sizes)] if n_groups > 2 else [1] * n_groups
    chunks = {sum(sizes[:i]): size for i, size in enumerate(sizes)}

    def fetches(g):
        if g not in chunks:
            return ()
        rows = pl.ds(g * GROUP * heads, chunks[g] * GROUP * heads)
        return (
            pltpu.make_async_copy(k2_ref.at[rows], bufk.at[rows], sems.at[0, g]),
            pltpu.make_async_copy(v2_ref.at[rows], bufv.at[rows], sems.at[1, g]),
        )

    doc_copy = pltpu.make_async_copy(doc_hbm, doc_ref, doc_sem)
    doc_copy.start()
    for g in range(n_groups):
        for copy in fetches(g):
            copy.start()
    doc_copy.wait()
    shard = lax.axis_index("seq")
    core = shard % 2
    anchor = shard * tokens
    ends = doc_ends_of(doc_ref)
    weights_of(fore_ref, ends, shard, tokens, n_seq, 1)
    weights_of(back_ref, ends, shard, tokens, n_seq, -1)
    tail = start_of(ends, anchor + tokens - 1) - anchor

    def prepare(g):
        for copy in fetches(g):
            copy.wait()
        rows = group_rows(g)
        keep = rows_iota(128) + g * GROUP >= tail
        ks = split_heads(bufk, tmpk, g, heads)
        vs = split_heads(bufv, tmpv, g, heads)
        ready = []
        for h in range(heads):
            vt = turn(vs[h])
            vt_ref[at(h), rows] = vt
            ready.append((vt, jnp.where(keep, ks[h], 0.0).astype(BF16)))
        return ready

    total = [jnp.zeros((128, 128), F32) for _ in range(heads)]
    ahead = prepare(0)
    for g in range(n_groups):
        ready = ahead
        if g + 1 < n_groups:
            ahead = prepare(g + 1)
        total = [t + dot(vt, k) for t, (vt, k) in zip(total, ready)]
    for h in range(heads):
        acc[h] = total[h]
    mine_ref[...] = acc[pl.ds(core * half, half)]
    send_ref[...] = acc[pl.ds((1 - core) * half, half)]


def split_kernel(pairs_ref, out_ref, tmp):
    tokens, width = out_ref.shape
    heads = width // 128
    for g in range(tokens // GROUP):
        parts = split_heads(pairs_ref, tmp, g, heads)
        for h in range(heads):
            out_ref[group_rows(g), at(h)] = parts[h].astype(BF16)


def later_forms_kernel(k_ref, v2_ref, kt_ref, vd_ref, tmp):
    split_kernel(v2_ref, vd_ref, tmp)
    width, tokens = kt_ref.shape
    for g in range(tokens // GROUP):
        rows = group_rows(g)
        for h in range(width // 128):
            kt_ref[at(h), rows] = k_ref[rows, at(h)].T


def local_kernel(
    doc_ref, kd_ref, vt_ref, q2_ref, c2_ref, qd_ref, qt_ref, ct_ref, pt_ref, ol_ref, sl_ref, table_ref,
    tmpq, tmpc,
):
    tokens, width = kd_ref.shape
    heads = width // 128
    n_groups = tokens // GROUP
    anchor = lax.axis_index("seq") * tokens
    ends = doc_ends_of(doc_ref)

    def prepare(g):
        rows = group_rows(g)
        qs = split_heads(q2_ref, tmpq, g, heads)
        cs = split_heads(c2_ref, tmpc, g, heads)
        qts = []
        for h in range(heads):
            qt = turn(qs[h])
            qd_ref[rows, at(h)] = qs[h].astype(BF16)
            qt_ref[at(h), rows] = qt
            ct_ref[at(h), rows] = turn(cs[h])
            qts.append(qt)
        return qts

    def scores(g, qts):
        rows = group_rows(g)
        mask = group_mask(known(table_ref, BEGIN, g))
        pts = []
        for h in range(heads):
            pt = jnp.where(mask, dot(kd_ref[rows, at(h)], qts[h]), 0.0).astype(BF16)
            pt_ref[h, rows, :] = pt
            pts.append(pt)
        return pts

    write_table(table_ref, ends, anchor, tokens)
    state = [jnp.zeros((128, 128), F32) for _ in range(heads)]
    next_pts = scores(0, prepare(0))
    next_qts = prepare(1) if n_groups > 1 else None
    for g in range(n_groups):
        pts = next_pts
        if g + 1 < n_groups:
            next_pts = scores(g + 1, next_qts)
        if g + 2 < n_groups:
            next_qts = prepare(g + 2)
        first = anchor + g * GROUP
        rows = group_rows(g)
        begin = start_of(ends, first + GROUP - 1)
        tail = rows_iota(128) >= begin - first
        kept = (begin < first).astype(F32)
        for h in range(heads):
            vt = vt_ref[at(h), rows]
            sl_ref[g, h] = state[h]
            state[h] = state[h] * kept + dot(vt, keep_where(tail, kd_ref[rows, at(h)]))
            ol_ref[at(h), rows] = dot(vt, pts[h])


def place_halves(core, out_ref, own_ref, other_ref):
    half = own_ref.shape[0]
    out_ref[pl.ds(core * half, half)] = own_ref[...]
    out_ref[pl.ds((1 - core) * half, half)] = other_ref[...]


def part_of(core, own, half):
    return (core if own else 1 - core) * half


def head_rows(head):
    return pl.ds(pl.multiple_of(head * 128, 128), 128)


def stats_kernel(own, table_ref, qt_ref, ol_ref, ct_ref, sl_ref, state_ref, *refs):
    (before_ref, o_ref, sb_ref, st_ref) = refs if len(refs) == 4 else (None, *refs)
    width, tokens = qt_ref.shape
    half = state_ref.shape[0]
    n_groups = tokens // GROUP
    base = part_of(lax.axis_index("seq") % 2, own, half)

    def opened_terms(g):
        rows = group_rows(g)
        opened = lanes_iota(128) < known(table_ref, OPENED, g)
        same = factor(table_ref, SAME_OPENED, g)
        terms = []
        for h in range(half):
            sb = (sl_ref[g, base + h] + same * state_ref[h]).astype(BF16)
            sb_ref[g, h] = sb
            terms.append(jnp.where(opened, dot(sb, qt_ref[head_rows(base + h), rows]), 0.0))
        return terms

    ahead = opened_terms(0)
    for g in range(n_groups):
        terms = ahead
        if g + 1 < n_groups:
            ahead = opened_terms(g + 1)
        rows = group_rows(g)
        squares = jnp.zeros((1, GROUP), F32)
        inner = jnp.zeros((1, GROUP), F32)
        for h in range(half):
            o = ol_ref[head_rows(base + h), rows] + terms[h]
            o_ref[at(h), rows] = o
            squares += jnp.sum(o * o, axis=0, keepdims=True)
            inner += jnp.sum(o * ct_ref[head_rows(base + h), rows].astype(F32), axis=0, keepdims=True)
        both = jnp.concatenate([squares, inner], axis=0)
        st_ref[:, rows] = both if before_ref is None else both + before_ref[:, rows]


def back_state(half, n_groups, prepare, qd_ref, base, out_ref):
    total = [jnp.zeros((128, 128), F32) for _ in range(half)]
    ahead = prepare(0)
    for g in range(n_groups):
        ready = ahead
        if g + 1 < n_groups:
            ahead = prepare(g + 1)
        total = [
            total[h] + dot(ready[h], qd_ref[group_rows(g), head_rows(base + h)]) for h in range(half)
        ]
    for h in range(half):
        out_ref[h] = total[h]


def norm_kernel(
    width_all, table_ref, st_ref, o_ref, ct_ref, qd_ref, dobt_ref, rows_ref, send_ref
):
    tokens, width = qd_ref.shape
    half = send_ref.shape[0]
    base = part_of(lax.axis_index("seq") % 2, False, half)

    def prepare(g):
        rows = group_rows(g)
        keep = lanes_iota(128) < known(table_ref, SHARD_HEAD, g)
        total = st_ref[:, rows] * (1.0 / width_all)
        inv = lax.rsqrt(total[0:1] + EPSILON)
        slope = total[1:2] * inv * inv * inv
        rows_ref[:, rows] = jnp.concatenate([inv, slope] * 4, axis=0)
        ready = []
        for h in range(half):
            dob = inv * ct_ref[head_rows(base + h), rows].astype(F32) - slope * o_ref[at(h), rows]
            dobt_ref[at(h), rows] = dob.astype(BF16)
            ready.append(jnp.where(keep, dob, 0.0).astype(BF16))
        return ready

    back_state(half, tokens // GROUP, prepare, qd_ref, base, send_ref)


def merge_kernel(
    table_ref, rows_ref, own_ref, other_ref, ct_ref, qd_ref, dob_other_ref, sb_own_ref, sb_other_ref,
    dobt_ref, normed_ref, sb_ref, mine_ref,
):
    tokens, width = qd_ref.shape
    half = mine_ref.shape[0]
    core = lax.axis_index("seq") % 2
    base, far = part_of(core, True, half), part_of(core, False, half)

    def prepare(g):
        rows = group_rows(g)
        keep = lanes_iota(128) < known(table_ref, SHARD_HEAD, g)
        inv = rows_ref[0:1, rows]
        slope = rows_ref[1:2, rows]
        ready = []
        for h in range(half):
            mine, others = head_rows(base + h), head_rows(far + h)
            o = own_ref[at(h), rows]
            dob = inv * ct_ref[mine, rows].astype(F32) - slope * o
            dobt_ref[mine, rows] = dob.astype(BF16)
            dobt_ref[others, rows] = dob_other_ref[at(h), rows]
            normed_ref[mine, rows] = (o * inv).astype(BF16)
            normed_ref[others, rows] = (other_ref[at(h), rows] * inv).astype(BF16)
            sb_ref[g, base + h] = sb_own_ref[g, h]
            sb_ref[g, far + h] = sb_other_ref[g, h]
            ready.append(jnp.where(keep, dob, 0.0).astype(BF16))
        return ready

    back_state(half, tokens // GROUP, prepare, qd_ref, base, mine_ref)


def grad_kernel(groups, *refs):
    table_ref, normed_ref, dobt_ref, pt_ref, qd_ref, kt_ref, vd_ref, sb_ref, *refs = refs
    width = dobt_ref.shape[0]
    heads = width // 128
    n_groups = dobt_ref.shape[1] // GROUP
    state = [jnp.zeros((128, 128), F32) for _ in range(heads)]
    if groups.stop < n_groups:
        state_ref, _, _, *refs = refs
        state = [state_ref[h] for h in range(heads)]
    left_ref = None
    if groups.start > 0:
        left_ref, *refs = refs
    dk_ref, dv_ref, rl_ref, out_ref, gq_ref, tmpo, tmpq, bufo, bufq, sems = refs

    def scores(g):
        rows = group_rows(g)
        mask = group_mask(known(table_ref, BEGIN, g))
        return [
            jnp.where(mask, dot(vd_ref[rows, at(h)], dobt_ref[at(h), rows]), 0.0).astype(BF16)
            for h in range(heads)
        ]

    started = []
    ahead = scores(groups[-1])
    for g in reversed(groups):
        dpts = ahead
        slot = g % tmpq.shape[0]
        rows = group_rows(g)
        here = group_rows(g - groups.start)
        buffered = pair_rows(g - groups.start, heads)
        opened = lanes_iota(128) < known(table_ref, OPENED, g)
        head_part = lanes_iota(128) < known(table_ref, HEAD, g)
        kept = factor(table_ref, KEPT, g)
        for h in range(heads):
            mine = pl.ds(h, GROUP, stride=heads)
            dv_ref[here, at(h)] = dot(pt_ref[h, rows, :], turn(dobt_ref[at(h), rows]))
            tmpo[slot, mine, :] = normed_ref[at(h), rows].T.astype(F32)
        bufo[buffered, :] = tmpo[slot].astype(BF16)
        if g > groups.start:
            ahead = scores(g - 1)
        near, grown = [], []
        for h in range(heads):
            dobt = dobt_ref[at(h), rows]
            near.append(jnp.where(opened, dot(turn(sb_ref[g, h]), dobt), 0.0))
            grown.append(dot(keep_where(head_part, dobt), qd_ref[rows, at(h)]))
        for h in range(heads):
            mine = pl.ds(h, GROUP, stride=heads)
            dk_ref[here, at(h)] = dot(dpts[h], qd_ref[rows, at(h)])
            gq = dot(kt_ref[at(h), rows], dpts[h]) + near[h]
            tmpq[slot, mine, :] = turn(gq).astype(F32)
            rl_ref[g - groups.start, h] = state[h]
            state[h] = state[h] * kept + grown[h]
        bufq[buffered, :] = tmpq[slot].astype(BF16)
        for n, (buf, out) in enumerate(((bufo, out_ref), (bufq, gq_ref))):
            copy = pltpu.make_async_copy(
                buf.at[buffered], out.at[pair_rows(g, heads)], sems.at[n, g]
            )
            copy.start()
            started.append(copy)
    if left_ref is not None:
        for h in range(heads):
            left_ref[h] = state[h]
    for copy in started:
        copy.wait()


def final_kernel(table_ref, kd_ref, vd_ref, own_ref, other_ref, *refs):
    *parts, gk_ref, gv_ref, rin, tmpk, tmpv, bufk, bufv, sems = refs
    tokens, width = kd_ref.shape
    heads = width // 128
    n_groups = tokens // GROUP
    place_halves(lax.axis_index("seq") % 2, rin, own_ref, other_ref)
    held = []
    for dk_ref, dv_ref, rl_ref in zip(parts[0::3], parts[1::3], parts[2::3]):
        held += [(dk_ref, dv_ref, rl_ref, i) for i in range(rl_ref.shape[0])]

    def closing_terms(g):
        rows = group_rows(g)
        rl_ref, i = held[g][2:]
        closing = rows_iota(128) >= known(table_ref, CLOSING, g, 128)
        same = factor(table_ref, SAME_CLOSING, g)
        terms = []
        for h in range(heads):
            rb = (rl_ref[i, h] + same * rin[h]).astype(BF16)
            terms.append(
                (
                    jnp.where(closing, dot(vd_ref[rows, at(h)], rb), 0.0),
                    jnp.where(closing, dot(kd_ref[rows, at(h)], rb, NT), 0.0),
                )
            )
        return terms

    started = []
    ahead = closing_terms(0)
    for g in range(n_groups):
        terms = ahead
        if g + 1 < n_groups:
            ahead = closing_terms(g + 1)
        dk_ref, dv_ref, _, i = held[g]
        pairs = pair_rows(g, heads)
        slot = g % tmpk.shape[0]
        for h in range(heads):
            mine = pl.ds(h, GROUP, stride=heads)
            tmpk[slot, mine, :] = dk_ref[group_rows(i), at(h)] + terms[h][0]
            tmpv[slot, mine, :] = dv_ref[group_rows(i), at(h)] + terms[h][1]
        bufk[pairs, :] = tmpk[slot].astype(BF16)
        bufv[pairs, :] = tmpv[slot].astype(BF16)
        for n, (buf, out) in enumerate(((bufk, gk_ref), (bufv, gv_ref))):
            copy = pltpu.make_async_copy(buf.at[pairs], out.at[pairs], sems.at[n, g])
            copy.start()
            started.append(copy)
    for copy in started:
        copy.wait()


def call(kernel, name, outs, scratch, n_in, in_hbm=(), out_hbm=(), in_smem=(), alias=None, flops=0):
    vmem = pl.BlockSpec(memory_space=pltpu.VMEM)
    hbm = pl.BlockSpec(memory_space=pltpu.HBM)
    smem = pl.BlockSpec(memory_space=pltpu.SMEM)
    return pl.pallas_call(
        kernel,
        name=name,
        out_shape=[jax.ShapeDtypeStruct(s, d) for s, d in outs],
        in_specs=[hbm if i in in_hbm else smem if i in in_smem else vmem for i in range(n_in)],
        out_specs=[hbm if i in out_hbm else vmem for i in range(len(outs))],
        scratch_shapes=scratch,
        input_output_aliases=alias or {},
        cost_estimate=pl.CostEstimate(flops=flops, bytes_accessed=8 << 20, transcendentals=0),
        compiler_params=pltpu.CompilerParams(vmem_limit_bytes=16 << 20),
    )


def per_device(queries, keys, values, cotangent, doc_lengths):
    tokens, heads, head_width = queries.shape
    width = heads * head_width
    half = heads // 2
    n_groups = tokens // GROUP
    n_seq = lax.axis_size("seq")
    n_head = lax.axis_size("head")
    n_chips = n_seq // 2

    def pairs(x):
        return x.reshape(tokens * heads, head_width)

    q2, k2, v2, c2 = pairs(queries), pairs(keys), pairs(values), pairs(cotangent)
    full = (tokens, width)
    piece = (half, head_width, head_width)
    state_shape = (heads, head_width, head_width)
    flat = (tokens * heads, head_width)
    buf = pltpu.VMEM(flat, BF16)
    tmp = pltpu.VMEM((2, GROUP * heads, head_width), F32)
    sems = pltpu.SemaphoreType.DMA((2, n_groups))
    swap_pairs = [(i, i ^ 1) for i in range(n_seq)]

    def swap(x):
        return lax.ppermute(x, "seq", swap_pairs)

    def exchange(mine, send, weights, after):
        got = swap(send)
        chip_state, after = lax.optimization_barrier((weights[0] * mine + weights[1] * got, after))
        total = jnp.zeros(piece, F32)
        for k in range(1, n_chips):
            links = [(2 * i + c, 2 * j + c) for i, j in links_of(k, n_chips) for c in (0, 1)]
            total = total + weights[5 + k] * lax.ppermute(chip_state, "seq", links)
        return got, total, after

    def finish(mine, got, total, weights):
        return weights[2] * total + weights[3] * got, swap(weights[4] * total + weights[5] * mine)

    mm = 2 * tokens * heads * head_width * head_width
    table = ((5 + n_chips, 128), F32)
    state = pltpu.VMEM(state_shape, F32)
    table = ((5 + n_chips, 128), F32)
    turned = (width, tokens)
    group_states = (n_groups, heads, head_width, head_width)
    raw_k, raw_v, vt, mine, send, fore, back = call(
        functools.partial(state_kernel, n_seq),
        "shard_state",
        [(flat, BF16), (flat, BF16), (turned, BF16), (piece, F32), (piece, F32), table, table],
        [
            pltpu.SMEM(doc_lengths.shape, jnp.int32),
            tmp,
            tmp,
            state,
            sems,
            pltpu.SemaphoreType.DMA,
        ],
        n_in=3,
        in_hbm=(0, 1, 2),
        flops=mm,
    )(*(pltpu.with_memory_space_constraint(x, pltpu.HBM) for x in (doc_lengths, k2, v2)))
    (kd,) = call(
        split_kernel,
        "split_keys",
        [(full, BF16)],
        [tmp],
        n_in=1,
    )(raw_k)
    got, total, (kd, vt) = exchange(mine, send, fore, (kd, vt))
    facts = (8, n_groups, GROUP)
    qd, qt, ct, pt, o_local, sl, known_of = call(
        local_kernel,
        "local_mix",
        [
            (full, BF16),
            (turned, BF16),
            (turned, BF16),
            ((heads, tokens, GROUP), BF16),
            (turned, F32),
            (group_states, F32),
            (facts, jnp.int32),
        ],
        [tmp, tmp],
        n_in=5,
        in_smem=(0,),
        flops=6 * mm,
    )(doc_lengths, kd, vt, q2, c2)
    total, o_local = lax.optimization_barrier((total, o_local))
    own, other = finish(mine, got, total, fore)
    half_turned = (half * head_width, tokens)
    half_states = (n_groups, half, head_width, head_width)

    def part(is_own, states, before, name):
        return call(
            functools.partial(stats_kernel, is_own),
            name,
            [(half_turned, F32), (half_states, BF16), ((2, tokens), F32)],
            [],
            n_in=6 + len(before),
            flops=mm // 2,
        )(known_of, qt, o_local, ct, sl, states, *before)

    o_own, sb_own, stats = part(True, own, (), "mix_own")
    o_other, sb_other, stats = part(False, other, (stats,), "mix_other")
    stats, kd_late, raw_v = lax.optimization_barrier((stats, kd, raw_v))
    kt, vd = call(
        later_forms_kernel,
        "later_forms",
        [(turned, BF16), (full, BF16)],
        [tmp],
        n_in=2,
    )(kd_late, raw_v)
    stats = stats + sum(
        lax.ppermute(stats, "head", links_of(k, n_head)) for k in range(1, n_head)
    )
    stats, kt, vd = lax.optimization_barrier((stats, kt, vd))
    dob_other, factors, send = call(
        functools.partial(norm_kernel, float(width * n_head)),
        "norm_other",
        [(half_turned, BF16), ((8, tokens), F32), (piece, F32)],
        [],
        n_in=5,
        flops=mm // 2,
    )(known_of, stats, o_other, ct, qd)
    dobt, normed, sb, mine = call(
        merge_kernel,
        "norm_own",
        [(turned, BF16), (turned, BF16), (group_states, BF16), (piece, F32)],
        [],
        n_in=9,
        flops=mm // 2,
    )(known_of, factors, o_own, o_other, ct, qd, dob_other, sb_own, sb_other)
    got, total, (dobt_b, normed_b) = exchange(mine, send, back, (dobt, normed))
    cut = max(1, n_groups // 4)
    earlier, later = range(0, cut), range(cut, n_groups)

    def grads(groups, name, before):
        count = len(groups)
        held = (count * GROUP, width)
        left = [(state_shape, F32)] if groups.start else []
        kept = [(held, F32), (held, F32), ((count, *state_shape), F32)]
        whole = len(left) + len(kept)
        return call(
            functools.partial(grad_kernel, groups),
            name,
            [*left, *kept, (flat, BF16), (flat, BF16)],
            [tmp, tmp, pltpu.VMEM((count * GROUP * heads, head_width), BF16)]
            + [pltpu.VMEM((count * GROUP * heads, head_width), BF16), sems],
            n_in=8 + len(before),
            in_hbm=(9, 10),
            out_hbm=(whole, whole + 1),
            alias={9: whole, 10: whole + 1} if before else None,
            flops=count * mm,
        )(known_of, normed_b, dobt_b, pt, qd, kt, vd, sb, *before)

    left, dk1, dv1, rl1, output, grad_q = grads(later, "grads_later", ())
    total, left = lax.optimization_barrier((total, left))
    own, other = finish(mine, got, total, back)
    dk0, dv0, rl0, output, grad_q = grads(earlier, "grads_earlier", (left, output, grad_q))
    grad_k, grad_v = call(
        final_kernel,
        "final_grads",
        [(flat, BF16), (flat, BF16)],
        [state, tmp, tmp, buf, buf, sems],
        n_in=11,
        out_hbm=(0, 1),
        flops=2 * mm,
    )(known_of, kd, vd, own, other, dk0, dv0, rl0, dk1, dv1, rl1)
    return tuple(x.reshape(queries.shape) for x in (output, grad_q, grad_k, grad_v))


def solution(mesh):
    spec = P("seq", "head", None)
    return jax.shard_map(
        per_device,
        mesh=mesh,
        in_specs=(spec, spec, spec, spec, P()),
        out_specs=(spec, spec, spec, spec),
        check_vma=False,
    )
```

```python
import functools

import jax
import jax.numpy as jnp
from jax import lax
from jax.experimental import pallas as pl
from jax.experimental.pallas import tpu as pltpu
from jax.sharding import PartitionSpec as P

GROUP = 256
EPSILON = 1e-06
OPENED, SAME_OPENED, HEAD, KEPT, SHARD_HEAD, CLOSING, SAME_CLOSING, BEGIN = range(8)
F32 = jnp.float32
BF16 = jnp.bfloat16

NN = (((1,), (0,)), ((), ()))
NT = (((1,), (1,)), ((), ()))
TN = (((0,), (0,)), ((), ()))


def dot(a, b, dims=NN):
    return lax.dot_general(a, b, dims, preferred_element_type=F32)


def doc_ends_of(doc_ref):
    ends, total = [], jnp.int32(0)
    for j in range(doc_ref.shape[0]):
        total = total + doc_ref[j]
        ends.append(total)
    return ends


def start_of(ends, place):
    found = jnp.int32(0)
    for end in ends:
        found = jnp.where(end <= place, end, found)
    return found


def end_of(ends, place):
    found = jnp.int32(2**30)
    for end in reversed(ends):
        found = jnp.where(end > place, end, found)
    return found


def rows_iota(width):
    return lax.broadcasted_iota(jnp.int32, (GROUP, width), 0)


def lanes_iota(rows):
    return lax.broadcasted_iota(jnp.int32, (rows, GROUP), 1)


def begin_row(ends, first):
    place = lanes_iota(8) + first
    begin = jnp.zeros((8, GROUP), jnp.int32)
    for end in ends:
        begin = jnp.where(place >= end, end, begin)
    return begin - first


def group_mask(begin):
    row = rows_iota(GROUP)
    return (row >= begin) & (row <= lanes_iota(GROUP))


def write_table(table_ref, ends, anchor, tokens):
    for g in range(tokens // GROUP):
        first = anchor + g * GROUP
        after = first + GROUP
        numbers = {
            OPENED: end_of(ends, first - 1) - first,
            SAME_OPENED: (start_of(ends, first - 1) < anchor).astype(jnp.int32),
            HEAD: end_of(ends, first) - first,
            KEPT: (end_of(ends, first) > after).astype(jnp.int32),
            SHARD_HEAD: end_of(ends, anchor) - first,
            CLOSING: start_of(ends, after) - first,
            SAME_CLOSING: (end_of(ends, after) > anchor + tokens).astype(jnp.int32),
        }
        for kind, number in numbers.items():
            table_ref[kind, pl.ds(g, 1), :] = jnp.full((1, GROUP), number, jnp.int32)
        table_ref[BEGIN, pl.ds(g, 1), :] = begin_row(ends, first)[:1]


def known(table_ref, kind, g, width=GROUP):
    return table_ref[kind, pl.ds(g, 1), :width]


def factor(table_ref, kind, g):
    return known(table_ref, kind, g, 128).astype(F32)


def keep_where(keep, x):
    return jnp.where(keep, x.astype(F32), 0.0).astype(BF16)


def at(h):
    return slice(h * 128, (h + 1) * 128)


def turn(x):
    return x.astype(BF16).T


def pair_rows(g, heads):
    return pl.ds(pl.multiple_of(g * (GROUP * heads), GROUP * heads), GROUP * heads)


def split_heads(buf_ref, tmp_ref, g, heads):
    slot = g % tmp_ref.shape[0]
    tmp_ref[slot] = buf_ref[pair_rows(g, heads), :].astype(F32)
    return [tmp_ref[slot, pl.ds(h, GROUP, stride=heads), :] for h in range(heads)]


def group_rows(g):
    return pl.ds(pl.multiple_of(g * GROUP, GROUP), GROUP)


def source_of(index, step, size):
    if size & (size - 1):
        return (index + size - step) % size
    return index ^ step


def links_of(step, size):
    return [(source_of(i, step, size), i) for i in range(size)]


def weights_of(out_ref, ends, shard, tokens, n_seq, sign):
    core = shard % 2
    chip = shard // 2
    n_chips = n_seq // 2
    others = [source_of(chip, k, n_chips) for k in range(1, n_chips)]
    chip_first = (shard - core) * tokens
    middle = chip_first + tokens
    chip_end = middle + tokens
    if sign > 0:
        join = start_of(ends, chip_end - 1) < middle
        onward = start_of(ends, middle - 1) < chip_first
        begin = start_of(ends, chip_first - 1)
        same = [(other < chip) & (begin < (other + 1) * (2 * tokens)) for other in others]
        is_near = core == 0
    else:
        join = end_of(ends, chip_first) > middle
        onward = end_of(ends, middle) > chip_end
        end = end_of(ends, chip_end)
        same = [(other > chip) & (end > other * (2 * tokens)) for other in others]
        is_near = core == 1
    join, onward, is_near = (x.astype(F32) for x in (join, onward, is_near))
    far = 1.0 - is_near
    table = [
        is_near * join + far,
        is_near + far * join,
        is_near + far * onward,
        far,
        is_near * onward + far,
        is_near,
    ] + [x.astype(F32) for x in same]
    for i, x in enumerate(table):
        out_ref[pl.ds(i, 1), :] = jnp.full((1, 128), x, F32)


def state_kernel(
    n_seq, doc_hbm, k2_ref, v2_ref, bufk, bufv, vt_ref, mine_ref, send_ref, fore_ref, back_ref,
    doc_ref, tmpk, tmpv, acc, sems, doc_sem,
):
    width, tokens = vt_ref.shape
    heads = width // 128
    half = heads // 2
    n_groups = tokens // GROUP

    sizes = [max(1, n_groups // 6), max(1, n_groups // 3)]
    sizes = [*sizes, n_groups - sum(sizes)] if n_groups > 2 else [1] * n_groups
    chunks = {sum(sizes[:i]): size for i, size in enumerate(sizes)}

    def fetches(g):
        if g not in chunks:
            return ()
        rows = pl.ds(g * GROUP * heads, chunks[g] * GROUP * heads)
        return (
            pltpu.make_async_copy(k2_ref.at[rows], bufk.at[rows], sems.at[0, g]),
            pltpu.make_async_copy(v2_ref.at[rows], bufv.at[rows], sems.at[1, g]),
        )

    doc_copy = pltpu.make_async_copy(doc_hbm, doc_ref, doc_sem)
    doc_copy.start()
    for g in range(n_groups):
        for copy in fetches(g):
            copy.start()
    doc_copy.wait()
    shard = lax.axis_index("seq")
    core = shard % 2
    anchor = shard * tokens
    ends = doc_ends_of(doc_ref)
    weights_of(fore_ref, ends, shard, tokens, n_seq, 1)
    weights_of(back_ref, ends, shard, tokens, n_seq, -1)
    tail = start_of(ends, anchor + tokens - 1) - anchor

    def prepare(g):
        for copy in fetches(g):
            copy.wait()
        rows = group_rows(g)
        keep = rows_iota(128) + g * GROUP >= tail
        ks = split_heads(bufk, tmpk, g, heads)
        vs = split_heads(bufv, tmpv, g, heads)
        ready = []
        for h in range(heads):
            vt = turn(vs[h])
            vt_ref[at(h), rows] = vt
            ready.append((vt, jnp.where(keep, ks[h], 0.0).astype(BF16)))
        return ready

    total = [jnp.zeros((128, 128), F32) for _ in range(heads)]
    ahead = prepare(0)
    for g in range(n_groups):
        ready = ahead
        if g + 1 < n_groups:
            ahead = prepare(g + 1)
        total = [t + dot(vt, k) for t, (vt, k) in zip(total, ready)]
    for h in range(heads):
        acc[h] = total[h]
    mine_ref[...] = acc[pl.ds(core * half, half)]
    send_ref[...] = acc[pl.ds((1 - core) * half, half)]


def split_kernel(pairs_ref, out_ref, tmp):
    tokens, width = out_ref.shape
    heads = width // 128
    for g in range(tokens // GROUP):
        parts = split_heads(pairs_ref, tmp, g, heads)
        for h in range(heads):
            out_ref[group_rows(g), at(h)] = parts[h].astype(BF16)


def later_forms_kernel(k_ref, v2_ref, own_ref, other_ref, kt_ref, vd_ref, st_ref, tmp):
    split_kernel(v2_ref, vd_ref, tmp)
    width, tokens = kt_ref.shape
    half = own_ref.shape[1]
    core = lax.axis_index("seq") % 2
    for g in range(tokens // GROUP):
        for h in range(half):
            st_ref[g, part_of(core, True, half) + h] = own_ref[g, h].T
            st_ref[g, part_of(core, False, half) + h] = other_ref[g, h].T
        rows = group_rows(g)
        for h in range(width // 128):
            kt_ref[at(h), rows] = k_ref[rows, at(h)].T


def local_kernel(
    doc_ref, kd_ref, vt_ref, q2_ref, c2_ref, qd_ref, qt_ref, ct_ref, pt_ref, ol_ref, sl_ref, table_ref,
    tmpq, tmpc,
):
    tokens, width = kd_ref.shape
    heads = width // 128
    n_groups = tokens // GROUP
    anchor = lax.axis_index("seq") * tokens
    ends = doc_ends_of(doc_ref)

    def prepare(g):
        rows = group_rows(g)
        qs = split_heads(q2_ref, tmpq, g, heads)
        cs = split_heads(c2_ref, tmpc, g, heads)
        qts = []
        for h in range(heads):
            qt = turn(qs[h])
            qd_ref[rows, at(h)] = qs[h].astype(BF16)
            qt_ref[at(h), rows] = qt
            ct_ref[at(h), rows] = turn(cs[h])
            qts.append(qt)
        return qts

    def scores(g, qts):
        rows = group_rows(g)
        mask = group_mask(known(table_ref, BEGIN, g))
        pts = []
        for h in range(heads):
            pt = jnp.where(mask, dot(kd_ref[rows, at(h)], qts[h]), 0.0).astype(BF16)
            pt_ref[h, rows, :] = pt
            pts.append(pt)
        return pts

    write_table(table_ref, ends, anchor, tokens)
    state = [jnp.zeros((128, 128), F32) for _ in range(heads)]
    next_pts = scores(0, prepare(0))
    next_qts = prepare(1) if n_groups > 1 else None
    for g in range(n_groups):
        pts = next_pts
        if g + 1 < n_groups:
            next_pts = scores(g + 1, next_qts)
        if g + 2 < n_groups:
            next_qts = prepare(g + 2)
        first = anchor + g * GROUP
        rows = group_rows(g)
        begin = start_of(ends, first + GROUP - 1)
        tail = rows_iota(128) >= begin - first
        kept = (begin < first).astype(F32)
        for h in range(heads):
            vt = vt_ref[at(h), rows]
            sl_ref[g, h] = state[h]
            state[h] = state[h] * kept + dot(vt, keep_where(tail, kd_ref[rows, at(h)]))
            ol_ref[at(h), rows] = dot(vt, pts[h])


def place_halves(core, out_ref, own_ref, other_ref):
    half = own_ref.shape[0]
    out_ref[pl.ds(core * half, half)] = own_ref[...]
    out_ref[pl.ds((1 - core) * half, half)] = other_ref[...]


def part_of(core, own, half):
    return (core if own else 1 - core) * half


def head_rows(head):
    return pl.ds(pl.multiple_of(head * 128, 128), 128)


def stats_kernel(own, table_ref, qt_ref, ol_ref, ct_ref, sl_ref, state_ref, *refs):
    (before_ref, o_ref, sb_ref, st_ref) = refs if len(refs) == 4 else (None, *refs)
    width, tokens = qt_ref.shape
    half = state_ref.shape[0]
    n_groups = tokens // GROUP
    base = part_of(lax.axis_index("seq") % 2, own, half)

    def opened_terms(g):
        rows = group_rows(g)
        opened = lanes_iota(128) < known(table_ref, OPENED, g)
        same = factor(table_ref, SAME_OPENED, g)
        terms = []
        for h in range(half):
            sb = (sl_ref[g, base + h] + same * state_ref[h]).astype(BF16)
            sb_ref[g, h] = sb
            terms.append(jnp.where(opened, dot(sb, qt_ref[head_rows(base + h), rows]), 0.0))
        return terms

    ahead = opened_terms(0)
    for g in range(n_groups):
        terms = ahead
        if g + 1 < n_groups:
            ahead = opened_terms(g + 1)
        rows = group_rows(g)
        squares = jnp.zeros((1, GROUP), F32)
        inner = jnp.zeros((1, GROUP), F32)
        for h in range(half):
            o = ol_ref[head_rows(base + h), rows] + terms[h]
            o_ref[at(h), rows] = o
            squares += jnp.sum(o * o, axis=0, keepdims=True)
            inner += jnp.sum(o * ct_ref[head_rows(base + h), rows].astype(F32), axis=0, keepdims=True)
        both = jnp.concatenate([squares, inner], axis=0)
        st_ref[:, rows] = both if before_ref is None else both + before_ref[:, rows]


def back_state(half, n_groups, prepare, qd_ref, base, out_ref):
    total = [jnp.zeros((128, 128), F32) for _ in range(half)]
    ahead = prepare(0)
    for g in range(n_groups):
        ready = ahead
        if g + 1 < n_groups:
            ahead = prepare(g + 1)
        total = [
            total[h] + dot(ready[h], qd_ref[group_rows(g), head_rows(base + h)]) for h in range(half)
        ]
    for h in range(half):
        out_ref[h] = total[h]


def norm_kernel(
    width_all, table_ref, st_ref, o_ref, ct_ref, qd_ref, dobt_ref, rows_ref, send_ref
):
    tokens, width = qd_ref.shape
    half = send_ref.shape[0]
    base = part_of(lax.axis_index("seq") % 2, False, half)

    def prepare(g):
        rows = group_rows(g)
        keep = lanes_iota(128) < known(table_ref, SHARD_HEAD, g)
        total = st_ref[:, rows] * (1.0 / width_all)
        inv = lax.rsqrt(total[0:1] + EPSILON)
        slope = total[1:2] * inv * inv * inv
        rows_ref[:, rows] = jnp.concatenate([inv, slope] * 4, axis=0)
        ready = []
        for h in range(half):
            dob = inv * ct_ref[head_rows(base + h), rows].astype(F32) - slope * o_ref[at(h), rows]
            dobt_ref[at(h), rows] = dob.astype(BF16)
            ready.append(jnp.where(keep, dob, 0.0).astype(BF16))
        return ready

    back_state(half, tokens // GROUP, prepare, qd_ref, base, send_ref)


def merge_kernel(
    table_ref, rows_ref, own_ref, other_ref, ct_ref, qd_ref, dob_other_ref,
    dobt_ref, normed_ref, mine_ref,
):
    tokens, width = qd_ref.shape
    half = mine_ref.shape[0]
    core = lax.axis_index("seq") % 2
    base, far = part_of(core, True, half), part_of(core, False, half)

    def prepare(g):
        rows = group_rows(g)
        keep = lanes_iota(128) < known(table_ref, SHARD_HEAD, g)
        inv = rows_ref[0:1, rows]
        slope = rows_ref[1:2, rows]
        ready = []
        for h in range(half):
            mine, others = head_rows(base + h), head_rows(far + h)
            o = own_ref[at(h), rows]
            dob = inv * ct_ref[mine, rows].astype(F32) - slope * o
            dobt_ref[mine, rows] = dob.astype(BF16)
            dobt_ref[others, rows] = dob_other_ref[at(h), rows]
            normed_ref[mine, rows] = (o * inv).astype(BF16)
            normed_ref[others, rows] = (other_ref[at(h), rows] * inv).astype(BF16)
            ready.append(jnp.where(keep, dob, 0.0).astype(BF16))
        return ready

    back_state(half, tokens // GROUP, prepare, qd_ref, base, mine_ref)


def grad_kernel(groups, *refs):
    table_ref, normed_ref, dobt_ref, pt_ref, qd_ref, kt_ref, vd_ref, sb_ref, *refs = refs
    width = dobt_ref.shape[0]
    heads = width // 128
    n_groups = dobt_ref.shape[1] // GROUP
    state = [jnp.zeros((128, 128), F32) for _ in range(heads)]
    if groups.stop < n_groups:
        state_ref, _, _, *refs = refs
        state = [state_ref[h] for h in range(heads)]
    left_ref = None
    if groups.start > 0:
        left_ref, *refs = refs
    dk_ref, dv_ref, rl_ref, out_ref, gq_ref, tmpo, tmpq, bufo, bufq, sems = refs

    def scores(g):
        rows = group_rows(g)
        mask = group_mask(known(table_ref, BEGIN, g))
        return [
            jnp.where(mask, dot(vd_ref[rows, at(h)], dobt_ref[at(h), rows]), 0.0).astype(BF16)
            for h in range(heads)
        ]

    started = []
    ahead = scores(groups[-1])
    for g in reversed(groups):
        dpts = ahead
        slot = g % tmpq.shape[0]
        rows = group_rows(g)
        here = group_rows(g - groups.start)
        buffered = pair_rows(g - groups.start, heads)
        opened = lanes_iota(128) < known(table_ref, OPENED, g)
        head_part = lanes_iota(128) < known(table_ref, HEAD, g)
        kept = factor(table_ref, KEPT, g)
        for h in range(heads):
            mine = pl.ds(h, GROUP, stride=heads)
            dv_ref[here, at(h)] = dot(pt_ref[h, rows, :], turn(dobt_ref[at(h), rows]))
            tmpo[slot, mine, :] = normed_ref[at(h), rows].T.astype(F32)
        bufo[buffered, :] = tmpo[slot].astype(BF16)
        if g > groups.start:
            ahead = scores(g - 1)
        near, grown = [], []
        for h in range(heads):
            dobt = dobt_ref[at(h), rows]
            near.append(jnp.where(opened, dot(sb_ref[g, h], dobt), 0.0))
            grown.append(dot(keep_where(head_part, dobt), qd_ref[rows, at(h)]))
        for h in range(heads):
            mine = pl.ds(h, GROUP, stride=heads)
            dk_ref[here, at(h)] = dot(dpts[h], qd_ref[rows, at(h)])
            gq = dot(kt_ref[at(h), rows], dpts[h]) + near[h]
            tmpq[slot, mine, :] = turn(gq).astype(F32)
            rl_ref[g - groups.start, h] = state[h]
            state[h] = state[h] * kept + grown[h]
        bufq[buffered, :] = tmpq[slot].astype(BF16)
        for n, (buf, out) in enumerate(((bufo, out_ref), (bufq, gq_ref))):
            copy = pltpu.make_async_copy(
                buf.at[buffered], out.at[pair_rows(g, heads)], sems.at[n, g]
            )
            copy.start()
            started.append(copy)
    if left_ref is not None:
        for h in range(heads):
            left_ref[h] = state[h]
    for copy in started:
        copy.wait()


def final_kernel(table_ref, kd_ref, vd_ref, own_ref, other_ref, *refs):
    *parts, gk_ref, gv_ref, rin, tmpk, tmpv, bufk, bufv, sems = refs
    tokens, width = kd_ref.shape
    heads = width // 128
    n_groups = tokens // GROUP
    place_halves(lax.axis_index("seq") % 2, rin, own_ref, other_ref)
    held = []
    for dk_ref, dv_ref, rl_ref in zip(parts[0::3], parts[1::3], parts[2::3]):
        held += [(dk_ref, dv_ref, rl_ref, i) for i in range(rl_ref.shape[0])]

    def closing_terms(g):
        rows = group_rows(g)
        rl_ref, i = held[g][2:]
        closing = rows_iota(128) >= known(table_ref, CLOSING, g, 128)
        same = factor(table_ref, SAME_CLOSING, g)
        terms = []
        for h in range(heads):
            rb = (rl_ref[i, h] + same * rin[h]).astype(BF16)
            terms.append(
                (
                    jnp.where(closing, dot(vd_ref[rows, at(h)], rb), 0.0),
                    jnp.where(closing, dot(kd_ref[rows, at(h)], rb, NT), 0.0),
                )
            )
        return terms

    started = []
    ahead = closing_terms(0)
    for g in range(n_groups):
        terms = ahead
        if g + 1 < n_groups:
            ahead = closing_terms(g + 1)
        dk_ref, dv_ref, _, i = held[g]
        pairs = pair_rows(g, heads)
        slot = g % tmpk.shape[0]
        for h in range(heads):
            mine = pl.ds(h, GROUP, stride=heads)
            tmpk[slot, mine, :] = dk_ref[group_rows(i), at(h)] + terms[h][0]
            tmpv[slot, mine, :] = dv_ref[group_rows(i), at(h)] + terms[h][1]
        bufk[pairs, :] = tmpk[slot].astype(BF16)
        bufv[pairs, :] = tmpv[slot].astype(BF16)
        for n, (buf, out) in enumerate(((bufk, gk_ref), (bufv, gv_ref))):
            copy = pltpu.make_async_copy(buf.at[pairs], out.at[pairs], sems.at[n, g])
            copy.start()
            started.append(copy)
    for copy in started:
        copy.wait()


def call(kernel, name, outs, scratch, n_in, in_hbm=(), out_hbm=(), in_smem=(), alias=None, flops=0):
    vmem = pl.BlockSpec(memory_space=pltpu.VMEM)
    hbm = pl.BlockSpec(memory_space=pltpu.HBM)
    smem = pl.BlockSpec(memory_space=pltpu.SMEM)
    return pl.pallas_call(
        kernel,
        name=name,
        out_shape=[jax.ShapeDtypeStruct(s, d) for s, d in outs],
        in_specs=[hbm if i in in_hbm else smem if i in in_smem else vmem for i in range(n_in)],
        out_specs=[hbm if i in out_hbm else vmem for i in range(len(outs))],
        scratch_shapes=scratch,
        input_output_aliases=alias or {},
        cost_estimate=pl.CostEstimate(flops=flops, bytes_accessed=8 << 20, transcendentals=0),
        compiler_params=pltpu.CompilerParams(vmem_limit_bytes=16 << 20),
    )


def per_device(queries, keys, values, cotangent, doc_lengths):
    tokens, heads, head_width = queries.shape
    width = heads * head_width
    half = heads // 2
    n_groups = tokens // GROUP
    n_seq = lax.axis_size("seq")
    n_head = lax.axis_size("head")
    n_chips = n_seq // 2

    def pairs(x):
        return x.reshape(tokens * heads, head_width)

    q2, k2, v2, c2 = pairs(queries), pairs(keys), pairs(values), pairs(cotangent)
    full = (tokens, width)
    piece = (half, head_width, head_width)
    state_shape = (heads, head_width, head_width)
    flat = (tokens * heads, head_width)
    buf = pltpu.VMEM(flat, BF16)
    tmp = pltpu.VMEM((2, GROUP * heads, head_width), F32)
    sems = pltpu.SemaphoreType.DMA((2, n_groups))
    swap_pairs = [(i, i ^ 1) for i in range(n_seq)]

    def swap(x):
        return lax.ppermute(x, "seq", swap_pairs)

    def exchange(mine, send, weights, after):
        got = swap(send)
        chip_state, after = lax.optimization_barrier((weights[0] * mine + weights[1] * got, after))
        total = jnp.zeros(piece, F32)
        for k in range(1, n_chips):
            links = [(2 * i + c, 2 * j + c) for i, j in links_of(k, n_chips) for c in (0, 1)]
            total = total + weights[5 + k] * lax.ppermute(chip_state, "seq", links)
        return got, total, after

    def finish(mine, got, total, weights):
        return weights[2] * total + weights[3] * got, swap(weights[4] * total + weights[5] * mine)

    mm = 2 * tokens * heads * head_width * head_width
    table = ((5 + n_chips, 128), F32)
    state = pltpu.VMEM(state_shape, F32)
    table = ((5 + n_chips, 128), F32)
    turned = (width, tokens)
    group_states = (n_groups, heads, head_width, head_width)
    raw_k, raw_v, vt, mine, send, fore, back = call(
        functools.partial(state_kernel, n_seq),
        "shard_state",
        [(flat, BF16), (flat, BF16), (turned, BF16), (piece, F32), (piece, F32), table, table],
        [
            pltpu.SMEM(doc_lengths.shape, jnp.int32),
            tmp,
            tmp,
            state,
            sems,
            pltpu.SemaphoreType.DMA,
        ],
        n_in=3,
        in_hbm=(0, 1, 2),
        flops=mm,
    )(*(pltpu.with_memory_space_constraint(x, pltpu.HBM) for x in (doc_lengths, k2, v2)))
    (kd,) = call(
        split_kernel,
        "split_keys",
        [(full, BF16)],
        [tmp],
        n_in=1,
    )(raw_k)
    got, total, (kd, vt) = exchange(mine, send, fore, (kd, vt))
    facts = (8, n_groups, GROUP)
    qd, qt, ct, pt, o_local, sl, known_of = call(
        local_kernel,
        "local_mix",
        [
            (full, BF16),
            (turned, BF16),
            (turned, BF16),
            ((heads, tokens, GROUP), BF16),
            (turned, F32),
            (group_states, F32),
            (facts, jnp.int32),
        ],
        [tmp, tmp],
        n_in=5,
        in_smem=(0,),
        flops=6 * mm,
    )(doc_lengths, kd, vt, q2, c2)
    total, o_local = lax.optimization_barrier((total, o_local))
    own, other = finish(mine, got, total, fore)
    half_turned = (half * head_width, tokens)
    half_states = (n_groups, half, head_width, head_width)

    def part(is_own, states, before, name):
        return call(
            functools.partial(stats_kernel, is_own),
            name,
            [(half_turned, F32), (half_states, BF16), ((2, tokens), F32)],
            [],
            n_in=6 + len(before),
            flops=mm // 2,
        )(known_of, qt, o_local, ct, sl, states, *before)

    o_own, sb_own, stats = part(True, own, (), "mix_own")
    o_other, sb_other, stats = part(False, other, (stats,), "mix_other")
    stats, kd_late, raw_v = lax.optimization_barrier((stats, kd, raw_v))
    kt, vd, sb = call(
        later_forms_kernel,
        "later_forms",
        [(turned, BF16), (full, BF16), (group_states, BF16)],
        [tmp],
        n_in=4,
    )(kd_late, raw_v, sb_own, sb_other)
    stats = stats + sum(
        lax.ppermute(stats, "head", links_of(k, n_head)) for k in range(1, n_head)
    )
    stats, kt, vd, sb = lax.optimization_barrier((stats, kt, vd, sb))
    dob_other, factors, send = call(
        functools.partial(norm_kernel, float(width * n_head)),
        "norm_other",
        [(half_turned, BF16), ((8, tokens), F32), (piece, F32)],
        [],
        n_in=5,
        flops=mm // 2,
    )(known_of, stats, o_other, ct, qd)
    dobt, normed, mine = call(
        merge_kernel,
        "norm_own",
        [(turned, BF16), (turned, BF16), (piece, F32)],
        [],
        n_in=7,
        flops=mm // 2,
    )(known_of, factors, o_own, o_other, ct, qd, dob_other)
    got, total, (dobt_b, normed_b) = exchange(mine, send, back, (dobt, normed))
    cut = max(1, n_groups // 12)
    earlier, later = range(0, cut), range(cut, n_groups)

    def grads(groups, name, before):
        count = len(groups)
        held = (count * GROUP, width)
        left = [(state_shape, F32)] if groups.start else []
        kept = [(held, F32), (held, F32), ((count, *state_shape), F32)]
        whole = len(left) + len(kept)
        return call(
            functools.partial(grad_kernel, groups),
            name,
            [*left, *kept, (flat, BF16), (flat, BF16)],
            [tmp, tmp, pltpu.VMEM((count * GROUP * heads, head_width), BF16)]
            + [pltpu.VMEM((count * GROUP * heads, head_width), BF16), sems],
            n_in=8 + len(before),
            in_hbm=(9, 10),
            out_hbm=(whole, whole + 1),
            alias={9: whole, 10: whole + 1} if before else None,
            flops=count * mm,
        )(known_of, normed_b, dobt_b, pt, qd, kt, vd, sb, *before)

    left, dk1, dv1, rl1, output, grad_q = grads(later, "grads_later", ())
    total, left = lax.optimization_barrier((total, left))
    own, other = finish(mine, got, total, back)
    dk0, dv0, rl0, output, grad_q = grads(earlier, "grads_earlier", (left, output, grad_q))
    grad_k, grad_v = call(
        final_kernel,
        "final_grads",
        [(flat, BF16), (flat, BF16)],
        [state, tmp, tmp, buf, buf, sems],
        n_in=11,
        out_hbm=(0, 1),
        flops=2 * mm,
    )(known_of, kd, vd, own, other, dk0, dv0, rl0, dk1, dv1, rl1)
    return tuple(x.reshape(queries.shape) for x in (output, grad_q, grad_k, grad_v))


def solution(mesh):
    spec = P("seq", "head", None)
    return jax.shard_map(
        per_device,
        mesh=mesh,
        in_specs=(spec, spec, spec, spec, P()),
        out_specs=(spec, spec, spec, spec),
        check_vma=False,
    )
```

```python
import functools

import jax
import jax.numpy as jnp
from jax import lax
from jax.experimental import pallas as pl
from jax.experimental.pallas import tpu as pltpu
from jax.sharding import PartitionSpec as P

GROUP = 256
EPSILON = 1e-06
OPENED, SAME_OPENED, HEAD, KEPT, SHARD_HEAD, CLOSING, SAME_CLOSING, BEGIN = range(8)
F32 = jnp.float32
BF16 = jnp.bfloat16

NN = (((1,), (0,)), ((), ()))
NT = (((1,), (1,)), ((), ()))
TN = (((0,), (0,)), ((), ()))


def dot(a, b, dims=NN):
    return lax.dot_general(a, b, dims, preferred_element_type=F32)


def doc_ends_of(doc_ref):
    ends, total = [], jnp.int32(0)
    for j in range(doc_ref.shape[0]):
        total = total + doc_ref[j]
        ends.append(total)
    return ends


def start_of(ends, place):
    found = jnp.int32(0)
    for end in ends:
        found = jnp.where(end <= place, end, found)
    return found


def end_of(ends, place):
    found = jnp.int32(2**30)
    for end in reversed(ends):
        found = jnp.where(end > place, end, found)
    return found


def rows_iota(width):
    return lax.broadcasted_iota(jnp.int32, (GROUP, width), 0)


def lanes_iota(rows):
    return lax.broadcasted_iota(jnp.int32, (rows, GROUP), 1)


def begin_row(ends, first):
    place = lanes_iota(8) + first
    begin = jnp.zeros((8, GROUP), jnp.int32)
    for end in ends:
        begin = jnp.where(place >= end, end, begin)
    return begin - first


def group_mask(begin):
    row = rows_iota(GROUP)
    return (row >= begin) & (row <= lanes_iota(GROUP))


def write_table(table_ref, ends, anchor, tokens):
    for g in range(tokens // GROUP):
        first = anchor + g * GROUP
        after = first + GROUP
        numbers = {
            OPENED: end_of(ends, first - 1) - first,
            SAME_OPENED: (start_of(ends, first - 1) < anchor).astype(jnp.int32),
            HEAD: end_of(ends, first) - first,
            KEPT: (end_of(ends, first) > after).astype(jnp.int32),
            SHARD_HEAD: end_of(ends, anchor) - first,
            CLOSING: start_of(ends, after) - first,
            SAME_CLOSING: (end_of(ends, after) > anchor + tokens).astype(jnp.int32),
        }
        for kind, number in numbers.items():
            table_ref[kind, pl.ds(g, 1), :] = jnp.full((1, GROUP), number, jnp.int32)
        table_ref[BEGIN, pl.ds(g, 1), :] = begin_row(ends, first)[:1]


def known(table_ref, kind, g, width=GROUP):
    return table_ref[kind, pl.ds(g, 1), :width]


def factor(table_ref, kind, g):
    return known(table_ref, kind, g, 128).astype(F32)


def keep_where(keep, x):
    return jnp.where(keep, x.astype(F32), 0.0).astype(BF16)


def at(h):
    return slice(h * 128, (h + 1) * 128)


def turn(x):
    return x.astype(BF16).T


def pair_rows(g, heads):
    return pl.ds(pl.multiple_of(g * (GROUP * heads), GROUP * heads), GROUP * heads)


def split_heads(buf_ref, tmp_ref, g, heads):
    slot = g % tmp_ref.shape[0]
    tmp_ref[slot] = buf_ref[pair_rows(g, heads), :].astype(F32)
    return [tmp_ref[slot, pl.ds(h, GROUP, stride=heads), :] for h in range(heads)]


def group_rows(g):
    return pl.ds(pl.multiple_of(g * GROUP, GROUP), GROUP)


def source_of(index, step, size):
    if size & (size - 1):
        return (index + size - step) % size
    return index ^ step


def links_of(step, size):
    return [(source_of(i, step, size), i) for i in range(size)]


def weights_of(out_ref, ends, shard, tokens, n_seq, sign):
    core = shard % 2
    chip = shard // 2
    n_chips = n_seq // 2
    others = [source_of(chip, k, n_chips) for k in range(1, n_chips)]
    chip_first = (shard - core) * tokens
    middle = chip_first + tokens
    chip_end = middle + tokens
    if sign > 0:
        join = start_of(ends, chip_end - 1) < middle
        onward = start_of(ends, middle - 1) < chip_first
        begin = start_of(ends, chip_first - 1)
        same = [(other < chip) & (begin < (other + 1) * (2 * tokens)) for other in others]
        is_near = core == 0
    else:
        join = end_of(ends, chip_first) > middle
        onward = end_of(ends, middle) > chip_end
        end = end_of(ends, chip_end)
        same = [(other > chip) & (end > other * (2 * tokens)) for other in others]
        is_near = core == 1
    join, onward, is_near = (x.astype(F32) for x in (join, onward, is_near))
    far = 1.0 - is_near
    table = [
        is_near * join + far,
        is_near + far * join,
        is_near + far * onward,
        far,
        is_near * onward + far,
        is_near,
    ] + [x.astype(F32) for x in same]
    for i, x in enumerate(table):
        out_ref[pl.ds(i, 1), :] = jnp.full((1, 128), x, F32)


def state_kernel(
    n_seq, doc_hbm, k2_ref, v2_ref, bufk, bufv, vt_ref, mine_ref, send_ref, fore_ref, back_ref,
    doc_ref, tmpk, tmpv, acc, sems, doc_sem,
):
    width, tokens = vt_ref.shape
    heads = width // 128
    half = heads // 2
    n_groups = tokens // GROUP

    sizes = [max(1, n_groups // 6), max(1, n_groups // 3)]
    sizes = [*sizes, n_groups - sum(sizes)] if n_groups > 2 else [1] * n_groups
    chunks = {sum(sizes[:i]): size for i, size in enumerate(sizes)}

    def fetches(g):
        if g not in chunks:
            return ()
        rows = pl.ds(g * GROUP * heads, chunks[g] * GROUP * heads)
        return (
            pltpu.make_async_copy(k2_ref.at[rows], bufk.at[rows], sems.at[0, g]),
            pltpu.make_async_copy(v2_ref.at[rows], bufv.at[rows], sems.at[1, g]),
        )

    doc_copy = pltpu.make_async_copy(doc_hbm, doc_ref, doc_sem)
    doc_copy.start()
    for g in range(n_groups):
        for copy in fetches(g):
            copy.start()
    doc_copy.wait()
    shard = lax.axis_index("seq")
    core = shard % 2
    anchor = shard * tokens
    ends = doc_ends_of(doc_ref)
    weights_of(fore_ref, ends, shard, tokens, n_seq, 1)
    weights_of(back_ref, ends, shard, tokens, n_seq, -1)
    tail = start_of(ends, anchor + tokens - 1) - anchor

    def prepare(g):
        for copy in fetches(g):
            copy.wait()
        rows = group_rows(g)
        keep = rows_iota(128) + g * GROUP >= tail
        ks = split_heads(bufk, tmpk, g, heads)
        vs = split_heads(bufv, tmpv, g, heads)
        ready = []
        for h in range(heads):
            vt = turn(vs[h])
            vt_ref[at(h), rows] = vt
            ready.append((vt, jnp.where(keep, ks[h], 0.0).astype(BF16)))
        return ready

    total = [jnp.zeros((128, 128), F32) for _ in range(heads)]
    ahead = prepare(0)
    for g in range(n_groups):
        ready = ahead
        if g + 1 < n_groups:
            ahead = prepare(g + 1)
        total = [t + dot(vt, k) for t, (vt, k) in zip(total, ready)]
    for h in range(heads):
        acc[h] = total[h]
    mine_ref[...] = acc[pl.ds(core * half, half)]
    send_ref[...] = acc[pl.ds((1 - core) * half, half)]


def split_kernel(pairs_ref, out_ref, tmp):
    tokens, width = out_ref.shape
    heads = width // 128
    for g in range(tokens // GROUP):
        parts = split_heads(pairs_ref, tmp, g, heads)
        for h in range(heads):
            out_ref[group_rows(g), at(h)] = parts[h].astype(BF16)


def later_forms_kernel(
    table_ref, k_ref, v2_ref, own_ref, other_ref, q_ref, kt_ref, vd_ref, st_ref, q_back_ref, tmp
):
    split_kernel(v2_ref, vd_ref, tmp)
    width, tokens = kt_ref.shape
    half = own_ref.shape[1]
    core = lax.axis_index("seq") % 2
    for g in range(tokens // GROUP):
        for h in range(half):
            st_ref[g, part_of(core, True, half) + h] = own_ref[g, h].T
            st_ref[g, part_of(core, False, half) + h] = other_ref[g, h].T
        rows = group_rows(g)
        for h in range(width // 128):
            kt_ref[at(h), rows] = k_ref[rows, at(h)].T
            keep = rows_iota(128) < known(table_ref, SHARD_HEAD, g, 128)
            q_back_ref[rows, at(h)] = keep_where(keep, q_ref[rows, at(h)])


def local_kernel(
    doc_ref, kd_ref, vt_ref, q2_ref, c2_ref, qd_ref, qt_ref, ct_ref, pt_ref, ol_ref, sl_ref, table_ref,
    tmpq, tmpc,
):
    tokens, width = kd_ref.shape
    heads = width // 128
    n_groups = tokens // GROUP
    anchor = lax.axis_index("seq") * tokens
    ends = doc_ends_of(doc_ref)

    def prepare(g):
        rows = group_rows(g)
        qs = split_heads(q2_ref, tmpq, g, heads)
        cs = split_heads(c2_ref, tmpc, g, heads)
        opened = lanes_iota(128) < known(table_ref, OPENED, g)
        qts = []
        for h in range(heads):
            qt = turn(qs[h])
            qd_ref[rows, at(h)] = qs[h].astype(BF16)
            qt_ref[at(h), rows] = keep_where(opened, qt)
            ct_ref[at(h), rows] = turn(cs[h])
            qts.append(qt)
        return qts

    def scores(g, qts):
        rows = group_rows(g)
        mask = group_mask(known(table_ref, BEGIN, g))
        pts = []
        for h in range(heads):
            pt = jnp.where(mask, dot(kd_ref[rows, at(h)], qts[h]), 0.0).astype(BF16)
            pt_ref[h, rows, :] = pt
            pts.append(pt)
        return pts

    write_table(table_ref, ends, anchor, tokens)
    state = [jnp.zeros((128, 128), F32) for _ in range(heads)]
    next_pts = scores(0, prepare(0))
    next_qts = prepare(1) if n_groups > 1 else None
    for g in range(n_groups):
        pts = next_pts
        if g + 1 < n_groups:
            next_pts = scores(g + 1, next_qts)
        if g + 2 < n_groups:
            next_qts = prepare(g + 2)
        first = anchor + g * GROUP
        rows = group_rows(g)
        begin = start_of(ends, first + GROUP - 1)
        tail = rows_iota(128) >= begin - first
        kept = (begin < first).astype(F32)
        for h in range(heads):
            vt = vt_ref[at(h), rows]
            sl_ref[g, h] = state[h]
            state[h] = state[h] * kept + dot(vt, keep_where(tail, kd_ref[rows, at(h)]))
            ol_ref[at(h), rows] = dot(vt, pts[h])


def place_halves(core, out_ref, own_ref, other_ref):
    half = own_ref.shape[0]
    out_ref[pl.ds(core * half, half)] = own_ref[...]
    out_ref[pl.ds((1 - core) * half, half)] = other_ref[...]


def part_of(core, own, half):
    return (core if own else 1 - core) * half


def head_rows(head):
    return pl.ds(pl.multiple_of(head * 128, 128), 128)


def stats_kernel(own, table_ref, qt_ref, ol_ref, ct_ref, sl_ref, state_ref, *refs):
    (before_ref, o_ref, sb_ref, st_ref) = refs if len(refs) == 4 else (None, *refs)
    width, tokens = qt_ref.shape
    half = state_ref.shape[0]
    n_groups = tokens // GROUP
    base = part_of(lax.axis_index("seq") % 2, own, half)

    def opened_terms(g):
        rows = group_rows(g)
        same = factor(table_ref, SAME_OPENED, g)
        terms = []
        for h in range(half):
            sb = (sl_ref[g, base + h] + same * state_ref[h]).astype(BF16)
            sb_ref[g, h] = sb
            terms.append(dot(sb, qt_ref[head_rows(base + h), rows]))
        return terms

    ahead = opened_terms(0)
    for g in range(n_groups):
        terms = ahead
        if g + 1 < n_groups:
            ahead = opened_terms(g + 1)
        rows = group_rows(g)
        squares = jnp.zeros((1, GROUP), F32)
        inner = jnp.zeros((1, GROUP), F32)
        for h in range(half):
            o = ol_ref[head_rows(base + h), rows] + terms[h]
            o_ref[at(h), rows] = o
            squares += jnp.sum(o * o, axis=0, keepdims=True)
            inner += jnp.sum(o * ct_ref[head_rows(base + h), rows].astype(F32), axis=0, keepdims=True)
        both = jnp.concatenate([squares, inner], axis=0)
        st_ref[:, rows] = both if before_ref is None else both + before_ref[:, rows]


def back_state(half, n_groups, prepare, qd_ref, base, out_ref):
    total = [jnp.zeros((128, 128), F32) for _ in range(half)]
    ahead = prepare(0)
    for g in range(n_groups):
        ready = ahead
        if g + 1 < n_groups:
            ahead = prepare(g + 1)
        total = [
            total[h] + dot(ready[h], qd_ref[group_rows(g), head_rows(base + h)]) for h in range(half)
        ]
    for h in range(half):
        out_ref[h] = total[h]


def norm_kernel(
    width_all, st_ref, o_ref, ct_ref, qd_ref, dobt_ref, rows_ref, send_ref
):
    tokens, width = qd_ref.shape
    half = send_ref.shape[0]
    base = part_of(lax.axis_index("seq") % 2, False, half)

    def prepare(g):
        rows = group_rows(g)
        total = st_ref[:, rows] * (1.0 / width_all)
        inv = lax.rsqrt(total[0:1] + EPSILON)
        slope = total[1:2] * inv * inv * inv
        rows_ref[:, rows] = jnp.concatenate([inv, slope] * 4, axis=0)
        ready = []
        for h in range(half):
            dob = inv * ct_ref[head_rows(base + h), rows].astype(F32) - slope * o_ref[at(h), rows]
            dob = dob.astype(BF16)
            dobt_ref[at(h), rows] = dob
            ready.append(dob)
        return ready

    back_state(half, tokens // GROUP, prepare, qd_ref, base, send_ref)


def merge_kernel(
    rows_ref, own_ref, other_ref, ct_ref, qd_ref, dob_other_ref,
    dobt_ref, normed_ref, mine_ref,
):
    tokens, width = qd_ref.shape
    half = mine_ref.shape[0]
    core = lax.axis_index("seq") % 2
    base, far = part_of(core, True, half), part_of(core, False, half)

    def prepare(g):
        rows = group_rows(g)
        inv = rows_ref[0:1, rows]
        slope = rows_ref[1:2, rows]
        ready = []
        for h in range(half):
            mine, others = head_rows(base + h), head_rows(far + h)
            o = own_ref[at(h), rows]
            dob = inv * ct_ref[mine, rows].astype(F32) - slope * o
            dob = dob.astype(BF16)
            dobt_ref[mine, rows] = dob
            dobt_ref[others, rows] = dob_other_ref[at(h), rows]
            normed_ref[mine, rows] = (o * inv).astype(BF16)
            normed_ref[others, rows] = (other_ref[at(h), rows] * inv).astype(BF16)
            ready.append(dob)
        return ready

    back_state(half, tokens // GROUP, prepare, qd_ref, base, mine_ref)


def grad_kernel(groups, *refs):
    table_ref, normed_ref, dobt_ref, pt_ref, qd_ref, kt_ref, vd_ref, sb_ref, *refs = refs
    width = dobt_ref.shape[0]
    heads = width // 128
    n_groups = dobt_ref.shape[1] // GROUP
    state = [jnp.zeros((128, 128), F32) for _ in range(heads)]
    if groups.stop < n_groups:
        state_ref, _, _, *refs = refs
        state = [state_ref[h] for h in range(heads)]
    left_ref = None
    if groups.start > 0:
        left_ref, *refs = refs
    dk_ref, dv_ref, rl_ref, out_ref, gq_ref, tmpo, tmpq, bufo, bufq, sems = refs

    def scores(g):
        rows = group_rows(g)
        mask = group_mask(known(table_ref, BEGIN, g))
        return [
            jnp.where(mask, dot(vd_ref[rows, at(h)], dobt_ref[at(h), rows]), 0.0).astype(BF16)
            for h in range(heads)
        ]

    started = []
    ahead = scores(groups[-1])
    for g in reversed(groups):
        dpts = ahead
        slot = g % tmpq.shape[0]
        rows = group_rows(g)
        here = group_rows(g - groups.start)
        buffered = pair_rows(g - groups.start, heads)
        opened = lanes_iota(128) < known(table_ref, OPENED, g)
        head_part = lanes_iota(128) < known(table_ref, HEAD, g)
        kept = factor(table_ref, KEPT, g)
        for h in range(heads):
            mine = pl.ds(h, GROUP, stride=heads)
            dv_ref[here, at(h)] = dot(pt_ref[h, rows, :], turn(dobt_ref[at(h), rows]))
            tmpo[slot, mine, :] = normed_ref[at(h), rows].T.astype(F32)
        bufo[buffered, :] = tmpo[slot].astype(BF16)
        if g > groups.start:
            ahead = scores(g - 1)
        near, grown = [], []
        for h in range(heads):
            dobt = dobt_ref[at(h), rows]
            near.append(jnp.where(opened, dot(sb_ref[g, h], dobt), 0.0))
            grown.append(dot(keep_where(head_part, dobt), qd_ref[rows, at(h)]))
        for h in range(heads):
            mine = pl.ds(h, GROUP, stride=heads)
            dk_ref[here, at(h)] = dot(dpts[h], qd_ref[rows, at(h)])
            gq = dot(kt_ref[at(h), rows], dpts[h]) + near[h]
            tmpq[slot, mine, :] = turn(gq).astype(F32)
            rl_ref[g - groups.start, h] = state[h]
            state[h] = state[h] * kept + grown[h]
        bufq[buffered, :] = tmpq[slot].astype(BF16)
        for n, (buf, out) in enumerate(((bufo, out_ref), (bufq, gq_ref))):
            copy = pltpu.make_async_copy(
                buf.at[buffered], out.at[pair_rows(g, heads)], sems.at[n, g]
            )
            copy.start()
            started.append(copy)
    if left_ref is not None:
        for h in range(heads):
            left_ref[h] = state[h]
    for copy in started:
        copy.wait()


def final_kernel(table_ref, kd_ref, vd_ref, own_ref, other_ref, *refs):
    *parts, gk_ref, gv_ref, rin, tmpk, tmpv, bufk, bufv, sems = refs
    tokens, width = kd_ref.shape
    heads = width // 128
    n_groups = tokens // GROUP
    place_halves(lax.axis_index("seq") % 2, rin, own_ref, other_ref)
    held = []
    for dk_ref, dv_ref, rl_ref in zip(parts[0::3], parts[1::3], parts[2::3]):
        held += [(dk_ref, dv_ref, rl_ref, i) for i in range(rl_ref.shape[0])]

    def closing_terms(g):
        rows = group_rows(g)
        rl_ref, i = held[g][2:]
        closing = rows_iota(128) >= known(table_ref, CLOSING, g, 128)
        same = factor(table_ref, SAME_CLOSING, g)
        terms = []
        for h in range(heads):
            rb = (rl_ref[i, h] + same * rin[h]).astype(BF16)
            terms.append(
                (
                    jnp.where(closing, dot(vd_ref[rows, at(h)], rb), 0.0),
                    jnp.where(closing, dot(kd_ref[rows, at(h)], rb, NT), 0.0),
                )
            )
        return terms

    started = []
    ahead = closing_terms(0)
    for g in range(n_groups):
        terms = ahead
        if g + 1 < n_groups:
            ahead = closing_terms(g + 1)
        dk_ref, dv_ref, _, i = held[g]
        pairs = pair_rows(g, heads)
        slot = g % tmpk.shape[0]
        for h in range(heads):
            mine = pl.ds(h, GROUP, stride=heads)
            tmpk[slot, mine, :] = dk_ref[group_rows(i), at(h)] + terms[h][0]
            tmpv[slot, mine, :] = dv_ref[group_rows(i), at(h)] + terms[h][1]
        bufk[pairs, :] = tmpk[slot].astype(BF16)
        bufv[pairs, :] = tmpv[slot].astype(BF16)
        for n, (buf, out) in enumerate(((bufk, gk_ref), (bufv, gv_ref))):
            copy = pltpu.make_async_copy(buf.at[pairs], out.at[pairs], sems.at[n, g])
            copy.start()
            started.append(copy)
    for copy in started:
        copy.wait()


def call(kernel, name, outs, scratch, n_in, in_hbm=(), out_hbm=(), in_smem=(), alias=None, flops=0):
    vmem = pl.BlockSpec(memory_space=pltpu.VMEM)
    hbm = pl.BlockSpec(memory_space=pltpu.HBM)
    smem = pl.BlockSpec(memory_space=pltpu.SMEM)
    return pl.pallas_call(
        kernel,
        name=name,
        out_shape=[jax.ShapeDtypeStruct(s, d) for s, d in outs],
        in_specs=[hbm if i in in_hbm else smem if i in in_smem else vmem for i in range(n_in)],
        out_specs=[hbm if i in out_hbm else vmem for i in range(len(outs))],
        scratch_shapes=scratch,
        input_output_aliases=alias or {},
        cost_estimate=pl.CostEstimate(flops=flops, bytes_accessed=8 << 20, transcendentals=0),
        compiler_params=pltpu.CompilerParams(vmem_limit_bytes=16 << 20),
    )


def per_device(queries, keys, values, cotangent, doc_lengths):
    tokens, heads, head_width = queries.shape
    width = heads * head_width
    half = heads // 2
    n_groups = tokens // GROUP
    n_seq = lax.axis_size("seq")
    n_head = lax.axis_size("head")
    n_chips = n_seq // 2

    def pairs(x):
        return x.reshape(tokens * heads, head_width)

    q2, k2, v2, c2 = pairs(queries), pairs(keys), pairs(values), pairs(cotangent)
    full = (tokens, width)
    piece = (half, head_width, head_width)
    state_shape = (heads, head_width, head_width)
    flat = (tokens * heads, head_width)
    buf = pltpu.VMEM(flat, BF16)
    tmp = pltpu.VMEM((2, GROUP * heads, head_width), F32)
    sems = pltpu.SemaphoreType.DMA((2, n_groups))
    swap_pairs = [(i, i ^ 1) for i in range(n_seq)]

    def swap(x):
        return lax.ppermute(x, "seq", swap_pairs)

    def exchange(mine, send, weights, after):
        got = swap(send)
        chip_state, after = lax.optimization_barrier((weights[0] * mine + weights[1] * got, after))
        total = jnp.zeros(piece, F32)
        for k in range(1, n_chips):
            links = [(2 * i + c, 2 * j + c) for i, j in links_of(k, n_chips) for c in (0, 1)]
            total = total + weights[5 + k] * lax.ppermute(chip_state, "seq", links)
        return got, total, after

    def finish(mine, got, total, weights):
        return weights[2] * total + weights[3] * got, swap(weights[4] * total + weights[5] * mine)

    mm = 2 * tokens * heads * head_width * head_width
    table = ((5 + n_chips, 128), F32)
    state = pltpu.VMEM(state_shape, F32)
    table = ((5 + n_chips, 128), F32)
    turned = (width, tokens)
    group_states = (n_groups, heads, head_width, head_width)
    raw_k, raw_v, vt, mine, send, fore, back = call(
        functools.partial(state_kernel, n_seq),
        "shard_state",
        [(flat, BF16), (flat, BF16), (turned, BF16), (piece, F32), (piece, F32), table, table],
        [
            pltpu.SMEM(doc_lengths.shape, jnp.int32),
            tmp,
            tmp,
            state,
            sems,
            pltpu.SemaphoreType.DMA,
        ],
        n_in=3,
        in_hbm=(0, 1, 2),
        flops=mm,
    )(*(pltpu.with_memory_space_constraint(x, pltpu.HBM) for x in (doc_lengths, k2, v2)))
    (kd,) = call(
        split_kernel,
        "split_keys",
        [(full, BF16)],
        [tmp],
        n_in=1,
    )(raw_k)
    got, total, (kd, vt) = exchange(mine, send, fore, (kd, vt))
    facts = (8, n_groups, GROUP)
    qd, qt, ct, pt, o_local, sl, known_of = call(
        local_kernel,
        "local_mix",
        [
            (full, BF16),
            (turned, BF16),
            (turned, BF16),
            ((heads, tokens, GROUP), BF16),
            (turned, F32),
            (group_states, F32),
            (facts, jnp.int32),
        ],
        [tmp, tmp],
        n_in=5,
        in_smem=(0,),
        flops=6 * mm,
    )(doc_lengths, kd, vt, q2, c2)
    total, o_local = lax.optimization_barrier((total, o_local))
    own, other = finish(mine, got, total, fore)
    half_turned = (half * head_width, tokens)
    half_states = (n_groups, half, head_width, head_width)

    def part(is_own, states, before, name):
        return call(
            functools.partial(stats_kernel, is_own),
            name,
            [(half_turned, F32), (half_states, BF16), ((2, tokens), F32)],
            [],
            n_in=6 + len(before),
            flops=mm // 2,
        )(known_of, qt, o_local, ct, sl, states, *before)

    o_own, sb_own, stats = part(True, own, (), "mix_own")
    o_other, sb_other, stats = part(False, other, (stats,), "mix_other")
    stats, kd_late, raw_v = lax.optimization_barrier((stats, kd, raw_v))
    kt, vd, sb, q_back = call(
        later_forms_kernel,
        "later_forms",
        [(turned, BF16), (full, BF16), (group_states, BF16), (full, BF16)],
        [tmp],
        n_in=6,
    )(known_of, kd_late, raw_v, sb_own, sb_other, qd)
    stats = stats + sum(
        lax.ppermute(stats, "head", links_of(k, n_head)) for k in range(1, n_head)
    )
    stats, kt, vd, sb, q_back = lax.optimization_barrier((stats, kt, vd, sb, q_back))
    dob_other, factors, send = call(
        functools.partial(norm_kernel, float(width * n_head)),
        "norm_other",
        [(half_turned, BF16), ((8, tokens), F32), (piece, F32)],
        [],
        n_in=4,
        flops=mm // 2,
    )(stats, o_other, ct, q_back)
    dobt, normed, mine = call(
        merge_kernel,
        "norm_own",
        [(turned, BF16), (turned, BF16), (piece, F32)],
        [],
        n_in=6,
        flops=mm // 2,
    )(factors, o_own, o_other, ct, q_back, dob_other)
    got, total, (dobt_b, normed_b) = exchange(mine, send, back, (dobt, normed))
    cut = max(1, n_groups // 12)
    earlier, later = range(0, cut), range(cut, n_groups)

    def grads(groups, name, before):
        count = len(groups)
        held = (count * GROUP, width)
        left = [(state_shape, F32)] if groups.start else []
        kept = [(held, F32), (held, F32), ((count, *state_shape), F32)]
        whole = len(left) + len(kept)
        return call(
            functools.partial(grad_kernel, groups),
            name,
            [*left, *kept, (flat, BF16), (flat, BF16)],
            [tmp, tmp, pltpu.VMEM((count * GROUP * heads, head_width), BF16)]
            + [pltpu.VMEM((count * GROUP * heads, head_width), BF16), sems],
            n_in=8 + len(before),
            in_hbm=(9, 10),
            out_hbm=(whole, whole + 1),
            alias={9: whole, 10: whole + 1} if before else None,
            flops=count * mm,
        )(known_of, normed_b, dobt_b, pt, qd, kt, vd, sb, *before)

    left, dk1, dv1, rl1, output, grad_q = grads(later, "grads_later", ())
    total, left = lax.optimization_barrier((total, left))
    own, other = finish(mine, got, total, back)
    dk0, dv0, rl0, output, grad_q = grads(earlier, "grads_earlier", (left, output, grad_q))
    grad_k, grad_v = call(
        final_kernel,
        "final_grads",
        [(flat, BF16), (flat, BF16)],
        [state, tmp, tmp, buf, buf, sems],
        n_in=11,
        out_hbm=(0, 1),
        flops=2 * mm,
    )(known_of, kd, vd, own, other, dk0, dv0, rl0, dk1, dv1, rl1)
    return tuple(x.reshape(queries.shape) for x in (output, grad_q, grad_k, grad_v))


def solution(mesh):
    spec = P("seq", "head", None)
    return jax.shard_map(
        per_device,
        mesh=mesh,
        in_specs=(spec, spec, spec, spec, P()),
        out_specs=(spec, spec, spec, spec),
        check_vma=False,
    )
```

```python
import functools

import jax
import jax.numpy as jnp
from jax import lax
from jax.experimental import pallas as pl
from jax.experimental.pallas import tpu as pltpu
from jax.sharding import PartitionSpec as P

GROUP = 256
EPSILON = 1e-06
OPENED, SAME_OPENED, HEAD, KEPT, SHARD_HEAD, CLOSING, SAME_CLOSING, BEGIN = range(8)
F32 = jnp.float32
BF16 = jnp.bfloat16

NN = (((1,), (0,)), ((), ()))
NT = (((1,), (1,)), ((), ()))
TN = (((0,), (0,)), ((), ()))


def dot(a, b, dims=NN):
    return lax.dot_general(a, b, dims, preferred_element_type=F32)


def doc_ends_of(doc_ref):
    ends, total = [], jnp.int32(0)
    for j in range(doc_ref.shape[0]):
        total = total + doc_ref[j]
        ends.append(total)
    return ends


def start_of(ends, place):
    found = jnp.int32(0)
    for end in ends:
        found = jnp.where(end <= place, end, found)
    return found


def end_of(ends, place):
    found = jnp.int32(2**30)
    for end in reversed(ends):
        found = jnp.where(end > place, end, found)
    return found


def rows_iota(width):
    return lax.broadcasted_iota(jnp.int32, (GROUP, width), 0)


def lanes_iota(rows):
    return lax.broadcasted_iota(jnp.int32, (rows, GROUP), 1)


def begin_row(ends, first):
    place = lanes_iota(8) + first
    begin = jnp.zeros((8, GROUP), jnp.int32)
    for end in ends:
        begin = jnp.where(place >= end, end, begin)
    return begin - first


def group_mask(begin):
    row = rows_iota(GROUP)
    return (row >= begin) & (row <= lanes_iota(GROUP))


def write_table(table_ref, ends, anchor, tokens):
    for g in range(tokens // GROUP):
        first = anchor + g * GROUP
        after = first + GROUP
        numbers = {
            OPENED: end_of(ends, first - 1) - first,
            SAME_OPENED: (start_of(ends, first - 1) < anchor).astype(jnp.int32),
            HEAD: end_of(ends, first) - first,
            KEPT: (end_of(ends, first) > after).astype(jnp.int32),
            SHARD_HEAD: end_of(ends, anchor) - first,
            CLOSING: start_of(ends, after) - first,
            SAME_CLOSING: (end_of(ends, after) > anchor + tokens).astype(jnp.int32),
        }
        for kind, number in numbers.items():
            table_ref[kind, pl.ds(g, 1), :] = jnp.full((1, GROUP), number, jnp.int32)
        table_ref[BEGIN, pl.ds(g, 1), :] = begin_row(ends, first)[:1]


def known(table_ref, kind, g, width=GROUP):
    return table_ref[kind, pl.ds(g, 1), :width]


def factor(table_ref, kind, g):
    return known(table_ref, kind, g, 128).astype(F32)


def keep_where(keep, x):
    return jnp.where(keep, x.astype(F32), 0.0).astype(BF16)


def at(h):
    return slice(h * 128, (h + 1) * 128)


def turn(x):
    return x.astype(BF16).T


def pair_rows(g, heads):
    return pl.ds(pl.multiple_of(g * (GROUP * heads), GROUP * heads), GROUP * heads)


def split_heads(buf_ref, tmp_ref, g, heads):
    slot = g % tmp_ref.shape[0]
    tmp_ref[slot] = buf_ref[pair_rows(g, heads), :].astype(F32)
    return [tmp_ref[slot, pl.ds(h, GROUP, stride=heads), :] for h in range(heads)]


def group_rows(g):
    return pl.ds(pl.multiple_of(g * GROUP, GROUP), GROUP)


def source_of(index, step, size):
    if size & (size - 1):
        return (index + size - step) % size
    return index ^ step


def links_of(step, size):
    return [(source_of(i, step, size), i) for i in range(size)]


def weights_of(out_ref, ends, shard, tokens, n_seq, sign):
    core = shard % 2
    chip = shard // 2
    n_chips = n_seq // 2
    others = [source_of(chip, k, n_chips) for k in range(1, n_chips)]
    chip_first = (shard - core) * tokens
    middle = chip_first + tokens
    chip_end = middle + tokens
    if sign > 0:
        join = start_of(ends, chip_end - 1) < middle
        onward = start_of(ends, middle - 1) < chip_first
        begin = start_of(ends, chip_first - 1)
        same = [(other < chip) & (begin < (other + 1) * (2 * tokens)) for other in others]
        is_near = core == 0
    else:
        join = end_of(ends, chip_first) > middle
        onward = end_of(ends, middle) > chip_end
        end = end_of(ends, chip_end)
        same = [(other > chip) & (end > other * (2 * tokens)) for other in others]
        is_near = core == 1
    join, onward, is_near = (x.astype(F32) for x in (join, onward, is_near))
    far = 1.0 - is_near
    table = [
        is_near * join + far,
        is_near + far * join,
        is_near + far * onward,
        far,
        is_near * onward + far,
        is_near,
    ] + [x.astype(F32) for x in same]
    for i, x in enumerate(table):
        out_ref[pl.ds(i, 1), :] = jnp.full((1, 128), x, F32)


def state_kernel(
    n_seq, doc_hbm, k2_ref, v2_ref, bufk, bufv, vt_ref, mine_ref, send_ref, fore_ref, back_ref,
    doc_ref, tmpk, tmpv, acc, sems, doc_sem,
):
    width, tokens = vt_ref.shape
    heads = width // 128
    half = heads // 2
    n_groups = tokens // GROUP

    sizes = [max(1, n_groups // 6), max(1, n_groups // 3)]
    sizes = [*sizes, n_groups - sum(sizes)] if n_groups > 2 else [1] * n_groups
    chunks = {sum(sizes[:i]): size for i, size in enumerate(sizes)}

    def fetches(g):
        if g not in chunks:
            return ()
        rows = pl.ds(g * GROUP * heads, chunks[g] * GROUP * heads)
        return (
            pltpu.make_async_copy(k2_ref.at[rows], bufk.at[rows], sems.at[0, g]),
            pltpu.make_async_copy(v2_ref.at[rows], bufv.at[rows], sems.at[1, g]),
        )

    doc_copy = pltpu.make_async_copy(doc_hbm, doc_ref, doc_sem)
    doc_copy.start()
    for g in range(n_groups):
        for copy in fetches(g):
            copy.start()
    doc_copy.wait()
    shard = lax.axis_index("seq")
    core = shard % 2
    anchor = shard * tokens
    ends = doc_ends_of(doc_ref)
    weights_of(fore_ref, ends, shard, tokens, n_seq, 1)
    weights_of(back_ref, ends, shard, tokens, n_seq, -1)
    tail = start_of(ends, anchor + tokens - 1) - anchor

    def prepare(g):
        for copy in fetches(g):
            copy.wait()
        rows = group_rows(g)
        keep = jnp.where(lanes_iota(1) + g * GROUP >= tail, 1.0, 0.0).astype(BF16)
        ks = split_heads(bufk, tmpk, g, heads)
        vs = split_heads(bufv, tmpv, g, heads)
        ready = []
        for h in range(heads):
            vt = turn(vs[h])
            vt_ref[at(h), rows] = vt
            ready.append((vt * keep, ks[h].astype(BF16)))
        return ready

    total = [jnp.zeros((128, 128), F32) for _ in range(heads)]
    ahead = prepare(0)
    for g in range(n_groups):
        ready = ahead
        if g + 1 < n_groups:
            ahead = prepare(g + 1)
        total = [t + dot(vt, k) for t, (vt, k) in zip(total, ready)]
    for h in range(heads):
        acc[h] = total[h]
    mine_ref[...] = acc[pl.ds(core * half, half)]
    send_ref[...] = acc[pl.ds((1 - core) * half, half)]


def split_kernel(pairs_ref, out_ref, tmp):
    tokens, width = out_ref.shape
    heads = width // 128
    for g in range(tokens // GROUP):
        parts = split_heads(pairs_ref, tmp, g, heads)
        for h in range(heads):
            out_ref[group_rows(g), at(h)] = parts[h].astype(BF16)


def later_forms_kernel(
    table_ref, k_ref, v2_ref, own_ref, other_ref, q_ref, kt_ref, vd_ref, st_ref, q_back_ref, tmp
):
    split_kernel(v2_ref, vd_ref, tmp)
    width, tokens = kt_ref.shape
    half = own_ref.shape[1]
    core = lax.axis_index("seq") % 2
    for g in range(tokens // GROUP):
        for h in range(half):
            st_ref[g, part_of(core, True, half) + h] = own_ref[g, h].T
            st_ref[g, part_of(core, False, half) + h] = other_ref[g, h].T
        rows = group_rows(g)
        for h in range(width // 128):
            kt_ref[at(h), rows] = k_ref[rows, at(h)].T
            keep = rows_iota(128) < known(table_ref, SHARD_HEAD, g, 128)
            q_back_ref[rows, at(h)] = keep_where(keep, q_ref[rows, at(h)])


def local_kernel(
    doc_ref, kd_ref, vt_ref, q2_ref, c2_ref, qd_ref, qt_ref, ct_ref, pt_ref, ol_ref, sl_ref, table_ref,
    tmpq, tmpc,
):
    tokens, width = kd_ref.shape
    heads = width // 128
    n_groups = tokens // GROUP
    anchor = lax.axis_index("seq") * tokens
    ends = doc_ends_of(doc_ref)

    def prepare(g):
        rows = group_rows(g)
        qs = split_heads(q2_ref, tmpq, g, heads)
        cs = split_heads(c2_ref, tmpc, g, heads)
        opened = lanes_iota(128) < known(table_ref, OPENED, g)
        qts = []
        for h in range(heads):
            qt = turn(qs[h])
            qd_ref[rows, at(h)] = qs[h].astype(BF16)
            qt_ref[at(h), rows] = keep_where(opened, qt)
            ct_ref[at(h), rows] = turn(cs[h])
            qts.append(qt)
        return qts

    def scores(g, qts):
        rows = group_rows(g)
        mask = group_mask(known(table_ref, BEGIN, g))
        pts = []
        for h in range(heads):
            pt = jnp.where(mask, dot(kd_ref[rows, at(h)], qts[h]), 0.0).astype(BF16)
            pt_ref[h, rows, :] = pt
            pts.append(pt)
        return pts

    write_table(table_ref, ends, anchor, tokens)
    state = [jnp.zeros((128, 128), F32) for _ in range(heads)]
    next_pts = scores(0, prepare(0))
    next_qts = prepare(1) if n_groups > 1 else None
    for g in range(n_groups):
        pts = next_pts
        if g + 1 < n_groups:
            next_pts = scores(g + 1, next_qts)
        if g + 2 < n_groups:
            next_qts = prepare(g + 2)
        first = anchor + g * GROUP
        rows = group_rows(g)
        begin = start_of(ends, first + GROUP - 1)
        tail = rows_iota(128) >= begin - first
        kept = (begin < first).astype(F32)
        for h in range(heads):
            vt = vt_ref[at(h), rows]
            sl_ref[g, h] = state[h]
            state[h] = state[h] * kept + dot(vt, keep_where(tail, kd_ref[rows, at(h)]))
            ol_ref[at(h), rows] = dot(vt, pts[h])


def place_halves(core, out_ref, own_ref, other_ref):
    half = own_ref.shape[0]
    out_ref[pl.ds(core * half, half)] = own_ref[...]
    out_ref[pl.ds((1 - core) * half, half)] = other_ref[...]


def part_of(core, own, half):
    return (core if own else 1 - core) * half


def head_rows(head):
    return pl.ds(pl.multiple_of(head * 128, 128), 128)


def stats_kernel(own, table_ref, qt_ref, ol_ref, ct_ref, sl_ref, state_ref, *refs):
    (before_ref, o_ref, sb_ref, st_ref) = refs if len(refs) == 4 else (None, *refs)
    width, tokens = qt_ref.shape
    half = state_ref.shape[0]
    n_groups = tokens // GROUP
    base = part_of(lax.axis_index("seq") % 2, own, half)

    def opened_terms(g):
        rows = group_rows(g)
        same = factor(table_ref, SAME_OPENED, g)
        terms = []
        for h in range(half):
            sb = (sl_ref[g, base + h] + same * state_ref[h]).astype(BF16)
            sb_ref[g, h] = sb
            terms.append(dot(sb, qt_ref[head_rows(base + h), rows]))
        return terms

    ahead = opened_terms(0)
    for g in range(n_groups):
        terms = ahead
        if g + 1 < n_groups:
            ahead = opened_terms(g + 1)
        rows = group_rows(g)
        squares = jnp.zeros((1, GROUP), F32)
        inner = jnp.zeros((1, GROUP), F32)
        for h in range(half):
            o = ol_ref[head_rows(base + h), rows] + terms[h]
            o_ref[at(h), rows] = o
            squares += jnp.sum(o * o, axis=0, keepdims=True)
            inner += jnp.sum(o * ct_ref[head_rows(base + h), rows].astype(F32), axis=0, keepdims=True)
        both = jnp.concatenate([squares, inner], axis=0)
        st_ref[:, rows] = both if before_ref is None else both + before_ref[:, rows]


def back_state(half, n_groups, prepare, qd_ref, base, out_ref):
    total = [jnp.zeros((128, 128), F32) for _ in range(half)]
    ahead = prepare(0)
    for g in range(n_groups):
        ready = ahead
        if g + 1 < n_groups:
            ahead = prepare(g + 1)
        total = [
            total[h] + dot(ready[h], qd_ref[group_rows(g), head_rows(base + h)]) for h in range(half)
        ]
    for h in range(half):
        out_ref[h] = total[h]


def norm_kernel(
    width_all, st_ref, o_ref, ct_ref, qd_ref, dobt_ref, rows_ref, send_ref
):
    tokens, width = qd_ref.shape
    half = send_ref.shape[0]
    base = part_of(lax.axis_index("seq") % 2, False, half)

    def prepare(g):
        rows = group_rows(g)
        total = st_ref[:, rows] * (1.0 / width_all)
        inv = lax.rsqrt(total[0:1] + EPSILON)
        slope = total[1:2] * inv * inv * inv
        rows_ref[:, rows] = jnp.concatenate([inv, slope] * 4, axis=0)
        ready = []
        for h in range(half):
            dob = inv * ct_ref[head_rows(base + h), rows].astype(F32) - slope * o_ref[at(h), rows]
            dob = dob.astype(BF16)
            dobt_ref[at(h), rows] = dob
            ready.append(dob)
        return ready

    back_state(half, tokens // GROUP, prepare, qd_ref, base, send_ref)


def merge_kernel(
    rows_ref, own_ref, other_ref, ct_ref, qd_ref, dob_other_ref,
    dobt_ref, normed_ref, mine_ref,
):
    tokens, width = qd_ref.shape
    half = mine_ref.shape[0]
    core = lax.axis_index("seq") % 2
    base, far = part_of(core, True, half), part_of(core, False, half)

    def prepare(g):
        rows = group_rows(g)
        inv = rows_ref[0:1, rows]
        slope = rows_ref[1:2, rows]
        ready = []
        for h in range(half):
            mine, others = head_rows(base + h), head_rows(far + h)
            o = own_ref[at(h), rows]
            dob = inv * ct_ref[mine, rows].astype(F32) - slope * o
            dob = dob.astype(BF16)
            dobt_ref[mine, rows] = dob
            dobt_ref[others, rows] = dob_other_ref[at(h), rows]
            normed_ref[mine, rows] = (o * inv).astype(BF16)
            normed_ref[others, rows] = (other_ref[at(h), rows] * inv).astype(BF16)
            ready.append(dob)
        return ready

    back_state(half, tokens // GROUP, prepare, qd_ref, base, mine_ref)


def grad_kernel(groups, *refs):
    table_ref, normed_ref, dobt_ref, pt_ref, qd_ref, kt_ref, vd_ref, sb_ref, *refs = refs
    width = dobt_ref.shape[0]
    heads = width // 128
    n_groups = dobt_ref.shape[1] // GROUP
    state = [jnp.zeros((128, 128), F32) for _ in range(heads)]
    if groups.stop < n_groups:
        state_ref, _, _, *refs = refs
        state = [state_ref[h] for h in range(heads)]
    left_ref = None
    if groups.start > 0:
        left_ref, *refs = refs
    dk_ref, dv_ref, rl_ref, out_ref, gq_ref, tmpo, tmpq, bufo, bufq, sems = refs

    def scores(g):
        rows = group_rows(g)
        mask = group_mask(known(table_ref, BEGIN, g))
        return [
            jnp.where(mask, dot(vd_ref[rows, at(h)], dobt_ref[at(h), rows]), 0.0).astype(BF16)
            for h in range(heads)
        ]

    started = []
    ahead = scores(groups[-1])
    for g in reversed(groups):
        dpts = ahead
        slot = g % tmpq.shape[0]
        rows = group_rows(g)
        here = group_rows(g - groups.start)
        buffered = pair_rows(g - groups.start, heads)
        opened = lanes_iota(128) < known(table_ref, OPENED, g)
        head_part = lanes_iota(128) < known(table_ref, HEAD, g)
        kept = factor(table_ref, KEPT, g)
        for h in range(heads):
            mine = pl.ds(h, GROUP, stride=heads)
            dv_ref[here, at(h)] = dot(pt_ref[h, rows, :], turn(dobt_ref[at(h), rows]))
            tmpo[slot, mine, :] = normed_ref[at(h), rows].T.astype(F32)
        bufo[buffered, :] = tmpo[slot].astype(BF16)
        if g > groups.start:
            ahead = scores(g - 1)
        near, grown = [], []
        for h in range(heads):
            dobt = dobt_ref[at(h), rows]
            near.append(jnp.where(opened, dot(sb_ref[g, h], dobt), 0.0))
            grown.append(dot(keep_where(head_part, dobt), qd_ref[rows, at(h)]))
        for h in range(heads):
            mine = pl.ds(h, GROUP, stride=heads)
            dk_ref[here, at(h)] = dot(dpts[h], qd_ref[rows, at(h)])
            gq = dot(kt_ref[at(h), rows], dpts[h]) + near[h]
            tmpq[slot, mine, :] = turn(gq).astype(F32)
            rl_ref[g - groups.start, h] = state[h]
            state[h] = state[h] * kept + grown[h]
        bufq[buffered, :] = tmpq[slot].astype(BF16)
        for n, (buf, out) in enumerate(((bufo, out_ref), (bufq, gq_ref))):
            copy = pltpu.make_async_copy(
                buf.at[buffered], out.at[pair_rows(g, heads)], sems.at[n, g]
            )
            copy.start()
            started.append(copy)
    if left_ref is not None:
        for h in range(heads):
            left_ref[h] = state[h]
    for copy in started:
        copy.wait()


def final_kernel(table_ref, kd_ref, vd_ref, own_ref, other_ref, *refs):
    *parts, gk_ref, gv_ref, rin, tmpk, tmpv, bufk, bufv, sems = refs
    tokens, width = kd_ref.shape
    heads = width // 128
    n_groups = tokens // GROUP
    place_halves(lax.axis_index("seq") % 2, rin, own_ref, other_ref)
    held = []
    for dk_ref, dv_ref, rl_ref in zip(parts[0::3], parts[1::3], parts[2::3]):
        held += [(dk_ref, dv_ref, rl_ref, i) for i in range(rl_ref.shape[0])]

    def closing_terms(g):
        rows = group_rows(g)
        rl_ref, i = held[g][2:]
        closing = rows_iota(128) >= known(table_ref, CLOSING, g, 128)
        same = factor(table_ref, SAME_CLOSING, g)
        terms = []
        for h in range(heads):
            rb = (rl_ref[i, h] + same * rin[h]).astype(BF16)
            terms.append(
                (
                    jnp.where(closing, dot(vd_ref[rows, at(h)], rb), 0.0),
                    jnp.where(closing, dot(kd_ref[rows, at(h)], rb, NT), 0.0),
                )
            )
        return terms

    started = []
    ahead = closing_terms(0)
    for g in range(n_groups):
        terms = ahead
        if g + 1 < n_groups:
            ahead = closing_terms(g + 1)
        dk_ref, dv_ref, _, i = held[g]
        pairs = pair_rows(g, heads)
        slot = g % tmpk.shape[0]
        for h in range(heads):
            mine = pl.ds(h, GROUP, stride=heads)
            tmpk[slot, mine, :] = dk_ref[group_rows(i), at(h)] + terms[h][0]
            tmpv[slot, mine, :] = dv_ref[group_rows(i), at(h)] + terms[h][1]
        bufk[pairs, :] = tmpk[slot].astype(BF16)
        bufv[pairs, :] = tmpv[slot].astype(BF16)
        for n, (buf, out) in enumerate(((bufk, gk_ref), (bufv, gv_ref))):
            copy = pltpu.make_async_copy(buf.at[pairs], out.at[pairs], sems.at[n, g])
            copy.start()
            started.append(copy)
    for copy in started:
        copy.wait()


def call(kernel, name, outs, scratch, n_in, in_hbm=(), out_hbm=(), in_smem=(), alias=None, flops=0):
    vmem = pl.BlockSpec(memory_space=pltpu.VMEM)
    hbm = pl.BlockSpec(memory_space=pltpu.HBM)
    smem = pl.BlockSpec(memory_space=pltpu.SMEM)
    return pl.pallas_call(
        kernel,
        name=name,
        out_shape=[jax.ShapeDtypeStruct(s, d) for s, d in outs],
        in_specs=[hbm if i in in_hbm else smem if i in in_smem else vmem for i in range(n_in)],
        out_specs=[hbm if i in out_hbm else vmem for i in range(len(outs))],
        scratch_shapes=scratch,
        input_output_aliases=alias or {},
        cost_estimate=pl.CostEstimate(flops=flops, bytes_accessed=8 << 20, transcendentals=0),
        compiler_params=pltpu.CompilerParams(vmem_limit_bytes=16 << 20),
    )


def per_device(queries, keys, values, cotangent, doc_lengths):
    tokens, heads, head_width = queries.shape
    width = heads * head_width
    half = heads // 2
    n_groups = tokens // GROUP
    n_seq = lax.axis_size("seq")
    n_head = lax.axis_size("head")
    n_chips = n_seq // 2

    def pairs(x):
        return x.reshape(tokens * heads, head_width)

    q2, k2, v2, c2 = pairs(queries), pairs(keys), pairs(values), pairs(cotangent)
    full = (tokens, width)
    piece = (half, head_width, head_width)
    state_shape = (heads, head_width, head_width)
    flat = (tokens * heads, head_width)
    buf = pltpu.VMEM(flat, BF16)
    tmp = pltpu.VMEM((2, GROUP * heads, head_width), F32)
    sems = pltpu.SemaphoreType.DMA((2, n_groups))
    swap_pairs = [(i, i ^ 1) for i in range(n_seq)]

    def swap(x):
        return lax.ppermute(x, "seq", swap_pairs)

    def exchange(mine, send, weights, after):
        got = swap(send)
        chip_state, after = lax.optimization_barrier((weights[0] * mine + weights[1] * got, after))
        total = jnp.zeros(piece, F32)
        for k in range(1, n_chips):
            links = [(2 * i + c, 2 * j + c) for i, j in links_of(k, n_chips) for c in (0, 1)]
            total = total + weights[5 + k] * lax.ppermute(chip_state, "seq", links)
        return got, total, after

    def finish(mine, got, total, weights):
        return weights[2] * total + weights[3] * got, swap(weights[4] * total + weights[5] * mine)

    mm = 2 * tokens * heads * head_width * head_width
    table = ((5 + n_chips, 128), F32)
    state = pltpu.VMEM(state_shape, F32)
    table = ((5 + n_chips, 128), F32)
    turned = (width, tokens)
    group_states = (n_groups, heads, head_width, head_width)
    raw_k, raw_v, vt, mine, send, fore, back = call(
        functools.partial(state_kernel, n_seq),
        "shard_state",
        [(flat, BF16), (flat, BF16), (turned, BF16), (piece, F32), (piece, F32), table, table],
        [
            pltpu.SMEM(doc_lengths.shape, jnp.int32),
            tmp,
            tmp,
            state,
            sems,
            pltpu.SemaphoreType.DMA,
        ],
        n_in=3,
        in_hbm=(0, 1, 2),
        flops=mm,
    )(*(pltpu.with_memory_space_constraint(x, pltpu.HBM) for x in (doc_lengths, k2, v2)))
    (kd,) = call(
        split_kernel,
        "split_keys",
        [(full, BF16)],
        [tmp],
        n_in=1,
    )(raw_k)
    got, total, (kd, vt) = exchange(mine, send, fore, (kd, vt))
    facts = (8, n_groups, GROUP)
    qd, qt, ct, pt, o_local, sl, known_of = call(
        local_kernel,
        "local_mix",
        [
            (full, BF16),
            (turned, BF16),
            (turned, BF16),
            ((heads, tokens, GROUP), BF16),
            (turned, F32),
            (group_states, F32),
            (facts, jnp.int32),
        ],
        [tmp, tmp],
        n_in=5,
        in_smem=(0,),
        flops=6 * mm,
    )(doc_lengths, kd, vt, q2, c2)
    total, o_local = lax.optimization_barrier((total, o_local))
    own, other = finish(mine, got, total, fore)
    half_turned = (half * head_width, tokens)
    half_states = (n_groups, half, head_width, head_width)

    def part(is_own, states, before, name):
        return call(
            functools.partial(stats_kernel, is_own),
            name,
            [(half_turned, F32), (half_states, BF16), ((2, tokens), F32)],
            [],
            n_in=6 + len(before),
            flops=mm // 2,
        )(known_of, qt, o_local, ct, sl, states, *before)

    o_own, sb_own, stats = part(True, own, (), "mix_own")
    o_other, sb_other, stats = part(False, other, (stats,), "mix_other")
    stats, kd_late, raw_v = lax.optimization_barrier((stats, kd, raw_v))
    kt, vd, sb, q_back = call(
        later_forms_kernel,
        "later_forms",
        [(turned, BF16), (full, BF16), (group_states, BF16), (full, BF16)],
        [tmp],
        n_in=6,
    )(known_of, kd_late, raw_v, sb_own, sb_other, qd)
    stats = stats + sum(
        lax.ppermute(stats, "head", links_of(k, n_head)) for k in range(1, n_head)
    )
    stats, kt, vd, sb, q_back = lax.optimization_barrier((stats, kt, vd, sb, q_back))
    dob_other, factors, send = call(
        functools.partial(norm_kernel, float(width * n_head)),
        "norm_other",
        [(half_turned, BF16), ((8, tokens), F32), (piece, F32)],
        [],
        n_in=4,
        flops=mm // 2,
    )(stats, o_other, ct, q_back)
    dobt, normed, mine = call(
        merge_kernel,
        "norm_own",
        [(turned, BF16), (turned, BF16), (piece, F32)],
        [],
        n_in=6,
        flops=mm // 2,
    )(factors, o_own, o_other, ct, q_back, dob_other)
    got, total, (dobt_b, normed_b) = exchange(mine, send, back, (dobt, normed))
    cut = max(1, n_groups // 12)
    earlier, later = range(0, cut), range(cut, n_groups)

    def grads(groups, name, before):
        count = len(groups)
        held = (count * GROUP, width)
        left = [(state_shape, F32)] if groups.start else []
        kept = [(held, F32), (held, F32), ((count, *state_shape), F32)]
        whole = len(left) + len(kept)
        return call(
            functools.partial(grad_kernel, groups),
            name,
            [*left, *kept, (flat, BF16), (flat, BF16)],
            [tmp, tmp, pltpu.VMEM((count * GROUP * heads, head_width), BF16)]
            + [pltpu.VMEM((count * GROUP * heads, head_width), BF16), sems],
            n_in=8 + len(before),
            in_hbm=(9, 10),
            out_hbm=(whole, whole + 1),
            alias={9: whole, 10: whole + 1} if before else None,
            flops=count * mm,
        )(known_of, normed_b, dobt_b, pt, qd, kt, vd, sb, *before)

    left, dk1, dv1, rl1, output, grad_q = grads(later, "grads_later", ())
    total, left = lax.optimization_barrier((total, left))
    own, other = finish(mine, got, total, back)
    dk0, dv0, rl0, output, grad_q = grads(earlier, "grads_earlier", (left, output, grad_q))
    grad_k, grad_v = call(
        final_kernel,
        "final_grads",
        [(flat, BF16), (flat, BF16)],
        [state, tmp, tmp, buf, buf, sems],
        n_in=11,
        out_hbm=(0, 1),
        flops=2 * mm,
    )(known_of, kd, vd, own, other, dk0, dv0, rl0, dk1, dv1, rl1)
    return tuple(x.reshape(queries.shape) for x in (output, grad_q, grad_k, grad_v))


def solution(mesh):
    spec = P("seq", "head", None)
    return jax.shard_map(
        per_device,
        mesh=mesh,
        in_specs=(spec, spec, spec, spec, P()),
        out_specs=(spec, spec, spec, spec),
        check_vma=False,
    )
```
